128 devices in a mesh: blk: 16 (over z, x_hi, core), fiber: 8 (over x_lo, y).
Axes of the slice: x: 4 (x_hi: 2, x_lo: 2; x = x_hi * 2 + x_lo), y: 4, z: 4, core: 2. Of those that a mesh axis runs over, the one named last changes fastest.
Arguments:
- embedding: bfloat16 [65536, 256], P(('blk', 'fiber')), may hold values from -2.09375 to 2.09375
- tile_dest: int32 [16, 8, 16, 24], P('blk', 'fiber'), may hold values from 0 to 31, as said below
- tile_source: int32 [16, 8, 16, 24], P('blk', 'fiber'), may hold values from 0 to 3
- tile_count: int32 [16, 8, 16], P('blk', 'fiber'), may hold values from 2 to 24, as said below
- pattern_id: int32 [16, 8, 16, 24], P('blk', 'fiber'), may hold values from 0 to 63
- pattern_bank: int32 [64, 4, 128], replicated, may hold values from -2147483648 to 2147483646
- negative_dest: int32 [16, 8, 16, 4], P('blk', 'fiber'), may hold values from 0 to 31
- negative_source: int32 [16, 8, 16, 4], P('blk', 'fiber'), may hold values from 0 to 3
Outputs:
- gradient: float32 [65536, 256], P(('blk', 'fiber'))
The draws below stay inside these ranges and needn't reach their ends.
Inputs may be any that keep to these rules, and one draw needn't show every extreme that they name: At each block, fiber and stop the 24 pairs (tile_dest, tile_source) are distinct. `tile_count`: slots at or past the count are unused; some block, fiber and stop lists 24 tiles.
All inputs are finite; a program needn't handle non-finite values.
Results may differ from the reference program's by a relative error of at most 0.00064.
Values may be sent and summed in bfloat16 or wider, within the bound.
A program may use at most 64 MiB of HBM per device.

```python
import jax
import jax.numpy as jnp
from jax import lax

D = 256
TILE = 128
SUB = 4
CAP = 24
NEG = 4
BANK = 64
WORDS = 4
STOPS = 16
FIBERS = 8
PT = 32
NODES = 65536


def shuffled_pairs(base_key):
    key_list = jax.random.split(jax.random.fold_in(base_key, 11), STOPS * FIBERS * STOPS)

    def first_pairs(one_key):
        return jax.random.permutation(one_key, PT * SUB)[:CAP]
    pair_ids = jax.vmap(first_pairs)(key_list)
    return pair_ids.reshape(STOPS, FIBERS, STOPS, CAP).astype(jnp.int32)


def draw_tile_dest(key, part):
    return (shuffled_pairs(key) // SUB).astype(jnp.int32)


def draw_tile_source(key, part):
    return (shuffled_pairs(key) % SUB).astype(jnp.int32)


def draw_tile_count(key, part):
    first_key, second_key = jax.random.split(jax.random.fold_in(key, 5))
    device_level = jax.random.randint(first_key, (STOPS, FIBERS, 1), 2, 5)
    base_count = jax.random.randint(second_key, (STOPS, FIBERS, STOPS), 2, CAP // 2 + 2)
    listed_count = jnp.minimum(base_count * device_level // 2, CAP)
    return listed_count.at[0, 0, 0].set(CAP).astype(jnp.int32)


def with_ends(entries, key, smallest, largest):
    dims = entries.shape
    spot = [jax.random.randint(jax.random.fold_in(key, axis), (), 0, dims[axis]) for axis in range(len(dims))]
    entries = entries.at[tuple(spot)].set(smallest)
    longest = dims.index(max(dims))
    spot[longest] = (spot[longest] + 1) % dims[longest]
    return entries.at[tuple(spot)].set(largest)


def levels(key, dims, cuts, least, largest):
    def one(axis_at, shards_of):
        steps = jax.random.uniform(jax.random.fold_in(jax.random.fold_in(key, 6), axis_at), (shards_of,), jnp.float32, least / len(cuts), largest / len(cuts))
        return jnp.repeat(jnp.exp(steps), dims[axis_at] // shards_of).reshape((-1,) + (1,) * (len(dims) - axis_at - 1))

    gain = one(*cuts[0])
    for cut in cuts[1:]:
        gain = gain * one(*cut)
    return gain


def scatter_about(rng, extent, deviation, most, cuts=(), kind=jnp.bfloat16):
    factor_of = levels(rng, extent, cuts, -0.22, 0.18) if cuts else 1.0
    entries = jax.random.normal(rng, extent, jnp.float32) * deviation * factor_of
    return jnp.minimum(jnp.maximum(entries, -most), most).astype(kind)


def setup_inputs(seed: int = 0) -> dict:
    arg_keys = jax.random.split(jax.random.key(seed), 9)
    return {
        "embedding": scatter_about(arg_keys[0], (NODES, D), 0.35, 2.09375, ((0, 128),)),
        "tile_dest": draw_tile_dest(jax.random.fold_in(arg_keys[8], 71), 0),
        "tile_source": draw_tile_source(jax.random.fold_in(arg_keys[8], 71), 0),
        "tile_count": draw_tile_count(jax.random.fold_in(arg_keys[8], 71), 0),
        "pattern_id": with_ends(jax.random.randint(arg_keys[4], (STOPS, FIBERS, STOPS, CAP), 0, BANK), jax.random.fold_in(arg_keys[4], 1), 0, BANK - 1).astype(jnp.int32),
        "pattern_bank": with_ends(jax.random.randint(arg_keys[5], (BANK, WORDS, TILE), -2147483648, 2147483647), jax.random.fold_in(arg_keys[5], 1), -2147483648, 2147483646).astype(jnp.int32),
        "negative_dest": with_ends(jax.random.randint(arg_keys[6], (STOPS, FIBERS, STOPS, NEG), 0, PT), jax.random.fold_in(arg_keys[6], 1), 0, PT - 1).astype(jnp.int32),
        "negative_source": with_ends(jax.random.randint(arg_keys[7], (STOPS, FIBERS, STOPS, NEG), 0, SUB), jax.random.fold_in(arg_keys[7], 1), 0, SUB - 1).astype(jnp.int32),
    }


def unpack_bits(packed_words):
    shifts = jnp.arange(32, dtype=jnp.int32)
    bit_values = jnp.right_shift(packed_words[:, :, None, :], shifts[None, None, :, None]) & 1
    return bit_values.reshape(packed_words.shape[0], packed_words.shape[1] * 32, packed_words.shape[2])

def reference(embedding, tile_dest, tile_source, tile_count, pattern_id, pattern_bank, negative_dest, negative_source):
    node_tiles = embedding.reshape(NODES // TILE, TILE, D)
    fibers = jnp.arange(FIBERS, dtype=jnp.int32)[:, None]
    slot_index = jnp.arange(CAP, dtype=jnp.int32)[None, :]

    def visit(flat_index, gradient_sum):
        block_index = flat_index // STOPS
        stop_index = flat_index % STOPS
        anchor = (block_index - stop_index) % STOPS
        live_slots = (slot_index < tile_count[block_index, :, stop_index][:, None]).astype(jnp.float32)
        live_slots = jnp.concatenate([live_slots, jnp.ones((FIBERS, NEG), jnp.float32)], axis=1).reshape(-1)
        dest_local = jnp.concatenate([tile_dest[block_index, :, stop_index], negative_dest[block_index, :, stop_index]], axis=1)
        source_local = jnp.concatenate([tile_source[block_index, :, stop_index], negative_source[block_index, :, stop_index]], axis=1)
        dest_ids = (block_index * PT + dest_local).reshape(-1).astype(jnp.int32)
        source_ids = (anchor * PT + fibers * SUB + source_local).reshape(-1).astype(jnp.int32)
        packed_words = pattern_bank[pattern_id[block_index, :, stop_index].reshape(-1)]
        mask_bits = unpack_bits(packed_words).astype(jnp.float32).reshape(FIBERS, CAP, TILE, TILE)
        mask_bits = jnp.concatenate([mask_bits, jnp.zeros((FIBERS, NEG, TILE, TILE), jnp.float32)], axis=1)
        mask_bits = mask_bits.reshape(FIBERS * (CAP + NEG), TILE, TILE)
        dest_rows = node_tiles[dest_ids].astype(jnp.float32)
        source_rows = node_tiles[source_ids].astype(jnp.float32)
        scores = jnp.einsum('gjd,gid->gji', source_rows, dest_rows, precision=lax.Precision.HIGHEST)
        residual = (live_slots[:, None, None] * (mask_bits - jax.nn.sigmoid(scores))).astype(jnp.bfloat16)
        residual = lax.optimization_barrier(residual).astype(jnp.float32)
        to_dest = jnp.einsum('gji,gjd->gid', residual, source_rows, precision=lax.Precision.HIGHEST)
        to_source = jnp.einsum('gji,gid->gjd', residual, dest_rows, precision=lax.Precision.HIGHEST)
        return gradient_sum.at[dest_ids].add(to_dest).at[source_ids].add(to_source)
    gradient_sum = lax.fori_loop(0, STOPS * STOPS, visit, jnp.zeros((NODES // TILE, TILE, D), jnp.float32))
    return (gradient_sum / jnp.sqrt(jnp.float32(TILE * STOPS))).reshape(NODES, D)
```

```python
import functools
import math

import jax
import jax.numpy as jnp
from jax import lax
from jax.experimental import pallas as pl
from jax.experimental.pallas import tpu as pltpu
from jax.sharding import PartitionSpec as P

ZS, XS, YS = 4, 2, 4
T = 128
MESH = pl.DeviceIdType.MESH
UNROLL = 4
DEST_BITS, BANK_BITS = 6, 7


def place():
    b, f = lax.axis_index("blk"), lax.axis_index("fiber")
    return b // 4, (b // 2) % 2, b % 2, f // YS, f % YS


def blk_of(z, xh, c):
    return ((z % ZS) * XS + xh) * 2 + c


def fiber_of(xl, y):
    return xl * YS + y % YS


def peers():
    z, xh, c, xl, y = place()
    b, f = blk_of(z, xh, c), fiber_of(xl, y)
    return {
        "sib": (blk_of(z, xh, 1 - c), f),
        "xh": (blk_of(z, 1 - xh, c), f),
        "z+": (blk_of(z + 1, xh, c), f),
        "z-": (blk_of(z + 3, xh, c), f),
        "xl": (b, fiber_of(1 - xl, y)),
        "y+": (b, fiber_of(xl, y + 1)),
        "y-": (b, fiber_of(xl, y + 3)),
    }


def meet(to):
    barrier = pltpu.get_barrier_semaphore()
    for device in to.values():
        pl.semaphore_signal(barrier, inc=1, device_id=device, device_id_type=MESH)
    pl.semaphore_wait(barrier, len(to))


def gather_kernel(e_ref, d_ref, g_ref, send, recv, local):
    rows = e_ref.shape[0]
    z, xh, c, xl, y = place()
    to = peers()

    def g_at(zz, xx, cc):
        return g_ref.at[pl.ds(blk_of(zz, xx, cc) * rows, rows)]

    def d_at(xx, yy):
        return d_ref.at[pl.ds(fiber_of(xx, yy) * rows, rows)]

    copies = {}

    def push(name, src, dst, peer):
        k = len(copies)
        copies[name] = pltpu.make_async_remote_copy(
            src_ref=src,
            dst_ref=dst,
            send_sem=send.at[k],
            recv_sem=recv.at[k],
            device_id=to[peer],
            device_id_type=MESH,
        )
        copies[name].start()

    def got(name):
        copies[name].wait_recv()

    def share(name, zz, xx):
        push(name, g_at(zz, xx, c), g_at(zz, xx, c), "sib")

    meet(to)
    own_g, own_d = g_at(z, xh, c), d_at(xl, y)
    push("z+", e_ref, own_g, "z+")
    push("y+", e_ref, own_d, "y+")
    push("z-", e_ref, own_g, "z-")
    push("y-", e_ref, own_d, "y-")
    push("xl", e_ref, own_d, "xl")
    push("xh", e_ref, own_g, "xh")
    push("s0", e_ref, own_g, "sib")
    keep_d = pltpu.make_async_copy(e_ref, own_d, local.at[0])
    keep_g = pltpu.make_async_copy(e_ref, own_g, local.at[1])
    keep_d.start()
    keep_g.start()
    got("xl")
    push("xl+", d_at(1 - xl, y), d_at(1 - xl, y), "y+")
    push("xl-", d_at(1 - xl, y), d_at(1 - xl, y), "y-")
    got("z+")
    push("z++", g_at(z + 3, xh, c), g_at(z + 3, xh, c), "z+")
    share("s1", z + 3, xh)
    got("y+")
    push("y++", d_at(xl, y + 3), d_at(xl, y + 3), "y+")
    got("xh")
    push("xh+", g_at(z, 1 - xh, c), g_at(z, 1 - xh, c), "z+")
    push("xh-", g_at(z, 1 - xh, c), g_at(z, 1 - xh, c), "z-")
    share("s2", z, 1 - xh)
    got("z-")
    share("s3", z + 1, xh)
    got("y-")
    got("xl-")
    push("xl--", d_at(1 - xl, y + 1), d_at(1 - xl, y + 1), "y-")
    got("xh-")
    push("xh--", g_at(z + 1, 1 - xh, c), g_at(z + 1, 1 - xh, c), "z-")
    share("s4", z + 1, 1 - xh)
    got("z++")
    share("s5", z + 2, xh)
    got("xh+")
    share("s6", z + 3, 1 - xh)
    got("xh--")
    share("s7", z + 2, 1 - xh)
    for name in ("xl+", "y++", "xl--", "s0", "s1", "s2", "s3", "s4", "s5", "s6", "s7"):
        got(name)
    for copy in copies.values():
        copy.wait_send()
    keep_d.wait()
    keep_g.wait()


def gather(e):
    rows, width = e.shape
    return pl.pallas_call(
        gather_kernel,
        out_shape=(
            jax.ShapeDtypeStruct((XS * YS * rows, width), e.dtype),
            jax.ShapeDtypeStruct((ZS * XS * 2 * rows, width), e.dtype),
        ),
        in_specs=[pl.BlockSpec(memory_space=pl.ANY)],
        out_specs=(pl.BlockSpec(memory_space=pl.ANY),) * 2,
        scratch_shapes=[
            pltpu.SemaphoreType.DMA((22,)),
            pltpu.SemaphoreType.DMA((22,)),
            pltpu.SemaphoreType.DMA((2,)),
        ],
        compiler_params=pltpu.CompilerParams(collective_id=0, has_side_effects=True),
    )(e)


def pair_lists(dest, source, count, pattern, neg_dest, neg_source, bank_size, dest_tiles, sub):
    stops, cap = dest.shape
    neg = neg_dest.shape[1]
    slots = cap + neg
    total = stops * (slots + sub)
    total += (-total) % (2 * UNROLL)
    origin = (lax.axis_index("blk") - jnp.arange(stops, dtype=jnp.int32)) % stops
    src = jnp.concatenate([source, neg_source], axis=1)
    live = jnp.concatenate(
        [jnp.arange(cap, dtype=jnp.int32)[None, :] < count[:, None], jnp.ones((stops, neg), bool)], axis=1
    )
    pick = (live[:, :, None] & (src[:, :, None] == jnp.arange(sub, dtype=jnp.int32))).astype(jnp.int32)
    earlier = jnp.arange(slots)[:, None] > jnp.arange(slots)[None, :]
    rank = jnp.sum(jnp.where(earlier[None, :, :, None], pick[:, None, :, :], 0), axis=2)
    held = (jnp.sum(pick, axis=1).reshape(-1) + 1) // 2
    before = jnp.arange(stops * sub)[:, None] > jnp.arange(stops * sub)[None, :]
    first = jnp.sum(jnp.where(before, held[None, :], 0), axis=1).reshape(stops, 1, sub)
    where = jnp.sum(pick * (2 * first + rank), axis=2)
    where = jnp.where(live, where, total).reshape(-1)
    group = origin[:, None] * sub + src
    ids = jnp.concatenate([pattern, jnp.full((stops, neg), bank_size, jnp.int32)], axis=1)
    code = (((group << BANK_BITS) | ids) << DEST_BITS) | jnp.concatenate([dest, neg_dest], axis=1)
    hit = where[None, :] == jnp.arange(total, dtype=jnp.int32)[:, None]
    placed = jnp.sum(jnp.where(hit, code.reshape(-1)[None, :] - dest_tiles, 0), axis=1) + dest_tiles
    return placed, jnp.sum(held).reshape(1)


def pair_kernel(list_ref, pairs_ref, bank_ref, d_hbm, g_hbm, dp_ref, sp_ref, d_v, g_v, gt_v, sems):
    cd = pltpu.make_async_copy(d_hbm, d_v.at[pl.ds(0, d_hbm.shape[0])], sems.at[0])
    cg = pltpu.make_async_copy(g_hbm, g_v, sems.at[1])
    cd.start()
    cg.start()
    d_v[pl.ds(d_hbm.shape[0], T)] = jnp.zeros((T, d_v.shape[1]), d_v.dtype)

    def clear(ref):
        def one(i, carry):
            ref[i] = jnp.zeros(ref.shape[1:], ref.dtype)
            return carry

        lax.fori_loop(0, ref.shape[0], one, 0)

    clear(dp_ref)
    clear(sp_ref)
    cd.wait()
    cg.wait()

    def turn(i, carry):
        gt_v[i] = g_v[pl.ds(i * T, T), :].T
        return carry

    lax.fori_loop(0, gt_v.shape[0], turn, 0)
    shifts = lax.broadcasted_iota(jnp.int32, (32, T), 0)

    def bits(index):
        words = bank_ref[index]
        return jnp.concatenate(
            [
                jnp.right_shift(jnp.broadcast_to(words[k : k + 1, :], (32, T)), shifts) & 1
                for k in range(words.shape[0])
            ],
            axis=0,
        )

    def terms(i):
        codes = [list_ref[2 * i], list_ref[2 * i + 1]]
        g = codes[0] >> (DEST_BITS + BANK_BITS)
        p = [code & (2**DEST_BITS - 1) for code in codes]
        ids = [(code >> DEST_BITS) & (2**BANK_BITS - 1) for code in codes]
        zq = g_v[pl.ds(pl.multiple_of(g * T, T), T), :]
        zp = jnp.concatenate([d_v[pl.ds(pl.multiple_of(k * T, T), T), :] for k in p], axis=0)
        s = lax.dot_general(zq, zp, (((1,), (1,)), ((), ())), preferred_element_type=jnp.float32)
        m = jnp.concatenate([bits(k) for k in ids], axis=1)
        r = (m.astype(jnp.float32) - 0.5 - 0.5 * jnp.tanh(0.5 * s)).astype(jnp.bfloat16)
        to_source = jnp.dot(r, zp, preferred_element_type=jnp.float32)
        to_dest = jnp.dot(gt_v[g], r, preferred_element_type=jnp.float32)
        return g, p, to_source, to_dest

    def body(step, carry):
        done = [terms(step * UNROLL + u) for u in range(UNROLL)]
        for g, p, to_source, to_dest in done:
            sp_ref[g] += to_source
            dp_ref[p[0]] += to_dest[:, :T]
            dp_ref[p[1]] += to_dest[:, T:]
        return carry

    lax.fori_loop(0, (pairs_ref[0] + UNROLL - 1) // UNROLL, body, 0)


def pair_sums(lists, pairs, bank, d, g):
    nd, ng = d.shape[0] // T, g.shape[0] // T
    width = d.shape[1]
    return pl.pallas_call(
        pair_kernel,
        out_shape=(
            jax.ShapeDtypeStruct((nd + 1, width, T), jnp.float32),
            jax.ShapeDtypeStruct((ng, T, width), jnp.float32),
        ),
        in_specs=[
            pl.BlockSpec(memory_space=pltpu.SMEM),
            pl.BlockSpec(memory_space=pltpu.SMEM),
            pl.BlockSpec(memory_space=pltpu.VMEM),
            pl.BlockSpec(memory_space=pl.ANY),
            pl.BlockSpec(memory_space=pl.ANY),
        ],
        out_specs=(pl.BlockSpec(memory_space=pltpu.VMEM),) * 2,
        scratch_shapes=[
            pltpu.VMEM(((nd + 1) * T, width), jnp.bfloat16),
            pltpu.VMEM((ng * T, width), jnp.bfloat16),
            pltpu.VMEM((ng, width, T), jnp.bfloat16),
            pltpu.SemaphoreType.DMA((2,)),
        ],
        compiler_params=pltpu.CompilerParams(vmem_limit_bytes=48 << 20),
    )(lists, pairs, bank, d, g)


def reduce_kernel(scale, dp_ref, sp_ref, out_ref, core_buf, z_buf, y_buf, xh_buf, xl_buf, send, recv):
    sub = core_buf.shape[1]
    z, xh, c, xl, y = place()
    to = peers()
    copies = {}

    def push(name, src, dst, peer):
        k = len(copies)
        copies[name] = pltpu.make_async_remote_copy(
            src_ref=src,
            dst_ref=dst,
            send_sem=send.at[k],
            recv_sem=recv.at[k],
            device_id=to[peer],
            device_id_type=MESH,
        )
        copies[name].start()

    def got(name):
        copies[name].wait_recv()

    def s_at(zz, xx, cc):
        return sp_ref.at[pl.ds(blk_of(zz, xx, cc) * sub, sub)]

    def d_at(xx, yy):
        return dp_ref.at[pl.ds(fiber_of(xx, yy) * sub, sub)]

    def add(total, *parts):
        def one(i, carry):
            value = total[i]
            for part in parts:
                value = value + part[i]
            total[i] = value
            return carry

        lax.fori_loop(0, sub, one, 0)

    meet(to)
    push("y0", d_at(0, y + 2), y_buf.at[0], "y+")
    push("y1", d_at(1, y + 2), y_buf.at[1], "y-")
    order = [(2, 0), (2, 1), (1, 1), (3, 0), (1, 0), (3, 1), (0, 0), (0, 1)]
    for n, (dz, xx) in enumerate(order):
        push(f"c{n}", s_at(z + dz, xx, 1 - c), core_buf.at[n], "sib")
    push("y2", d_at(1, y + 1), y_buf.at[2], "y+")
    push("y3", d_at(0, y + 3), y_buf.at[3], "y-")

    def both(n):
        got(f"c{n}")
        dz, xx = order[n]
        add(core_buf.at[n], s_at(z + dz, xx, c))

    both(0)
    push("z0", core_buf.at[0], z_buf.at[0], "z+")
    both(1)
    push("z1", core_buf.at[1], z_buf.at[1], "z-")
    both(2)
    push("z2", core_buf.at[2], z_buf.at[2], "z+")
    both(3)
    push("z3", core_buf.at[3], z_buf.at[3], "z-")
    for n in range(4, 8):
        both(n)
    got("y0")
    add(y_buf.at[0], d_at(0, y + 1))
    push("y4", y_buf.at[0], y_buf.at[4], "y+")
    got("y1")
    add(y_buf.at[1], d_at(1, y + 3))
    push("y5", y_buf.at[1], y_buf.at[5], "y-")
    got("z0")
    add(z_buf.at[0], core_buf.at[4])
    push("z4", z_buf.at[0], z_buf.at[4], "z+")
    got("z1")
    add(z_buf.at[1], core_buf.at[5])
    push("z5", z_buf.at[1], z_buf.at[5], "z-")
    got("y2")
    got("y3")
    add(y_buf.at[2], d_at(1, y))
    add(y_buf.at[3], d_at(0, y))
    got("z2")
    got("z3")
    add(z_buf.at[2], core_buf.at[7])
    add(z_buf.at[3], core_buf.at[6])
    got("y4")
    got("y5")
    add(y_buf.at[2], y_buf.at[5])
    add(y_buf.at[3], y_buf.at[4])
    push("xl", y_buf.at[2 + xl], xl_buf, "xl")
    got("z4")
    got("z5")
    add(z_buf.at[2], z_buf.at[5])
    add(z_buf.at[3], z_buf.at[4])
    push("xh", z_buf.at[2 + xh], xh_buf, "xh")
    got("xl")
    add(xl_buf, y_buf.at[3 - xl])
    got("xh")
    add(xh_buf, z_buf.at[3 - xh])

    def finish(i, carry):
        out_ref[pl.ds(pl.multiple_of(i * T, T), T), :] = (xh_buf[i] + xl_buf[i].T) * scale
        return carry

    lax.fori_loop(0, sub, finish, 0)
    for copy in copies.values():
        copy.wait_send()


def reduce_sums(dp, sp, rows, scale):
    width = sp.shape[2]
    sub = rows // T
    return pl.pallas_call(
        functools.partial(reduce_kernel, scale),
        out_shape=jax.ShapeDtypeStruct((rows, width), jnp.float32),
        in_specs=[pl.BlockSpec(memory_space=pltpu.VMEM)] * 2,
        out_specs=pl.BlockSpec(memory_space=pltpu.VMEM),
        scratch_shapes=[
            pltpu.VMEM((8, sub, T, width), jnp.float32),
            pltpu.VMEM((6, sub, T, width), jnp.float32),
            pltpu.VMEM((6, sub, width, T), jnp.float32),
            pltpu.VMEM((sub, T, width), jnp.float32),
            pltpu.VMEM((sub, width, T), jnp.float32),
            pltpu.SemaphoreType.DMA((22,)),
            pltpu.SemaphoreType.DMA((22,)),
        ],
        compiler_params=pltpu.CompilerParams(
            collective_id=1, has_side_effects=True, vmem_limit_bytes=48 << 20
        ),
    )(dp, sp)


def on_device(
    embedding, tile_dest, tile_source, tile_count, pattern_id, pattern_bank, negative_dest, negative_source
):
    rows = embedding.shape[0]
    d, g = gather(embedding)
    lists, pairs = pair_lists(
        tile_dest[0, 0],
        tile_source[0, 0],
        tile_count[0, 0],
        pattern_id[0, 0],
        negative_dest[0, 0],
        negative_source[0, 0],
        pattern_bank.shape[0],
        d.shape[0] // T,
        rows // T,
    )
    bank = jnp.concatenate([pattern_bank, jnp.zeros_like(pattern_bank[:1])], axis=0)
    dp, sp = pair_sums(lists, pairs, bank, d, g)
    scale = 1.0 / math.sqrt(T * tile_dest.shape[2])
    return reduce_sums(dp, sp, rows, scale)


def solution(mesh):
    in_specs = (
        P(("blk", "fiber"), None),
        P("blk", "fiber", None, None),
        P("blk", "fiber", None, None),
        P("blk", "fiber", None),
        P("blk", "fiber", None, None),
        P(),
        P("blk", "fiber", None, None),
        P("blk", "fiber", None, None),
    )
    out_specs = P(("blk", "fiber"), None)
    return jax.shard_map(
        on_device, mesh=mesh, in_specs=in_specs, out_specs=out_specs, check_vma=False
    )
```

```python
import functools
import math

import jax
import jax.numpy as jnp
from jax import lax
from jax.experimental import pallas as pl
from jax.experimental.pallas import tpu as pltpu
from jax.sharding import PartitionSpec as P

ZS, XS, YS = 4, 2, 4
T = 128
MESH = pl.DeviceIdType.MESH
UNROLL = 6
CHUNKS = 2
VMEM_LIMIT = 60 << 20
DEST_BITS, BANK_BITS = 6, 7


def place():
    b, f = lax.axis_index("blk"), lax.axis_index("fiber")
    return b // 4, (b // 2) % 2, b % 2, f // YS, f % YS


def blk_of(z, xh, c):
    return ((z % ZS) * XS + xh) * 2 + c


def fiber_of(xl, y):
    return xl * YS + y % YS


def peers():
    z, xh, c, xl, y = place()
    b, f = blk_of(z, xh, c), fiber_of(xl, y)
    return {
        "sib": (blk_of(z, xh, 1 - c), f),
        "xh": (blk_of(z, 1 - xh, c), f),
        "z+": (blk_of(z + 1, xh, c), f),
        "z-": (blk_of(z + 3, xh, c), f),
        "xl": (b, fiber_of(1 - xl, y)),
        "y+": (b, fiber_of(xl, y + 1)),
        "y-": (b, fiber_of(xl, y + 3)),
    }


def meet(to):
    barrier = pltpu.get_barrier_semaphore()
    for device in to.values():
        pl.semaphore_signal(barrier, inc=1, device_id=device, device_id_type=MESH)
    pl.semaphore_wait(barrier, len(to))


def gather_kernel(e_ref, d_ref, g_ref, send, recv, local):
    rows = e_ref.shape[0]
    part = rows // CHUNKS
    z, xh, c, xl, y = place()
    to = peers()
    copies = {}

    def push(name, h, src, dst, peer):
        k = len(copies)
        copies[name, h] = pltpu.make_async_remote_copy(
            src_ref=src,
            dst_ref=dst,
            send_sem=send.at[k],
            recv_sem=recv.at[k],
            device_id=to[peer],
            device_id_type=MESH,
        )
        copies[name, h].start()

    def got(name, h):
        copies[name, h].wait_recv()

    def e_at(h):
        return e_ref.at[pl.ds(h * part, part)]

    def g_at(zz, xx, h):
        return g_ref.at[pl.ds(blk_of(zz, xx, c) * rows + h * part, part)]

    def d_at(xx, yy, h):
        return d_ref.at[pl.ds(fiber_of(xx, yy) * rows + h * part, part)]

    def pass_g(name, zz, xx, h, peer):
        push(name, h, g_at(zz, xx, h), g_at(zz, xx, h), peer)

    def pass_d(name, xx, yy, h, peer):
        push(name, h, d_at(xx, yy, h), d_at(xx, yy, h), peer)

    keep_d = pltpu.make_async_copy(e_ref, d_ref.at[pl.ds(fiber_of(xl, y) * rows, rows)], local.at[0])
    keep_g = pltpu.make_async_copy(e_ref, g_ref.at[pl.ds(blk_of(z, xh, c) * rows, rows)], local.at[1])
    keep_d.start()
    keep_g.start()
    meet(to)
    for h in range(CHUNKS):
        push("xh", h, e_at(h), g_at(z, xh, h), "xh")
        push("xl", h, e_at(h), d_at(xl, y, h), "xl")
        push("z+", h, e_at(h), g_at(z, xh, h), "z+")
        push("y+", h, e_at(h), d_at(xl, y, h), "y+")
        push("z-", h, e_at(h), g_at(z, xh, h), "z-")
        push("y-", h, e_at(h), d_at(xl, y, h), "y-")
    for h in range(CHUNKS):
        push("s0", h, e_at(h), g_at(z, xh, h), "sib")
    for h in range(CHUNKS):
        got("xl", h)
        pass_d("xl-", 1 - xl, y, h, "y-")
        pass_d("xl+", 1 - xl, y, h, "y+")
        got("xh", h)
        pass_g("xh-", z, 1 - xh, h, "z-")
        pass_g("xh+", z, 1 - xh, h, "z+")
        pass_g("s2", z, 1 - xh, h, "sib")
    for h in range(CHUNKS):
        got("z+", h)
        pass_g("z++", z + 3, xh, h, "z+")
        pass_g("s1", z + 3, xh, h, "sib")
        got("y+", h)
        pass_d("y++", xl, y + 3, h, "y+")
        got("z-", h)
        pass_g("s3", z + 1, xh, h, "sib")
        got("y-", h)
    for h in range(CHUNKS):
        got("xl-", h)
        pass_d("xl--", 1 - xl, y + 1, h, "y-")
        got("xh-", h)
        pass_g("xh--", z + 1, 1 - xh, h, "z-")
        pass_g("s4", z + 1, 1 - xh, h, "sib")
    for h in range(CHUNKS):
        got("xh+", h)
        pass_g("s6", z + 3, 1 - xh, h, "sib")
        got("z++", h)
        pass_g("s5", z + 2, xh, h, "sib")
        got("xh--", h)
        pass_g("s7", z + 2, 1 - xh, h, "sib")
    for h in range(CHUNKS):
        for name in ("xl+", "y++", "xl--", "s0", "s1", "s2", "s3", "s4", "s5", "s6", "s7"):
            got(name, h)
    for copy in copies.values():
        copy.wait_send()
    keep_d.wait()
    keep_g.wait()


def gather(e):
    rows, width = e.shape
    return pl.pallas_call(
        gather_kernel,
        out_shape=(
            jax.ShapeDtypeStruct((XS * YS * rows, width), e.dtype),
            jax.ShapeDtypeStruct((ZS * XS * 2 * rows, width), e.dtype),
        ),
        in_specs=[pl.BlockSpec(memory_space=pl.ANY)],
        out_specs=(pl.BlockSpec(memory_space=pl.ANY),) * 2,
        scratch_shapes=[
            pltpu.SemaphoreType.DMA((22 * CHUNKS,)),
            pltpu.SemaphoreType.DMA((22 * CHUNKS,)),
            pltpu.SemaphoreType.DMA((2,)),
        ],
        compiler_params=pltpu.CompilerParams(collective_id=0, has_side_effects=True),
    )(e)


def pair_kernel(
    dest_ref, source_ref, count_ref, pattern_ref, neg_dest_ref, neg_source_ref,
    bank_hbm, d_hbm, g_hbm, dp_ref, sp_ref,
    list_ref, open_ref, d_v, g_v, gt_v, bank_v, sems,
):
    stops, cap = dest_ref.shape
    neg = neg_dest_ref.shape[1]
    banks = bank_hbm.shape[0]
    sub = g_hbm.shape[0] // T // stops
    empty = d_hbm.shape[0] // T
    loads = [
        pltpu.make_async_copy(d_hbm, d_v.at[pl.ds(0, d_hbm.shape[0])], sems.at[0]),
        pltpu.make_async_copy(g_hbm, g_v, sems.at[1]),
        pltpu.make_async_copy(bank_hbm, bank_v.at[pl.ds(0, banks)], sems.at[2]),
    ]
    for load in loads:
        load.start()
    d_v[pl.ds(d_hbm.shape[0], T)] = jnp.zeros((T, d_v.shape[1]), d_v.dtype)
    bank_v[banks] = jnp.zeros(bank_v.shape[1:], bank_v.dtype)

    def clear(ref):
        def one(i, carry):
            ref[i] = jnp.zeros(ref.shape[1:], ref.dtype)
            return carry

        lax.fori_loop(0, ref.shape[0], one, 0)

    clear(dp_ref)
    clear(sp_ref)

    b = lax.axis_index("blk")

    def add_slot(pairs, group, src, code):
        held = open_ref[src]
        fresh = held < 0
        list_ref[jnp.where(fresh, 2 * pairs, held)] = code | (group << (DEST_BITS + BANK_BITS))
        open_ref[src] = jnp.where(fresh, 2 * pairs + 1, -1)
        return pairs + fresh.astype(jnp.int32)

    def preset(i, carry):
        list_ref[i] = empty
        return carry

    lax.fori_loop(0, list_ref.shape[0], preset, 0, unroll=8)

    def add_stop(stop, pairs):
        group = lax.rem(b - stop + stops, stops) * sub
        for q in range(sub):
            open_ref[q] = -1
        for k in range(neg):
            src = neg_source_ref[stop, k]
            pairs = add_slot(pairs, group + src, src, (banks << DEST_BITS) | neg_dest_ref[stop, k])

        def listed(k, pairs):
            src = source_ref[stop, k]
            return add_slot(pairs, group + src, src, (pattern_ref[stop, k] << DEST_BITS) | dest_ref[stop, k])

        return lax.fori_loop(0, count_ref[stop], listed, pairs)

    pairs = lax.fori_loop(0, stops, add_stop, 0)
    for load in loads:
        load.wait()

    def turn(i, carry):
        gt_v[i] = g_v[pl.ds(i * T, T), :].T
        return carry

    lax.fori_loop(0, gt_v.shape[0], turn, 0)
    one_bit = jnp.left_shift(1, lax.broadcasted_iota(jnp.int32, (32, T), 0))

    def mask_less_half(index):
        words = bank_v[index]
        return jnp.concatenate(
            [
                jnp.where((jnp.broadcast_to(words[k : k + 1, :], (32, T)) & one_bit) != 0, 0.5, -0.5)
                for k in range(words.shape[0])
            ],
            axis=0,
        )

    def first(i):
        codes = [list_ref[2 * i], list_ref[2 * i + 1]]
        g = codes[0] >> (DEST_BITS + BANK_BITS)
        p = [code & (2**DEST_BITS - 1) for code in codes]
        ids = [(code >> DEST_BITS) & (2**BANK_BITS - 1) for code in codes]
        zq = g_v[pl.ds(pl.multiple_of(g * T, T), T), :]
        zp = jnp.concatenate([d_v[pl.ds(pl.multiple_of(k * T, T), T), :] for k in p], axis=0)
        s = lax.dot_general(zq, zp, (((1,), (1,)), ((), ())), preferred_element_type=jnp.float32)
        m = jnp.concatenate([mask_less_half(k) for k in ids], axis=1)
        r = (m - 0.5 * jnp.tanh(0.5 * s)).astype(jnp.bfloat16)
        return g, p, zp, r

    def second(g, p, zp, r):
        to_source = jnp.dot(r, zp, preferred_element_type=jnp.float32)
        to_dest = jnp.dot(gt_v[g], r, preferred_element_type=jnp.float32)
        sp_ref[g] += to_source
        dp_ref[p[0]] += to_dest[:, :T]
        dp_ref[p[1]] += to_dest[:, T:]

    def body(step, carry):
        for held in [first(step * UNROLL + u) for u in range(UNROLL)]:
            second(*held)
        return carry

    lax.fori_loop(0, (pairs + UNROLL - 1) // UNROLL, body, 0)


def pair_sums(dest, source, count, pattern, neg_dest, neg_source, bank, d, g):
    nd, ng = d.shape[0] // T, g.shape[0] // T
    width = d.shape[1]
    stops, cap = dest.shape
    sub = ng // stops
    most = stops * ((cap + neg_dest.shape[1] + sub) // 2) + UNROLL
    smem = pl.BlockSpec(memory_space=pltpu.SMEM)
    hbm = pl.BlockSpec(memory_space=pl.ANY)
    return pl.pallas_call(
        pair_kernel,
        out_shape=(
            jax.ShapeDtypeStruct((nd + 1, width, T), jnp.float32),
            jax.ShapeDtypeStruct((ng, T, width), jnp.float32),
        ),
        in_specs=[smem] * 6 + [hbm] * 3,
        out_specs=(pl.BlockSpec(memory_space=pltpu.VMEM),) * 2,
        scratch_shapes=[
            pltpu.SMEM((2 * most,), jnp.int32),
            pltpu.SMEM((sub,), jnp.int32),
            pltpu.VMEM(((nd + 1) * T, width), jnp.bfloat16),
            pltpu.VMEM((ng * T, width), jnp.bfloat16),
            pltpu.VMEM((ng, width, T), jnp.bfloat16),
            pltpu.VMEM((bank.shape[0] + 1,) + bank.shape[1:], bank.dtype),
            pltpu.SemaphoreType.DMA((3,)),
        ],
        compiler_params=pltpu.CompilerParams(vmem_limit_bytes=VMEM_LIMIT),
    )(dest, source, count, pattern, neg_dest, neg_source, bank, d, g)


def code16(value_at, blocks, dst, amax):
    height = (dst.shape[0] - 16) // blocks
    power = jnp.ceil(jnp.log2(jnp.maximum(amax, 1e-37)))
    gain = jnp.exp2(-power) * 32767.0

    def one(i, carry):
        q = jnp.clip(jnp.round(value_at(i) * gain), -32767.0, 32767.0)
        dst[pl.ds(pl.multiple_of(i * height, height), height), :] = q.astype(jnp.int32).astype(jnp.int16)
        return carry

    lax.fori_loop(0, blocks, one, 0)
    dst[pl.ds(blocks * height, 16), :] = jnp.broadcast_to(power, (16, power.shape[1])).astype(jnp.int32).astype(jnp.int16)


def reduce_kernel(
    scale, dp_hbm, sp_hbm, out_ref,
    dest, own, core, s_send, s_recv, d_send, d_recv, send, recv, local,
):
    sub = own.shape[1]
    width = own.shape[3]
    per = sub // CHUNKS
    z, xh, c, xl, y = place()
    to = peers()
    copies = {}

    def push(name, src, dst, peer):
        k = len(copies)
        copies[name] = pltpu.make_async_remote_copy(
            src_ref=src,
            dst_ref=dst,
            send_sem=send.at[k],
            recv_sem=recv.at[k],
            device_id=to[peer],
            device_id_type=MESH,
        )
        copies[name].start()

    def got(name):
        copies[name].wait_recv()

    order = [(2, 0), (2, 1), (1, 1), (3, 0), (1, 0), (3, 1), (0, 0), (0, 1)]
    dest_loads, own_loads = [], []
    for n, (dy, xx) in enumerate(order):
        first = pl.ds(fiber_of(xx, y + dy) * sub, sub)
        dest_loads.append(pltpu.make_async_copy(dp_hbm.at[first], dest.at[n], local.at[n]))
        dest_loads[-1].start()
    for n, (dz, xx) in enumerate(order):
        first = pl.ds(blk_of(z + dz, xx, c) * sub, sub)
        own_loads.append(pltpu.make_async_copy(sp_hbm.at[first], own.at[n], local.at[8 + n]))
        own_loads[-1].start()
    meet(to)
    for n, (dz, xx) in enumerate(order):
        first = pl.ds(blk_of(z + dz, xx, 1 - c) * sub, sub)
        push(f"c{n}", sp_hbm.at[first], core.at[n], "sib")

    def decoded(ref, h, height):
        gain = jnp.exp2(ref[h, pl.ds(per * height, 16), :].astype(jnp.float32)[:1]) * (1.0 / 32767.0)

        def at(i):
            rows = pl.ds(pl.multiple_of(i * height, height), height)
            return ref[h, rows, :].astype(jnp.float32) * gain

        return at

    def plain(ref, h):
        return lambda i: ref[h * per + i]

    def total(parts, keep, h):
        def one(i, most):
            value = parts[0](i)
            for part in parts[1:]:
                value = value + part(i)
            keep[h * per + i] = value
            return jnp.maximum(most, jnp.max(jnp.abs(value), axis=0, keepdims=True))

        return lax.fori_loop(0, per, one, jnp.zeros((1, keep.shape[2]), jnp.float32))

    def hand_on(name, parts, keep, h, out_buf, in_buf, peer):
        amax = total(parts, keep, h)
        code16(plain(keep, h), per, out_buf.at[h], amax)
        push(name + str(h), out_buf.at[h], in_buf.at[h], peer)

    def z_send(k, h, peer, *parts):
        hand_on(f"z{k}", parts, core.at[k], h, s_send.at[k], s_recv.at[k], peer)

    def y_send(k, h, peer, *parts):
        hand_on(f"y{k}", parts, dest.at[k], h, d_send.at[k], d_recv.at[k], peer)

    def s_in(name, k, h):
        got(name + str(h))
        return decoded(s_recv.at[k], h, T)

    def d_in(name, k, h):
        got(name + str(h))
        return decoded(d_recv.at[k], h, width)

    def cores(n, h):
        return plain(core.at[n], h), plain(own.at[n], h)

    def ready(n):
        own_loads[n].wait()
        got(f"c{n}")

    dest_loads[0].wait()
    y_send(0, 0, "y+", plain(dest.at[0], 0))
    dest_loads[1].wait()
    y_send(1, 0, "y-", plain(dest.at[1], 0))
    ready(0)
    z_send(0, 0, "z+", *cores(0, 0))
    ready(1)
    z_send(1, 0, "z-", *cores(1, 0))
    ready(2)
    ready(3)
    dest_loads[2].wait()
    dest_loads[3].wait()
    for h in range(CHUNKS):
        if h:
            y_send(0, h, "y+", plain(dest.at[0], h))
            y_send(1, h, "y-", plain(dest.at[1], h))
            z_send(0, h, "z+", *cores(0, h))
            z_send(1, h, "z-", *cores(1, h))
        else:
            y_send(2, h, "y+", plain(dest.at[2], h))
            y_send(3, h, "y-", plain(dest.at[3], h))
            z_send(2, h, "z+", *cores(2, h))
            z_send(3, h, "z-", *cores(3, h))
    for n in range(4, 8):
        ready(n)
        dest_loads[n].wait()
    for h in range(CHUNKS):
        y_send(4, h, "y+", plain(dest.at[4], h), d_in("y0", 0, h))
        y_send(5, h, "y-", plain(dest.at[5], h), d_in("y1", 1, h))
        z_send(4, h, "z+", *cores(4, h), s_in("z0", 0, h))
        z_send(5, h, "z-", *cores(5, h), s_in("z1", 1, h))
    for h in range(1, CHUNKS):
        y_send(2, h, "y+", plain(dest.at[2], h))
        y_send(3, h, "y-", plain(dest.at[3], h))
        z_send(2, h, "z+", *cores(2, h))
        z_send(3, h, "z-", *cores(3, h))
    for h in range(CHUNKS):
        most_d = [
            total((plain(dest.at[6], h), d_in("y3", 3, h), d_in("y4", 4, h)), dest.at[6], h),
            total((plain(dest.at[7], h), d_in("y2", 2, h), d_in("y5", 5, h)), dest.at[7], h),
        ]
        code16(plain(dest.at[7 - xl], h), per, d_send.at[6, h], jnp.where(xl == 0, most_d[1], most_d[0]))
        push(f"xl{h}", d_send.at[6, h], d_recv.at[6, h], "xl")
        most_s = [
            total((*cores(6, h), s_in("z3", 3, h), s_in("z4", 4, h)), core.at[6], h),
            total((*cores(7, h), s_in("z2", 2, h), s_in("z5", 5, h)), core.at[7], h),
        ]
        code16(plain(core.at[7 - xh], h), per, s_send.at[6, h], jnp.where(xh == 0, most_s[1], most_s[0]))
        push(f"xh{h}", s_send.at[6, h], s_recv.at[6, h], "xh")
    for h in range(CHUNKS):
        from_xl = d_in("xl", 6, h)
        from_xh = s_in("xh", 6, h)

        def finish(i, carry):
            by_dest = dest[6 + xl, h * per + i] + from_xl(i)
            by_source = core[6 + xh, h * per + i] + from_xh(i)
            rows = pl.ds(pl.multiple_of((h * per + i) * T, T), T)
            out_ref[rows, :] = (by_source + by_dest.T) * scale
            return carry

        lax.fori_loop(0, per, finish, 0)
    for copy in copies.values():
        copy.wait_send()


def reduce_sums(dp, sp, rows, scale):
    width = sp.shape[2]
    sub = rows // T
    per = sub // CHUNKS
    return pl.pallas_call(
        functools.partial(reduce_kernel, scale),
        out_shape=jax.ShapeDtypeStruct((rows, width), jnp.float32),
        in_specs=[pl.BlockSpec(memory_space=pl.ANY)] * 2,
        out_specs=pl.BlockSpec(memory_space=pltpu.VMEM),
        scratch_shapes=[
            pltpu.VMEM((8, sub, width, T), jnp.float32),
            pltpu.VMEM((8, sub, T, width), jnp.float32),
            pltpu.VMEM((8, sub, T, width), jnp.float32),
            pltpu.VMEM((7, CHUNKS, per * T + 16, width), jnp.int16),
            pltpu.VMEM((7, CHUNKS, per * T + 16, width), jnp.int16),
            pltpu.VMEM((7, CHUNKS, per * width + 16, T), jnp.int16),
            pltpu.VMEM((7, CHUNKS, per * width + 16, T), jnp.int16),
            pltpu.SemaphoreType.DMA((8 + 14 * CHUNKS,)),
            pltpu.SemaphoreType.DMA((8 + 14 * CHUNKS,)),
            pltpu.SemaphoreType.DMA((16,)),
        ],
        compiler_params=pltpu.CompilerParams(
            collective_id=1, has_side_effects=True, vmem_limit_bytes=VMEM_LIMIT
        ),
    )(dp, sp)


def on_device(
    embedding, tile_dest, tile_source, tile_count, pattern_id, pattern_bank, negative_dest, negative_source
):
    rows = embedding.shape[0]
    d, g = gather(embedding)
    dp, sp = pair_sums(
        tile_dest[0, 0],
        tile_source[0, 0],
        tile_count[0, 0],
        pattern_id[0, 0],
        negative_dest[0, 0],
        negative_source[0, 0],
        pattern_bank,
        d,
        g,
    )
    scale = 1.0 / math.sqrt(T * tile_dest.shape[2])
    return reduce_sums(dp, sp, rows, scale)


def solution(mesh):
    in_specs = (
        P(("blk", "fiber"), None),
        P("blk", "fiber", None, None),
        P("blk", "fiber", None, None),
        P("blk", "fiber", None),
        P("blk", "fiber", None, None),
        P(),
        P("blk", "fiber", None, None),
        P("blk", "fiber", None, None),
    )
    out_specs = P(("blk", "fiber"), None)
    return jax.shard_map(
        on_device, mesh=mesh, in_specs=in_specs, out_specs=out_specs, check_vma=False
    )
```

```python
import functools
import math

import jax
import jax.numpy as jnp
from jax import lax
from jax.experimental import pallas as pl
from jax.experimental.pallas import tpu as pltpu
from jax.sharding import PartitionSpec as P

ZS, XS, YS = 4, 2, 4
T = 128
MESH = pl.DeviceIdType.MESH
UNROLL = 6
CHUNKS = 2
PARTS = 4
PAIR_VMEM, REDUCE_VMEM = 30, 36
DEST_BITS, BANK_BITS = 6, 7


def place():
    b, f = lax.axis_index("blk"), lax.axis_index("fiber")
    return b // 4, (b // 2) % 2, b % 2, f // YS, f % YS


def blk_of(z, xh, c):
    return ((z % ZS) * XS + xh) * 2 + c


def fiber_of(xl, y):
    return xl * YS + y % YS


def peers():
    z, xh, c, xl, y = place()
    b, f = blk_of(z, xh, c), fiber_of(xl, y)
    return {
        "sib": (blk_of(z, xh, 1 - c), f),
        "xh": (blk_of(z, 1 - xh, c), f),
        "z+": (blk_of(z + 1, xh, c), f),
        "z-": (blk_of(z + 3, xh, c), f),
        "xl": (b, fiber_of(1 - xl, y)),
        "y+": (b, fiber_of(xl, y + 1)),
        "y-": (b, fiber_of(xl, y + 3)),
    }


def meet(to):
    barrier = pltpu.get_barrier_semaphore()
    for device in to.values():
        pl.semaphore_signal(barrier, inc=1, device_id=device, device_id_type=MESH)
    pl.semaphore_wait(barrier, len(to))


def gather_kernel(e_ref, d_ref, g_ref, send, recv, local):
    rows = e_ref.shape[0]
    part = rows // PARTS
    z, xh, c, xl, y = place()
    to = peers()
    copies = {}

    def push(name, src, dst, peer):
        k = len(copies)
        copies[name] = pltpu.make_async_remote_copy(
            src_ref=src,
            dst_ref=dst,
            send_sem=send.at[k],
            recv_sem=recv.at[k],
            device_id=to[peer],
            device_id_type=MESH,
        )
        copies[name].start()

    def got(name, h):
        copies[name, h].wait_recv()

    def e_at(h):
        return e_ref.at[pl.ds(h * part, part)]

    def g_at(zz, xx, h):
        return g_ref.at[pl.ds(blk_of(zz, xx, c) * rows + h * part, part)]

    def d_at(xx, yy, h):
        return d_ref.at[pl.ds(fiber_of(xx, yy) * rows + h * part, part)]

    def pass_g(name, zz, xx, h, peer):
        push((name, h), g_at(zz, xx, h), g_at(zz, xx, h), peer)

    def pass_d(name, xx, yy, h, peer):
        push((name, h), d_at(xx, yy, h), d_at(xx, yy, h), peer)

    def share(zz, xx, src=None):
        whole = g_ref.at[pl.ds(blk_of(zz, xx, c) * rows, rows)]
        push(("sib", len(copies)), whole if src is None else src, whole, "sib")

    keep_d = pltpu.make_async_copy(e_ref, d_ref.at[pl.ds(fiber_of(xl, y) * rows, rows)], local.at[0])
    keep_g = pltpu.make_async_copy(e_ref, g_ref.at[pl.ds(blk_of(z, xh, c) * rows, rows)], local.at[1])
    keep_d.start()
    keep_g.start()
    meet(to)
    for h in range(PARTS):
        push(("xh", h), e_at(h), g_at(z, xh, h), "xh")
        push(("xl", h), e_at(h), d_at(xl, y, h), "xl")
        push(("z+", h), e_at(h), g_at(z, xh, h), "z+")
        push(("y+", h), e_at(h), d_at(xl, y, h), "y+")
        push(("z-", h), e_at(h), g_at(z, xh, h), "z-")
        push(("y-", h), e_at(h), d_at(xl, y, h), "y-")

    def second_hop(h):
        got("xl-", h)
        pass_d("xl--", 1 - xl, y + 1, h, "y-")
        got("xh-", h)
        pass_g("xh--", z + 1, 1 - xh, h, "z-")

    for h in range(PARTS):
        got("z+", h)
        pass_g("z++", z + 3, xh, h, "z+")
        got("y+", h)
        pass_d("y++", xl, y + 3, h, "y+")
        got("xl", h)
        pass_d("xl-", 1 - xl, y, h, "y-")
        pass_d("xl+", 1 - xl, y, h, "y+")
        got("xh", h)
        pass_g("xh-", z, 1 - xh, h, "z-")
        pass_g("xh+", z, 1 - xh, h, "z+")
        if h:
            second_hop(h - 1)
    share(z, xh, e_ref)
    share(z + 3, xh)
    share(z, 1 - xh)
    second_hop(PARTS - 1)
    share(z + 1, 1 - xh)
    for name, zz, xx in (("z-", z + 1, xh), ("z++", z + 2, xh), ("xh+", z + 3, 1 - xh), ("xh--", z + 2, 1 - xh)):
        for h in range(PARTS):
            got(name, h)
        share(zz, xx)
    for h in range(PARTS):
        for name in ("y-", "xl+", "y++", "xl--"):
            got(name, h)
    for (name, _), copy in copies.items():
        if name == "sib":
            copy.wait_recv()
    for copy in copies.values():
        copy.wait_send()
    keep_d.wait()
    keep_g.wait()


def gather(e):
    rows, width = e.shape
    copies = 14 * PARTS + 8
    return pl.pallas_call(
        gather_kernel,
        out_shape=(
            jax.ShapeDtypeStruct((XS * YS * rows, width), e.dtype),
            jax.ShapeDtypeStruct((ZS * XS * 2 * rows, width), e.dtype),
        ),
        in_specs=[pl.BlockSpec(memory_space=pl.ANY)],
        out_specs=(pl.BlockSpec(memory_space=pl.ANY),) * 2,
        scratch_shapes=[
            pltpu.SemaphoreType.DMA((copies,)),
            pltpu.SemaphoreType.DMA((copies,)),
            pltpu.SemaphoreType.DMA((2,)),
        ],
        compiler_params=pltpu.CompilerParams(
            collective_id=0, has_side_effects=True, vmem_limit_bytes=4 << 20
        ),
    )(e)


def pair_kernel(
    dest_ref, source_ref, count_ref, pattern_ref, neg_dest_ref, neg_source_ref, bank_ref, d_ref, g_ref,
    dp_ref, sp_ref, list_ref, open_ref, gt_v,
):
    stops, cap = dest_ref.shape[2:]
    neg = neg_dest_ref.shape[2]
    sub = sp_ref.shape[0] // stops
    per = dp_ref.shape[0] // stops
    dump = list_ref.shape[0] - 1
    b = lax.axis_index("blk")

    def preset(i, carry):
        list_ref[i] = 0
        return carry

    lax.fori_loop(0, list_ref.shape[0], preset, 0, unroll=16)

    def add_slot(pairs, src, code, live):
        held = open_ref[src]
        fresh = held < 0
        at = jnp.where(fresh, 2 * pairs, held)
        list_ref[jnp.where(live, at, dump)] = (code << 2) | 2
        open_ref[src] = jnp.where(live, jnp.where(fresh, 2 * pairs + 1, -1), held)
        return pairs + jnp.where(live & fresh, 1, 0)

    def add_stop(stop, pairs):
        group = lax.rem(b - stop + stops, stops) * sub
        count = count_ref[0, 0, stop]
        for q in range(sub):
            open_ref[q] = -1
            tile = stop * sub + q
            gt_v[tile] = g_ref[pl.ds(pl.multiple_of(tile * T, T), T), :].T
            sp_ref[tile] = jnp.zeros(sp_ref.shape[1:], sp_ref.dtype)
        for q in range(per):
            dp_ref[stop * per + q] = jnp.zeros(dp_ref.shape[1:], dp_ref.dtype)

        def code(src, index, dest, negative):
            return ((((group + src) << BANK_BITS) | index) << DEST_BITS | dest) << 1 | negative

        for k in range(neg):
            src = neg_source_ref[0, 0, k, stop]
            pairs = add_slot(pairs, src, code(src, 0, neg_dest_ref[0, 0, k, stop], 1), True)
        for k in range(cap):
            src = source_ref[0, 0, stop, k]
            value = code(src, pattern_ref[0, 0, stop, k], dest_ref[0, 0, stop, k], 0)
            pairs = add_slot(pairs, src, value, k < count)
        return pairs

    pairs = lax.fori_loop(0, stops, add_stop, 0)
    one_bit = jnp.left_shift(1, lax.broadcasted_iota(jnp.int32, (32, T), 0))

    def mask_less_half(index, keep):
        words = bank_ref[index] & keep
        return jnp.concatenate(
            [
                jnp.where((jnp.broadcast_to(words[k : k + 1, :], (32, T)) & one_bit) != 0, 0.5, -0.5)
                for k in range(words.shape[0])
            ],
            axis=0,
        )

    def first(i):
        codes = [list_ref[2 * i], list_ref[2 * i + 1]]
        g = codes[0] >> (DEST_BITS + BANK_BITS + 3)
        p = [(code >> 3) & (2**DEST_BITS - 1) for code in codes]
        ids = [(code >> (DEST_BITS + 3)) & (2**BANK_BITS - 1) for code in codes]
        keep = [((code >> 2) & 1) - 1 for code in codes]
        live = [((code >> 1) & 1).astype(jnp.float32) for code in codes]
        zq = g_ref[pl.ds(pl.multiple_of(g * T, T), T), :]
        zp = jnp.concatenate([d_ref[pl.ds(pl.multiple_of(k * T, T), T), :] for k in p], axis=0)
        s = lax.dot_general(zq, zp, (((1,), (1,)), ((), ())), preferred_element_type=jnp.float32)
        half = 0.5 * jnp.tanh(0.5 * s)
        r = jnp.concatenate(
            [live[u] * (mask_less_half(ids[u], keep[u]) - half[:, u * T : (u + 1) * T]) for u in range(2)], axis=1
        ).astype(jnp.bfloat16)
        return g, p, zp, r

    def second(g, p, zp, r):
        to_source = jnp.dot(r, zp, preferred_element_type=jnp.float32)
        to_dest = jnp.dot(gt_v[g], r, preferred_element_type=jnp.float32)
        sp_ref[g] += to_source
        dp_ref[p[0]] += to_dest[:, :T]
        dp_ref[p[1]] += to_dest[:, T:]

    def body(step, carry):
        for held in [first(step * UNROLL + u) for u in range(UNROLL)]:
            second(*held)
        return carry

    lax.fori_loop(0, (pairs + UNROLL - 1) // UNROLL, body, 0)


def pair_sums(dest, source, count, pattern, neg_dest, neg_source, bank, d, g):
    nd, ng = d.shape[0] // T, g.shape[0] // T
    width = d.shape[1]
    stops, cap = dest.shape[2:]
    sub = ng // stops
    most = stops * ((cap + neg_dest.shape[2] + sub) // 2) + UNROLL
    most += (-most) % 8 + 8
    smem = pl.BlockSpec(memory_space=pltpu.SMEM)
    vmem = pl.BlockSpec(memory_space=pltpu.VMEM)
    return pl.pallas_call(
        pair_kernel,
        out_shape=(
            jax.ShapeDtypeStruct((nd, width, T), jnp.float32),
            jax.ShapeDtypeStruct((ng, T, width), jnp.float32),
        ),
        in_specs=[smem] * 6 + [vmem] * 3,
        out_specs=(vmem, vmem),
        scratch_shapes=[
            pltpu.SMEM((2 * most,), jnp.int32),
            pltpu.SMEM((sub,), jnp.int32),
            pltpu.VMEM((ng, width, T), jnp.bfloat16),
        ],
        compiler_params=pltpu.CompilerParams(vmem_limit_bytes=PAIR_VMEM << 20),
    )(dest, source, count, pattern, neg_dest, neg_source, bank, d, g)


def code16(value_at, blocks, dst, amax):
    height = (dst.shape[0] - 16) // blocks
    power = jnp.ceil(jnp.log2(jnp.maximum(amax, 1e-37)))
    gain = jnp.exp2(-power) * 32767.0

    def one(i, carry):
        q = jnp.clip(jnp.round(value_at(i) * gain), -32767.0, 32767.0)
        dst[pl.ds(pl.multiple_of(i * height, height), height), :] = q.astype(jnp.int32).astype(jnp.int16)
        return carry

    lax.fori_loop(0, blocks, one, 0)
    dst[pl.ds(blocks * height, 16), :] = jnp.broadcast_to(power, (16, power.shape[1])).astype(jnp.int32).astype(jnp.int16)


def reduce_kernel(
    scale, dp_ref, sp_ref, out_ref, dest, core, s_send, s_recv, d_send, d_recv, send, recv
):
    sub = core.shape[1]
    width = core.shape[3]
    per = sub // CHUNKS
    z, xh, c, xl, y = place()
    to = peers()
    copies = {}

    def push(name, src, dst, peer):
        k = len(copies)
        copies[name] = pltpu.make_async_remote_copy(
            src_ref=src,
            dst_ref=dst,
            send_sem=send.at[k],
            recv_sem=recv.at[k],
            device_id=to[peer],
            device_id_type=MESH,
        )
        copies[name].start()

    def got(name):
        copies[name].wait_recv()

    order = [(2, 0), (2, 1), (1, 1), (3, 0), (1, 0), (3, 1), (0, 0), (0, 1)]

    def s_at(n, core_at):
        dz, xx = order[n]
        return sp_ref.at[pl.ds(blk_of(z + dz, xx, core_at) * sub, sub)]

    def mine(n, h):
        dy, xx = order[n]
        return plain(dp_ref.at[pl.ds(fiber_of(xx, y + dy) * sub, sub)], h)

    meet(to)
    for n in range(8):
        push(f"c{n}", s_at(n, 1 - c), core.at[n], "sib")

    def decoded(ref, h, height):
        gain = jnp.exp2(ref[h, pl.ds(per * height, 16), :].astype(jnp.float32)[:1]) * (1.0 / 32767.0)

        def at(i):
            rows = pl.ds(pl.multiple_of(i * height, height), height)
            return ref[h, rows, :].astype(jnp.float32) * gain

        return at

    def plain(ref, h):
        return lambda i: ref[h * per + i]

    def total(parts, keep, h):
        def one(i, most):
            value = parts[0](i)
            for part in parts[1:]:
                value = value + part(i)
            keep[h * per + i] = value
            return jnp.maximum(most, jnp.max(jnp.abs(value), axis=0, keepdims=True))

        return lax.fori_loop(0, per, one, jnp.zeros((1, keep.shape[2]), jnp.float32))

    def hand_on(name, parts, keep, h, out_buf, in_buf, peer):
        amax = total(parts, keep, h)
        code16(plain(keep, h), per, out_buf.at[h], amax)
        push(name + str(h), out_buf.at[h], in_buf.at[h], peer)

    def z_send(k, h, peer, *parts):
        hand_on(f"z{k}", parts, core.at[k], h, s_send.at[k], s_recv.at[k], peer)

    def y_send(k, h, peer, *parts):
        hand_on(f"y{k}", parts, dest.at[k], h, d_send.at[k], d_recv.at[k], peer)

    def s_in(name, k, h):
        got(name + str(h))
        return decoded(s_recv.at[k], h, T)

    def d_in(name, k, h):
        got(name + str(h))
        return decoded(d_recv.at[k], h, width)

    def cores(n, h):
        return plain(core.at[n], h), plain(s_at(n, c), h)

    y_send(0, 0, "y+", mine(0, 0))
    y_send(1, 0, "y-", mine(1, 0))
    got("c0")
    z_send(0, 0, "z+", *cores(0, 0))
    got("c1")
    z_send(1, 0, "z-", *cores(1, 0))
    for h in range(1, CHUNKS):
        y_send(0, h, "y+", mine(0, h))
        y_send(1, h, "y-", mine(1, h))
        z_send(0, h, "z+", *cores(0, h))
        z_send(1, h, "z-", *cores(1, h))
    for n in range(2, 8):
        got(f"c{n}")
    for h in range(CHUNKS):
        y_send(2, h, "y+", mine(2, h))
        y_send(3, h, "y-", mine(3, h))
        z_send(2, h, "z+", *cores(2, h))
        z_send(3, h, "z-", *cores(3, h))
        y_send(4, h, "y+", mine(4, h), d_in("y0", 0, h))
        y_send(5, h, "y-", mine(5, h), d_in("y1", 1, h))
        z_send(4, h, "z+", *cores(4, h), s_in("z0", 0, h))
        z_send(5, h, "z-", *cores(5, h), s_in("z1", 1, h))
    for h in range(CHUNKS):
        most_d = [
            total((mine(6, h), d_in("y3", 3, h), d_in("y4", 4, h)), dest.at[6], h),
            total((mine(7, h), d_in("y2", 2, h), d_in("y5", 5, h)), dest.at[7], h),
        ]
        code16(plain(dest.at[7 - xl], h), per, d_send.at[6, h], jnp.where(xl == 0, most_d[1], most_d[0]))
        push(f"xl{h}", d_send.at[6, h], d_recv.at[6, h], "xl")
        most_s = [
            total((*cores(6, h), s_in("z3", 3, h), s_in("z4", 4, h)), core.at[6], h),
            total((*cores(7, h), s_in("z2", 2, h), s_in("z5", 5, h)), core.at[7], h),
        ]
        code16(plain(core.at[7 - xh], h), per, s_send.at[6, h], jnp.where(xh == 0, most_s[1], most_s[0]))
        push(f"xh{h}", s_send.at[6, h], s_recv.at[6, h], "xh")
    for h in range(CHUNKS):
        from_xl = d_in("xl", 6, h)
        from_xh = s_in("xh", 6, h)

        def finish(i, carry):
            by_dest = dest[6 + xl, h * per + i] + from_xl(i)
            by_source = core[6 + xh, h * per + i] + from_xh(i)
            rows = pl.ds(pl.multiple_of((h * per + i) * T, T), T)
            out_ref[rows, :] = (by_source + by_dest.T) * scale
            return carry

        lax.fori_loop(0, per, finish, 0)
    for copy in copies.values():
        copy.wait_send()


def reduce_sums(dp, sp, rows, scale):
    width = sp.shape[2]
    sub = rows // T
    per = sub // CHUNKS
    return pl.pallas_call(
        functools.partial(reduce_kernel, scale),
        out_shape=jax.ShapeDtypeStruct((rows, width), jnp.float32),
        in_specs=[pl.BlockSpec(memory_space=pltpu.VMEM)] * 2,
        out_specs=pl.BlockSpec(memory_space=pltpu.VMEM),
        scratch_shapes=[
            pltpu.VMEM((8, sub, width, T), jnp.float32),
            pltpu.VMEM((8, sub, T, width), jnp.float32),
            pltpu.VMEM((7, CHUNKS, per * T + 16, width), jnp.int16),
            pltpu.VMEM((7, CHUNKS, per * T + 16, width), jnp.int16),
            pltpu.VMEM((7, CHUNKS, per * width + 16, T), jnp.int16),
            pltpu.VMEM((7, CHUNKS, per * width + 16, T), jnp.int16),
            pltpu.SemaphoreType.DMA((8 + 14 * CHUNKS,)),
            pltpu.SemaphoreType.DMA((8 + 14 * CHUNKS,)),
        ],
        compiler_params=pltpu.CompilerParams(
            collective_id=1, has_side_effects=True, vmem_limit_bytes=REDUCE_VMEM << 20
        ),
    )(dp, sp)


def on_device(
    embedding, tile_dest, tile_source, tile_count, pattern_id, pattern_bank, negative_dest, negative_source
):
    rows = embedding.shape[0]
    d, g = gather(embedding)
    dp, sp = pair_sums(
        tile_dest,
        tile_source,
        tile_count,
        pattern_id,
        negative_dest.swapaxes(2, 3),
        negative_source.swapaxes(2, 3),
        pattern_bank,
        d,
        g,
    )
    scale = 1.0 / math.sqrt(T * tile_dest.shape[2])
    return reduce_sums(dp, sp, rows, scale)


def solution(mesh):
    in_specs = (
        P(("blk", "fiber"), None),
        P("blk", "fiber", None, None),
        P("blk", "fiber", None, None),
        P("blk", "fiber", None),
        P("blk", "fiber", None, None),
        P(),
        P("blk", "fiber", None, None),
        P("blk", "fiber", None, None),
    )
    out_specs = P(("blk", "fiber"), None)
    return jax.shard_map(
        on_device, mesh=mesh, in_specs=in_specs, out_specs=out_specs, check_vma=False
    )
```

```python
import functools
import math

import jax
import jax.numpy as jnp
from jax import lax
from jax.experimental import pallas as pl
from jax.experimental.pallas import tpu as pltpu
from jax.sharding import PartitionSpec as P

ZS, XS, YS = 4, 2, 4
T = 128
MESH = pl.DeviceIdType.MESH
UNROLL = 6
CHUNKS = 4
PARTS = 4
PAIR_VMEM, REDUCE_VMEM = 30, 36
SOURCE_BITS, DEST_BITS, BANK_BITS = 3, 6, 7
LIVE = 1 << (DEST_BITS + BANK_BITS)
NEGATIVE = LIVE << 1
G_AT = DEST_BITS + BANK_BITS + 2


def place():
    b, f = lax.axis_index("blk"), lax.axis_index("fiber")
    return b // 4, (b // 2) % 2, b % 2, f // YS, f % YS


def blk_of(z, xh, c):
    return ((z % ZS) * XS + xh) * 2 + c


def fiber_of(xl, y):
    return xl * YS + y % YS


def peers():
    z, xh, c, xl, y = place()
    b, f = blk_of(z, xh, c), fiber_of(xl, y)
    return {
        "sib": (blk_of(z, xh, 1 - c), f),
        "xh": (blk_of(z, 1 - xh, c), f),
        "z+": (blk_of(z + 1, xh, c), f),
        "z-": (blk_of(z + 3, xh, c), f),
        "xl": (b, fiber_of(1 - xl, y)),
        "y+": (b, fiber_of(xl, y + 1)),
        "y-": (b, fiber_of(xl, y + 3)),
    }


def meet(to):
    barrier = pltpu.get_barrier_semaphore()
    for device in to.values():
        pl.semaphore_signal(barrier, inc=1, device_id=device, device_id_type=MESH)
    pl.semaphore_wait(barrier, len(to))


def gather_kernel(e_ref, d_ref, g_ref, send, recv, local):
    rows = e_ref.shape[0]
    part = rows // PARTS
    z, xh, c, xl, y = place()
    to = peers()
    copies = {}

    def push(name, src, dst, peer):
        k = len(copies)
        copies[name] = pltpu.make_async_remote_copy(
            src_ref=src,
            dst_ref=dst,
            send_sem=send.at[k],
            recv_sem=recv.at[k],
            device_id=to[peer],
            device_id_type=MESH,
        )
        copies[name].start()

    def got(name, h):
        copies[name, h].wait_recv()

    def e_at(h):
        return e_ref.at[pl.ds(h * part, part)]

    def g_at(zz, xx, h):
        return g_ref.at[pl.ds(blk_of(zz, xx, c) * rows + h * part, part)]

    def d_at(xx, yy, h):
        return d_ref.at[pl.ds(fiber_of(xx, yy) * rows + h * part, part)]

    def pass_g(name, zz, xx, h, peer):
        push((name, h), g_at(zz, xx, h), g_at(zz, xx, h), peer)

    def pass_d(name, xx, yy, h, peer):
        push((name, h), d_at(xx, yy, h), d_at(xx, yy, h), peer)

    def share(zz, xx, src=None):
        whole = g_ref.at[pl.ds(blk_of(zz, xx, c) * rows, rows)]
        push(("sib", len(copies)), whole if src is None else src, whole, "sib")

    keep_d = pltpu.make_async_copy(e_ref, d_ref.at[pl.ds(fiber_of(xl, y) * rows, rows)], local.at[0])
    keep_g = pltpu.make_async_copy(e_ref, g_ref.at[pl.ds(blk_of(z, xh, c) * rows, rows)], local.at[1])
    keep_d.start()
    keep_g.start()
    meet(to)
    for h in range(PARTS):
        push(("xh", h), e_at(h), g_at(z, xh, h), "xh")
        push(("xl", h), e_at(h), d_at(xl, y, h), "xl")
        push(("z+", h), e_at(h), g_at(z, xh, h), "z+")
        push(("y+", h), e_at(h), d_at(xl, y, h), "y+")
        push(("z-", h), e_at(h), g_at(z, xh, h), "z-")
        push(("y-", h), e_at(h), d_at(xl, y, h), "y-")

    def second_hop(h):
        got("xl-", h)
        pass_d("xl--", 1 - xl, y + 1, h, "y-")
        got("xh-", h)
        pass_g("xh--", z + 1, 1 - xh, h, "z-")

    for h in range(PARTS):
        got("z+", h)
        pass_g("z++", z + 3, xh, h, "z+")
        got("y+", h)
        pass_d("y++", xl, y + 3, h, "y+")
        got("xl", h)
        pass_d("xl-", 1 - xl, y, h, "y-")
        pass_d("xl+", 1 - xl, y, h, "y+")
        got("xh", h)
        pass_g("xh-", z, 1 - xh, h, "z-")
        pass_g("xh+", z, 1 - xh, h, "z+")
        if h:
            second_hop(h - 1)
    share(z, xh, e_ref)
    share(z + 3, xh)
    share(z, 1 - xh)
    second_hop(PARTS - 1)
    share(z + 1, 1 - xh)
    for name, zz, xx in (("z-", z + 1, xh), ("z++", z + 2, xh), ("xh+", z + 3, 1 - xh), ("xh--", z + 2, 1 - xh)):
        for h in range(PARTS):
            got(name, h)
        share(zz, xx)
    for h in range(PARTS):
        for name in ("y-", "xl+", "y++", "xl--"):
            got(name, h)
    for (name, _), copy in copies.items():
        if name == "sib":
            copy.wait_recv()
    for copy in copies.values():
        copy.wait_send()
    keep_d.wait()
    keep_g.wait()


def gather(e):
    rows, width = e.shape
    copies = 14 * PARTS + 8
    return pl.pallas_call(
        gather_kernel,
        out_shape=(
            jax.ShapeDtypeStruct((XS * YS * rows, width), e.dtype),
            jax.ShapeDtypeStruct((ZS * XS * 2 * rows, width), e.dtype),
        ),
        in_specs=[pl.BlockSpec(memory_space=pl.ANY)],
        out_specs=(pl.BlockSpec(memory_space=pl.ANY),) * 2,
        scratch_shapes=[
            pltpu.SemaphoreType.DMA((copies,)),
            pltpu.SemaphoreType.DMA((copies,)),
            pltpu.SemaphoreType.DMA((2,)),
        ],
        compiler_params=pltpu.CompilerParams(
            collective_id=0, has_side_effects=True, vmem_limit_bytes=4 << 20
        ),
    )(e)


def pair_kernel(
    slot_ref, neg_ref, bank_ref, d_ref, g_ref, dp_ref, sp_ref, list_ref, open_ref, gt_v
):
    stops, cap = slot_ref.shape[2:]
    neg = neg_ref.shape[2]
    sub = sp_ref.shape[0] // stops
    per = dp_ref.shape[0] // stops
    dump = list_ref.shape[0] - 1
    b = lax.axis_index("blk")

    def preset(i, carry):
        list_ref[i] = 0
        return carry

    lax.fori_loop(0, list_ref.shape[0], preset, 0, unroll=16)

    def add_slot(pairs, src, code, live):
        held = open_ref[src]
        fresh = held < 0
        at = jnp.where(fresh, 2 * pairs, held)
        list_ref[jnp.where(live, at, dump)] = code
        open_ref[src] = jnp.where(live, jnp.where(fresh, 2 * pairs + 1, -1), held)
        return pairs + jnp.where(live & fresh, 1, 0)

    def add_stop(stop, pairs):
        group = lax.rem(b - stop + stops, stops) * sub
        for q in range(sub):
            open_ref[q] = -1
            tile = stop * sub + q
            gt_v[tile] = g_ref[pl.ds(pl.multiple_of(tile * T, T), T), :].T
            sp_ref[tile] = jnp.zeros(sp_ref.shape[1:], sp_ref.dtype)
        for q in range(per):
            dp_ref[stop * per + q] = jnp.zeros(dp_ref.shape[1:], dp_ref.dtype)

        for ref, slots in ((neg_ref, neg), (slot_ref, cap)):
            for k in range(slots):
                value = ref[0, 0, k, stop] if ref is neg_ref else ref[0, 0, stop, k]
                src = value & (2**SOURCE_BITS - 1)
                code = (value >> SOURCE_BITS) | ((group + src) << G_AT)
                pairs = add_slot(pairs, src, code, (value & (LIVE << SOURCE_BITS)) != 0)
        return pairs

    pairs = lax.fori_loop(0, stops, add_stop, 0)
    one_bit = jnp.left_shift(1, lax.broadcasted_iota(jnp.int32, (32, T), 0))

    def mask_less_half(index, keep):
        words = bank_ref[index] & keep
        return jnp.concatenate(
            [
                jnp.where((jnp.broadcast_to(words[k : k + 1, :], (32, T)) & one_bit) != 0, 0.5, -0.5)
                for k in range(words.shape[0])
            ],
            axis=0,
        )

    def first(i):
        codes = [list_ref[2 * i], list_ref[2 * i + 1]]
        g = codes[0] >> G_AT
        p = [code & (2**DEST_BITS - 1) for code in codes]
        ids = [(code >> DEST_BITS) & (2**BANK_BITS - 1) for code in codes]
        keep = [((code >> (DEST_BITS + BANK_BITS + 1)) & 1) - 1 for code in codes]
        live = [((code >> (DEST_BITS + BANK_BITS)) & 1).astype(jnp.float32) for code in codes]
        zq = g_ref[pl.ds(pl.multiple_of(g * T, T), T), :]
        zp = jnp.concatenate([d_ref[pl.ds(pl.multiple_of(k * T, T), T), :] for k in p], axis=0)
        s = lax.dot_general(zq, zp, (((1,), (1,)), ((), ())), preferred_element_type=jnp.float32)
        half = 0.5 * jnp.tanh(0.5 * s)
        r = jnp.concatenate(
            [live[u] * (mask_less_half(ids[u], keep[u]) - half[:, u * T : (u + 1) * T]) for u in range(2)], axis=1
        ).astype(jnp.bfloat16)
        return g, p, zp, r

    def second(g, p, zp, r):
        to_source = jnp.dot(r, zp, preferred_element_type=jnp.float32)
        to_dest = jnp.dot(gt_v[g], r, preferred_element_type=jnp.float32)
        sp_ref[g] += to_source
        dp_ref[p[0]] += to_dest[:, :T]
        dp_ref[p[1]] += to_dest[:, T:]

    def body(step, carry):
        for held in [first(step * UNROLL + u) for u in range(UNROLL)]:
            second(*held)
        return carry

    lax.fori_loop(0, (pairs + UNROLL - 1) // UNROLL, body, 0)


def pair_sums(slots, negatives, bank, d, g):
    nd, ng = d.shape[0] // T, g.shape[0] // T
    width = d.shape[1]
    stops, cap = slots.shape[2:]
    sub = ng // stops
    most = stops * ((cap + negatives.shape[2] + sub) // 2) + UNROLL
    most += (-most) % 8 + 8
    smem = pl.BlockSpec(memory_space=pltpu.SMEM)
    vmem = pl.BlockSpec(memory_space=pltpu.VMEM)
    return pl.pallas_call(
        pair_kernel,
        out_shape=(
            jax.ShapeDtypeStruct((nd, width, T), jnp.float32),
            jax.ShapeDtypeStruct((ng, T, width), jnp.float32),
        ),
        in_specs=[smem] * 2 + [vmem] * 3,
        out_specs=(vmem, vmem),
        scratch_shapes=[
            pltpu.SMEM((2 * most,), jnp.int32),
            pltpu.SMEM((sub,), jnp.int32),
            pltpu.VMEM((ng, width, T), jnp.bfloat16),
        ],
        compiler_params=pltpu.CompilerParams(vmem_limit_bytes=PAIR_VMEM << 20),
    )(slots, negatives, bank, d, g)


def code16(value_at, blocks, dst, amax):
    height = (dst.shape[0] - 16) // blocks
    power = jnp.ceil(jnp.log2(jnp.maximum(amax, 1e-37)))
    gain = jnp.exp2(-power) * 32767.0

    def one(i, carry):
        q = jnp.clip(jnp.round(value_at(i) * gain), -32767.0, 32767.0)
        dst[pl.ds(pl.multiple_of(i * height, height), height), :] = q.astype(jnp.int32).astype(jnp.int16)
        return carry

    lax.fori_loop(0, blocks, one, 0)
    dst[pl.ds(blocks * height, 16), :] = jnp.broadcast_to(power, (16, power.shape[1])).astype(jnp.int32).astype(jnp.int16)


def reduce_kernel(
    scale, dp_ref, sp_ref, out_ref, dest, core, s_send, s_recv, d_send, d_recv, send, recv
):
    sub = core.shape[1]
    width = core.shape[3]
    per = sub // CHUNKS
    z, xh, c, xl, y = place()
    to = peers()
    copies = {}

    def push(name, src, dst, peer):
        k = len(copies)
        copies[name] = pltpu.make_async_remote_copy(
            src_ref=src,
            dst_ref=dst,
            send_sem=send.at[k],
            recv_sem=recv.at[k],
            device_id=to[peer],
            device_id_type=MESH,
        )
        copies[name].start()

    def got(name):
        copies[name].wait_recv()

    order = [(2, 0), (2, 1), (1, 1), (3, 0), (1, 0), (3, 1), (0, 0), (0, 1)]

    def s_at(n, core_at):
        dz, xx = order[n]
        return sp_ref.at[pl.ds(blk_of(z + dz, xx, core_at) * sub, sub)]

    def mine(n, h):
        dy, xx = order[n]
        return plain(dp_ref.at[pl.ds(fiber_of(xx, y + dy) * sub, sub)], h)

    meet(to)
    for n in range(8):
        push(f"c{n}", s_at(n, 1 - c), core.at[n], "sib")

    def decoded(ref, h, height):
        gain = jnp.exp2(ref[h, pl.ds(per * height, 16), :].astype(jnp.float32)[:1]) * (1.0 / 32767.0)

        def at(i):
            rows = pl.ds(pl.multiple_of(i * height, height), height)
            return ref[h, rows, :].astype(jnp.float32) * gain

        return at

    def plain(ref, h):
        return lambda i: ref[h * per + i]

    def total(parts, keep, h):
        def one(i, most):
            value = parts[0](i)
            for part in parts[1:]:
                value = value + part(i)
            keep[h * per + i] = value
            return jnp.maximum(most, jnp.max(jnp.abs(value), axis=0, keepdims=True))

        return lax.fori_loop(0, per, one, jnp.zeros((1, keep.shape[2]), jnp.float32))

    def hand_on(name, parts, keep, h, out_buf, in_buf, peer):
        amax = total(parts, keep, h)
        code16(plain(keep, h), per, out_buf.at[h], amax)
        push(name + str(h), out_buf.at[h], in_buf.at[h], peer)

    def z_send(k, h, peer, *parts):
        hand_on(f"z{k}", parts, core.at[k], h, s_send.at[k], s_recv.at[k], peer)

    def y_send(k, h, peer, *parts):
        hand_on(f"y{k}", parts, dest.at[k], h, d_send.at[k], d_recv.at[k], peer)

    def s_in(name, k, h):
        got(name + str(h))
        return decoded(s_recv.at[k], h, T)

    def d_in(name, k, h):
        got(name + str(h))
        return decoded(d_recv.at[k], h, width)

    def cores(n, h):
        return plain(core.at[n], h), plain(s_at(n, c), h)

    y_send(0, 0, "y+", mine(0, 0))
    y_send(1, 0, "y-", mine(1, 0))
    got("c0")
    z_send(0, 0, "z+", *cores(0, 0))
    got("c1")
    z_send(1, 0, "z-", *cores(1, 0))
    for h in range(1, CHUNKS):
        y_send(0, h, "y+", mine(0, h))
        y_send(1, h, "y-", mine(1, h))
        z_send(0, h, "z+", *cores(0, h))
        z_send(1, h, "z-", *cores(1, h))
    for n in range(2, 8):
        got(f"c{n}")
    for h in range(CHUNKS):
        y_send(2, h, "y+", mine(2, h))
        y_send(3, h, "y-", mine(3, h))
        z_send(2, h, "z+", *cores(2, h))
        z_send(3, h, "z-", *cores(3, h))
        y_send(4, h, "y+", mine(4, h), d_in("y0", 0, h))
        y_send(5, h, "y-", mine(5, h), d_in("y1", 1, h))
        z_send(4, h, "z+", *cores(4, h), s_in("z0", 0, h))
        z_send(5, h, "z-", *cores(5, h), s_in("z1", 1, h))
    for h in range(CHUNKS):
        most_d = [
            total((mine(6, h), d_in("y3", 3, h), d_in("y4", 4, h)), dest.at[6], h),
            total((mine(7, h), d_in("y2", 2, h), d_in("y5", 5, h)), dest.at[7], h),
        ]
        code16(plain(dest.at[7 - xl], h), per, d_send.at[6, h], jnp.where(xl == 0, most_d[1], most_d[0]))
        push(f"xl{h}", d_send.at[6, h], d_recv.at[6, h], "xl")
        most_s = [
            total((*cores(6, h), s_in("z3", 3, h), s_in("z4", 4, h)), core.at[6], h),
            total((*cores(7, h), s_in("z2", 2, h), s_in("z5", 5, h)), core.at[7], h),
        ]
        code16(plain(core.at[7 - xh], h), per, s_send.at[6, h], jnp.where(xh == 0, most_s[1], most_s[0]))
        push(f"xh{h}", s_send.at[6, h], s_recv.at[6, h], "xh")
    for h in range(CHUNKS):
        from_xl = d_in("xl", 6, h)
        from_xh = s_in("xh", 6, h)

        def finish(i, carry):
            by_dest = dest[6 + xl, h * per + i] + from_xl(i)
            by_source = core[6 + xh, h * per + i] + from_xh(i)
            rows = pl.ds(pl.multiple_of((h * per + i) * T, T), T)
            out_ref[rows, :] = (by_source + by_dest.T) * scale
            return carry

        lax.fori_loop(0, per, finish, 0)
    for copy in copies.values():
        copy.wait_send()


def reduce_sums(dp, sp, rows, scale):
    width = sp.shape[2]
    sub = rows // T
    per = sub // CHUNKS
    return pl.pallas_call(
        functools.partial(reduce_kernel, scale),
        out_shape=jax.ShapeDtypeStruct((rows, width), jnp.float32),
        in_specs=[pl.BlockSpec(memory_space=pltpu.VMEM)] * 2,
        out_specs=pl.BlockSpec(memory_space=pltpu.VMEM),
        scratch_shapes=[
            pltpu.VMEM((8, sub, width, T), jnp.float32),
            pltpu.VMEM((8, sub, T, width), jnp.float32),
            pltpu.VMEM((7, CHUNKS, per * T + 16, width), jnp.int16),
            pltpu.VMEM((7, CHUNKS, per * T + 16, width), jnp.int16),
            pltpu.VMEM((7, CHUNKS, per * width + 16, T), jnp.int16),
            pltpu.VMEM((7, CHUNKS, per * width + 16, T), jnp.int16),
            pltpu.SemaphoreType.DMA((8 + 14 * CHUNKS,)),
            pltpu.SemaphoreType.DMA((8 + 14 * CHUNKS,)),
        ],
        compiler_params=pltpu.CompilerParams(
            collective_id=1, has_side_effects=True, vmem_limit_bytes=REDUCE_VMEM << 20
        ),
    )(dp, sp)


def on_device(
    embedding, tile_dest, tile_source, tile_count, pattern_id, pattern_bank, negative_dest, negative_source
):
    rows = embedding.shape[0]
    d, g = gather(embedding)
    live = jnp.arange(tile_dest.shape[3], dtype=jnp.int32) < tile_count[..., None]
    slots = ((pattern_id << DEST_BITS | tile_dest | jnp.where(live, LIVE, 0)) << SOURCE_BITS) | tile_source
    negatives = ((negative_dest | LIVE | NEGATIVE) << SOURCE_BITS) | negative_source
    dp, sp = pair_sums(slots, negatives.swapaxes(2, 3), pattern_bank, d, g)
    scale = 1.0 / math.sqrt(T * tile_dest.shape[2])
    return reduce_sums(dp, sp, rows, scale)


def solution(mesh):
    in_specs = (
        P(("blk", "fiber"), None),
        P("blk", "fiber", None, None),
        P("blk", "fiber", None, None),
        P("blk", "fiber", None),
        P("blk", "fiber", None, None),
        P(),
        P("blk", "fiber", None, None),
        P("blk", "fiber", None, None),
    )
    out_specs = P(("blk", "fiber"), None)
    return jax.shard_map(
        on_device, mesh=mesh, in_specs=in_specs, out_specs=out_specs, check_vma=False
    )
```

```python
import functools
import math

import jax
import jax.numpy as jnp
from jax import lax
from jax.experimental import pallas as pl
from jax.experimental.pallas import tpu as pltpu
from jax.sharding import PartitionSpec as P

ZS, XS, YS = 4, 2, 4
T = 128
MESH = pl.DeviceIdType.MESH
UNROLL = 6
CHUNKS = 4
PARTS = 4
GATHER_VMEM, PAIR_VMEM, REDUCE_VMEM = 14, 28, 36
SOURCE_BITS, DEST_BITS, BANK_BITS = 3, 6, 7
LIVE = 1 << (DEST_BITS + BANK_BITS)
NEGATIVE = LIVE << 1
G_AT = DEST_BITS + BANK_BITS + 2


def place():
    b, f = lax.axis_index("blk"), lax.axis_index("fiber")
    return b // 4, (b // 2) % 2, b % 2, f // YS, f % YS


def blk_of(z, xh, c):
    return ((z % ZS) * XS + xh) * 2 + c


def fiber_of(xl, y):
    return xl * YS + y % YS


def peers():
    z, xh, c, xl, y = place()
    b, f = blk_of(z, xh, c), fiber_of(xl, y)
    return {
        "sib": (blk_of(z, xh, 1 - c), f),
        "xh": (blk_of(z, 1 - xh, c), f),
        "z+": (blk_of(z + 1, xh, c), f),
        "z-": (blk_of(z + 3, xh, c), f),
        "xl": (b, fiber_of(1 - xl, y)),
        "y+": (b, fiber_of(xl, y + 1)),
        "y-": (b, fiber_of(xl, y + 3)),
    }


def meet(to):
    barrier = pltpu.get_barrier_semaphore()
    for device in to.values():
        pl.semaphore_signal(barrier, inc=1, device_id=device, device_id_type=MESH)
    pl.semaphore_wait(barrier, len(to))


def pair_words(words, block, stops, sub, room):
    slots, lanes = words.shape
    f32, bf16 = jnp.float32, jnp.bfloat16
    lane = lax.broadcasted_iota(jnp.int32, words.shape, 1)
    src = words & (2**SOURCE_BITS - 1)
    live = (words & (LIVE << SOURCE_BITS)) != 0
    picks = [jnp.where(live & (src == q), 1.0, 0.0) for q in range(sub)]

    def earlier(n, axis):
        shape = (n, n)
        return jnp.where(
            lax.broadcasted_iota(jnp.int32, shape, 1 - axis) < lax.broadcasted_iota(jnp.int32, shape, axis), 1.0, 0.0
        ).astype(bf16)

    before = earlier(slots, 0)
    ranks = [jnp.dot(before, pick.astype(bf16), preferred_element_type=f32) for pick in picks]
    held = [(jnp.sum(pick, axis=0, keepdims=True).astype(jnp.int32) + 1 >> 1).astype(f32) for pick in picks]
    in_stop = functools.reduce(lambda a, b: a + b, held)
    start = jnp.dot(
        jnp.broadcast_to(in_stop, (8, lanes)).astype(bf16), earlier(lanes, 1), preferred_element_type=f32
    )[:1]
    at = jnp.full(words.shape, -1.0, f32)
    for q in range(sub):
        at = jnp.where(picks[q] > 0.0, 2.0 * start + ranks[q], at)
        start = start + held[q]
    origin = block - lane
    origin = jnp.where(origin < 0, origin + stops, origin)
    code = (words >> SOURCE_BITS) | ((origin * sub + src) << G_AT)
    code = jnp.where(live, code, 0)

    def turned(values):
        tall = jnp.concatenate([values, jnp.zeros((lanes - slots, lanes), f32)], axis=0)
        return tall.T

    bytes_of = [turned(((code >> shift) & 255).astype(f32)) for shift in (0, 8, 16)]
    row = lax.broadcasted_iota(jnp.int32, (8, lanes), 0)
    spots = lax.broadcasted_iota(jnp.int32, (slots, room), 1).astype(f32)
    placed = jnp.zeros((8, room), f32)
    for stop in range(stops):
        parts = jnp.zeros((8, lanes), f32)
        for k in range(3):
            parts = jnp.where(row == k, jnp.broadcast_to(bytes_of[k][stop : stop + 1], (8, lanes)), parts)
        hit = jnp.where(jnp.broadcast_to(at[:, stop : stop + 1], spots.shape) == spots, 1.0, 0.0)
        placed = placed + jnp.dot(
            parts[:, :slots].astype(bf16), hit.astype(bf16), preferred_element_type=f32
        )
    placed = placed.astype(jnp.int32)
    listed = placed[0:1] | (placed[1:2] << 8) | (placed[2:3] << 16)
    total = jnp.sum(jnp.where(lane[:1] < stops, in_stop, 0.0), axis=1, keepdims=True).astype(jnp.int32)
    return jnp.where(lax.broadcasted_iota(jnp.int32, (1, room), 1) == room - 1, total, listed)


def gather_kernel(e_ref, slot_ref, neg_ref, d_ref, g_ref, gt_ref, list_ref, words, send, recv, local):
    rows = e_ref.shape[0]
    part = rows // PARTS
    z, xh, c, xl, y = place()
    to = peers()
    copies = {}

    def push(name, src, dst, peer):
        k = len(copies)
        copies[name] = pltpu.make_async_remote_copy(
            src_ref=src,
            dst_ref=dst,
            send_sem=send.at[k],
            recv_sem=recv.at[k],
            device_id=to[peer],
            device_id_type=MESH,
        )
        copies[name].start()

    def got(name, h):
        copies[name, h].wait_recv()

    def e_at(h):
        return e_ref.at[pl.ds(h * part, part)]

    def g_at(zz, xx, h):
        return g_ref.at[pl.ds(blk_of(zz, xx, c) * rows + h * part, part)]

    def d_at(xx, yy, h):
        return d_ref.at[pl.ds(fiber_of(xx, yy) * rows + h * part, part)]

    def pass_g(name, zz, xx, h, peer):
        push((name, h), g_at(zz, xx, h), g_at(zz, xx, h), peer)

    def pass_d(name, xx, yy, h, peer):
        push((name, h), d_at(xx, yy, h), d_at(xx, yy, h), peer)

    def turn(block, from_ref=None):
        def one(i, carry):
            at = pl.ds(pl.multiple_of((0 if from_ref is not None else block * rows) + i * T, T), T)
            gt_ref[block * (rows // T) + i] = (g_ref if from_ref is None else from_ref)[at, :].T
            return carry

        lax.fori_loop(0, rows // T, one, 0)

    shared = []

    def share(zz, xx, src=None):
        whole = g_ref.at[pl.ds(blk_of(zz, xx, c) * rows, rows)]
        push(("sib", len(copies)), whole if src is None else src, whole, "sib")
        shared.append((copies["sib", len(copies) - 1], blk_of(zz, xx, 1 - c)))
        turn(blk_of(zz, xx, c), src)

    keep_d = pltpu.make_async_copy(e_ref, d_ref.at[pl.ds(fiber_of(xl, y) * rows, rows)], local.at[0])
    keep_g = pltpu.make_async_copy(e_ref, g_ref.at[pl.ds(blk_of(z, xh, c) * rows, rows)], local.at[1])
    keep_d.start()
    keep_g.start()
    meet(to)
    for h in range(PARTS):
        push(("xh", h), e_at(h), g_at(z, xh, h), "xh")
        push(("xl", h), e_at(h), d_at(xl, y, h), "xl")
        push(("z+", h), e_at(h), g_at(z, xh, h), "z+")
        push(("y+", h), e_at(h), d_at(xl, y, h), "y+")
        push(("z-", h), e_at(h), g_at(z, xh, h), "z-")
        push(("y-", h), e_at(h), d_at(xl, y, h), "y-")

    share(z, xh, e_ref)
    stops, cap = slot_ref.shape[2:]
    neg = neg_ref.shape[2]
    words[...] = jnp.zeros_like(words)
    words[0:stops, 0:cap] = slot_ref[0, 0]
    by_slot = words[...].T
    words[...] = jnp.zeros_like(words)
    words[0:cap, :] = by_slot[0:cap]
    words[cap : cap + neg, 0:stops] = neg_ref[0, 0]
    list_ref[...] = pair_words(
        words[0 : cap + neg + 4, :], lax.axis_index("blk"), stops, gt_ref.shape[0] // stops, list_ref.shape[1]
    )

    def second_hop(h):
        got("xl-", h)
        pass_d("xl--", 1 - xl, y + 1, h, "y-")
        got("xh-", h)
        pass_g("xh--", z + 1, 1 - xh, h, "z-")

    for h in range(PARTS):
        got("z+", h)
        pass_g("z++", z + 3, xh, h, "z+")
        got("y+", h)
        pass_d("y++", xl, y + 3, h, "y+")
        got("xl", h)
        pass_d("xl-", 1 - xl, y, h, "y-")
        pass_d("xl+", 1 - xl, y, h, "y+")
        got("xh", h)
        pass_g("xh-", z, 1 - xh, h, "z-")
        pass_g("xh+", z, 1 - xh, h, "z+")
        if h:
            second_hop(h - 1)
    share(z + 3, xh)
    share(z, 1 - xh)
    second_hop(PARTS - 1)
    share(z + 1, 1 - xh)
    for name, zz, xx in (("z-", z + 1, xh), ("z++", z + 2, xh), ("xh+", z + 3, 1 - xh), ("xh--", z + 2, 1 - xh)):
        for h in range(PARTS):
            got(name, h)
        share(zz, xx)
    for h in range(PARTS):
        for name in ("y-", "xl+", "y++", "xl--"):
            got(name, h)
    for copy, block in shared:
        copy.wait_recv()
        turn(block)
    for copy in copies.values():
        copy.wait_send()
    keep_d.wait()
    keep_g.wait()


def gather(e, slots, negatives):
    rows, width = e.shape
    copies = 14 * PARTS + 8
    stops, cap = slots.shape[2:]
    total = ZS * XS * 2 * rows
    room = stops * (cap + negatives.shape[2] + total // T // stops) + 2 * UNROLL + 1
    room += (-room) % T
    vmem, anywhere = pl.BlockSpec(memory_space=pltpu.VMEM), pl.BlockSpec(memory_space=pl.ANY)
    return pl.pallas_call(
        gather_kernel,
        out_shape=(
            jax.ShapeDtypeStruct((XS * YS * rows, width), e.dtype),
            jax.ShapeDtypeStruct((total, width), e.dtype),
            jax.ShapeDtypeStruct((total // T, width, T), e.dtype),
            jax.ShapeDtypeStruct((1, room), jnp.int32),
        ),
        in_specs=[vmem, vmem, vmem],
        out_specs=(anywhere, vmem, vmem, vmem),
        scratch_shapes=[
            pltpu.VMEM((T, T), jnp.int32),
            pltpu.SemaphoreType.DMA((copies,)),
            pltpu.SemaphoreType.DMA((copies,)),
            pltpu.SemaphoreType.DMA((2,)),
        ],
        compiler_params=pltpu.CompilerParams(
            collective_id=0, has_side_effects=True, vmem_limit_bytes=GATHER_VMEM << 20
        ),
    )(e, slots, negatives)


def pair_kernel(list_ref, bank_ref, d_ref, g_ref, gt_ref, dp_ref, sp_ref):
    def clear(i, carry):
        dp_ref[i] = jnp.zeros(dp_ref.shape[1:], dp_ref.dtype)
        for k in range(sp_ref.shape[0] // dp_ref.shape[0]):
            sp_ref[i * (sp_ref.shape[0] // dp_ref.shape[0]) + k] = jnp.zeros(sp_ref.shape[1:], sp_ref.dtype)
        return carry

    lax.fori_loop(0, dp_ref.shape[0], clear, 0)
    pairs = list_ref[0, list_ref.shape[1] - 1]
    one_bit = jnp.left_shift(1, lax.broadcasted_iota(jnp.int32, (32, T), 0))

    def mask_less_half(index, keep):
        words = bank_ref[index] & keep
        return jnp.concatenate(
            [
                jnp.where((jnp.broadcast_to(words[k : k + 1, :], (32, T)) & one_bit) != 0, 0.5, -0.5)
                for k in range(words.shape[0])
            ],
            axis=0,
        )

    def first(i):
        codes = [list_ref[0, 2 * i], list_ref[0, 2 * i + 1]]
        g = codes[0] >> G_AT
        p = [code & (2**DEST_BITS - 1) for code in codes]
        ids = [(code >> DEST_BITS) & (2**BANK_BITS - 1) for code in codes]
        keep = [((code >> (DEST_BITS + BANK_BITS + 1)) & 1) - 1 for code in codes]
        live = [((code >> (DEST_BITS + BANK_BITS)) & 1).astype(jnp.float32) for code in codes]
        zq = g_ref[pl.ds(pl.multiple_of(g * T, T), T), :]
        zp = jnp.concatenate([d_ref[pl.ds(pl.multiple_of(k * T, T), T), :] for k in p], axis=0)
        s = lax.dot_general(zq, zp, (((1,), (1,)), ((), ())), preferred_element_type=jnp.float32)
        half = 0.5 * jnp.tanh(0.5 * s)
        r = jnp.concatenate(
            [live[u] * (mask_less_half(ids[u], keep[u]) - half[:, u * T : (u + 1) * T]) for u in range(2)], axis=1
        ).astype(jnp.bfloat16)
        return g, p, zp, r

    def second(g, p, zp, r):
        to_source = jnp.dot(r, zp, preferred_element_type=jnp.float32)
        to_dest = jnp.dot(gt_ref[g], r, preferred_element_type=jnp.float32)
        sp_ref[g] += to_source
        dp_ref[p[0]] += to_dest[:, :T]
        dp_ref[p[1]] += to_dest[:, T:]

    def body(step, carry):
        for held in [first(step * UNROLL + u) for u in range(UNROLL)]:
            second(*held)
        return carry

    lax.fori_loop(0, (pairs + UNROLL - 1) // UNROLL, body, 0)


def pair_sums(words, bank, d, g, gt):
    width = d.shape[1]
    smem = pl.BlockSpec(memory_space=pltpu.SMEM)
    vmem = pl.BlockSpec(memory_space=pltpu.VMEM)
    return pl.pallas_call(
        pair_kernel,
        out_shape=(
            jax.ShapeDtypeStruct((d.shape[0] // T, width, T), jnp.float32),
            jax.ShapeDtypeStruct((g.shape[0] // T, T, width), jnp.float32),
        ),
        in_specs=[smem] + [vmem] * 4,
        out_specs=(vmem, vmem),
        compiler_params=pltpu.CompilerParams(vmem_limit_bytes=PAIR_VMEM << 20),
    )(words, bank, d, g, gt)


def code16(value_at, blocks, dst, amax):
    height = (dst.shape[0] - 16) // blocks
    power = jnp.ceil(jnp.log2(jnp.maximum(amax, 1e-37)))
    gain = jnp.exp2(-power) * 32767.0

    def one(i, carry):
        q = jnp.clip(jnp.round(value_at(i) * gain), -32767.0, 32767.0)
        dst[pl.ds(pl.multiple_of(i * height, height), height), :] = q.astype(jnp.int32).astype(jnp.int16)
        return carry

    lax.fori_loop(0, blocks, one, 0)
    dst[pl.ds(blocks * height, 16), :] = jnp.broadcast_to(power, (16, power.shape[1])).astype(jnp.int32).astype(jnp.int16)


def reduce_kernel(
    scale, dp_ref, sp_ref, out_ref, dest, core, s_send, s_recv, d_send, d_recv, send, recv
):
    sub = core.shape[1]
    width = core.shape[3]
    per = sub // CHUNKS
    z, xh, c, xl, y = place()
    to = peers()
    copies = {}

    def push(name, src, dst, peer):
        k = len(copies)
        copies[name] = pltpu.make_async_remote_copy(
            src_ref=src,
            dst_ref=dst,
            send_sem=send.at[k],
            recv_sem=recv.at[k],
            device_id=to[peer],
            device_id_type=MESH,
        )
        copies[name].start()

    def got(name):
        copies[name].wait_recv()

    order = [(2, 0), (2, 1), (1, 1), (3, 0), (1, 0), (3, 1), (0, 0), (0, 1)]

    def s_at(n, core_at):
        dz, xx = order[n]
        return sp_ref.at[pl.ds(blk_of(z + dz, xx, core_at) * sub, sub)]

    def mine(n, h):
        dy, xx = order[n]
        return plain(dp_ref.at[pl.ds(fiber_of(xx, y + dy) * sub, sub)], h)

    meet(to)
    for n in range(8):
        push(f"c{n}", s_at(n, 1 - c), core.at[n], "sib")

    def decoded(ref, h, height):
        gain = jnp.exp2(ref[h, pl.ds(per * height, 16), :].astype(jnp.float32)[:1]) * (1.0 / 32767.0)

        def at(i):
            rows = pl.ds(pl.multiple_of(i * height, height), height)
            return ref[h, rows, :].astype(jnp.float32) * gain

        return at

    def plain(ref, h):
        return lambda i: ref[h * per + i]

    def total(parts, keep, h):
        def one(i, most):
            value = parts[0](i)
            for part in parts[1:]:
                value = value + part(i)
            keep[h * per + i] = value
            return jnp.maximum(most, jnp.max(jnp.abs(value), axis=0, keepdims=True))

        return lax.fori_loop(0, per, one, jnp.zeros((1, keep.shape[2]), jnp.float32))

    def hand_on(name, parts, keep, h, out_buf, in_buf, peer):
        amax = total(parts, keep, h)
        code16(plain(keep, h), per, out_buf.at[h], amax)
        push(name + str(h), out_buf.at[h], in_buf.at[h], peer)

    def z_send(k, h, peer, *parts):
        hand_on(f"z{k}", parts, core.at[k], h, s_send.at[k], s_recv.at[k], peer)

    def y_send(k, h, peer, *parts):
        hand_on(f"y{k}", parts, dest.at[k], h, d_send.at[k], d_recv.at[k], peer)

    def s_in(name, k, h):
        got(name + str(h))
        return decoded(s_recv.at[k], h, T)

    def d_in(name, k, h):
        got(name + str(h))
        return decoded(d_recv.at[k], h, width)

    def cores(n, h):
        return plain(core.at[n], h), plain(s_at(n, c), h)

    y_send(0, 0, "y+", mine(0, 0))
    y_send(1, 0, "y-", mine(1, 0))
    got("c0")
    z_send(0, 0, "z+", *cores(0, 0))
    got("c1")
    z_send(1, 0, "z-", *cores(1, 0))
    for h in range(1, CHUNKS):
        y_send(0, h, "y+", mine(0, h))
        y_send(1, h, "y-", mine(1, h))
        z_send(0, h, "z+", *cores(0, h))
        z_send(1, h, "z-", *cores(1, h))
    for n in range(2, 8):
        got(f"c{n}")
    for h in range(CHUNKS):
        y_send(2, h, "y+", mine(2, h))
        y_send(3, h, "y-", mine(3, h))
        z_send(2, h, "z+", *cores(2, h))
        z_send(3, h, "z-", *cores(3, h))
        y_send(4, h, "y+", mine(4, h), d_in("y0", 0, h))
        y_send(5, h, "y-", mine(5, h), d_in("y1", 1, h))
        z_send(4, h, "z+", *cores(4, h), s_in("z0", 0, h))
        z_send(5, h, "z-", *cores(5, h), s_in("z1", 1, h))
    for h in range(CHUNKS):
        most_d = [
            total((mine(6, h), d_in("y3", 3, h), d_in("y4", 4, h)), dest.at[6], h),
            total((mine(7, h), d_in("y2", 2, h), d_in("y5", 5, h)), dest.at[7], h),
        ]
        code16(plain(dest.at[7 - xl], h), per, d_send.at[6, h], jnp.where(xl == 0, most_d[1], most_d[0]))
        push(f"xl{h}", d_send.at[6, h], d_recv.at[6, h], "xl")
        most_s = [
            total((*cores(6, h), s_in("z3", 3, h), s_in("z4", 4, h)), core.at[6], h),
            total((*cores(7, h), s_in("z2", 2, h), s_in("z5", 5, h)), core.at[7], h),
        ]
        code16(plain(core.at[7 - xh], h), per, s_send.at[6, h], jnp.where(xh == 0, most_s[1], most_s[0]))
        push(f"xh{h}", s_send.at[6, h], s_recv.at[6, h], "xh")
    for h in range(CHUNKS):
        from_xl = d_in("xl", 6, h)
        from_xh = s_in("xh", 6, h)

        def finish(i, carry):
            by_dest = dest[6 + xl, h * per + i] + from_xl(i)
            by_source = core[6 + xh, h * per + i] + from_xh(i)
            rows = pl.ds(pl.multiple_of((h * per + i) * T, T), T)
            out_ref[rows, :] = (by_source + by_dest.T) * scale
            return carry

        lax.fori_loop(0, per, finish, 0)
    for copy in copies.values():
        copy.wait_send()


def reduce_sums(dp, sp, rows, scale):
    width = sp.shape[2]
    sub = rows // T
    per = sub // CHUNKS
    return pl.pallas_call(
        functools.partial(reduce_kernel, scale),
        out_shape=jax.ShapeDtypeStruct((rows, width), jnp.float32),
        in_specs=[pl.BlockSpec(memory_space=pltpu.VMEM)] * 2,
        out_specs=pl.BlockSpec(memory_space=pltpu.VMEM),
        scratch_shapes=[
            pltpu.VMEM((8, sub, width, T), jnp.float32),
            pltpu.VMEM((8, sub, T, width), jnp.float32),
            pltpu.VMEM((7, CHUNKS, per * T + 16, width), jnp.int16),
            pltpu.VMEM((7, CHUNKS, per * T + 16, width), jnp.int16),
            pltpu.VMEM((7, CHUNKS, per * width + 16, T), jnp.int16),
            pltpu.VMEM((7, CHUNKS, per * width + 16, T), jnp.int16),
            pltpu.SemaphoreType.DMA((8 + 14 * CHUNKS,)),
            pltpu.SemaphoreType.DMA((8 + 14 * CHUNKS,)),
        ],
        compiler_params=pltpu.CompilerParams(
            collective_id=1, has_side_effects=True, vmem_limit_bytes=REDUCE_VMEM << 20
        ),
    )(dp, sp)


def on_device(
    embedding, tile_dest, tile_source, tile_count, pattern_id, pattern_bank, negative_dest, negative_source
):
    rows = embedding.shape[0]
    live = jnp.arange(tile_dest.shape[3], dtype=jnp.int32) < tile_count[..., None]
    slots = ((pattern_id << DEST_BITS | tile_dest | jnp.where(live, LIVE, 0)) << SOURCE_BITS) | tile_source
    negatives = ((negative_dest | LIVE | NEGATIVE) << SOURCE_BITS) | negative_source
    d, g, gt, words = gather(embedding, slots, negatives.swapaxes(2, 3))
    dp, sp = pair_sums(words, pattern_bank, d, g, gt)
    scale = 1.0 / math.sqrt(T * tile_dest.shape[2])
    return reduce_sums(dp, sp, rows, scale)


def solution(mesh):
    in_specs = (
        P(("blk", "fiber"), None),
        P("blk", "fiber", None, None),
        P("blk", "fiber", None, None),
        P("blk", "fiber", None),
        P("blk", "fiber", None, None),
        P(),
        P("blk", "fiber", None, None),
        P("blk", "fiber", None, None),
    )
    out_specs = P(("blk", "fiber"), None)
    return jax.shard_map(
        on_device, mesh=mesh, in_specs=in_specs, out_specs=out_specs, check_vma=False
    )
```

```python
import functools
import math

import jax
import jax.numpy as jnp
from jax import lax
from jax.experimental import pallas as pl
from jax.experimental.pallas import tpu as pltpu
from jax.sharding import PartitionSpec as P

ZS, XS, YS = 4, 2, 4
T = 128
MESH = pl.DeviceIdType.MESH
UNROLL = 6
PARTS = 4
GATHER_VMEM, PAIR_VMEM, REDUCE_VMEM = 14, 28, 36
SOURCE_BITS, DEST_BITS, BANK_BITS = 3, 6, 7
LIVE = 1 << (DEST_BITS + BANK_BITS)
NEGATIVE = LIVE << 1
G_AT = DEST_BITS + BANK_BITS + 2


def place():
    b, f = lax.axis_index("blk"), lax.axis_index("fiber")
    return b // 4, (b // 2) % 2, b % 2, f // YS, f % YS


def blk_of(z, xh, c):
    return ((z % ZS) * XS + xh) * 2 + c


def fiber_of(xl, y):
    return xl * YS + y % YS


def peers():
    z, xh, c, xl, y = place()
    b, f = blk_of(z, xh, c), fiber_of(xl, y)
    return {
        "sib": (blk_of(z, xh, 1 - c), f),
        "xh": (blk_of(z, 1 - xh, c), f),
        "z+": (blk_of(z + 1, xh, c), f),
        "z-": (blk_of(z + 3, xh, c), f),
        "xl": (b, fiber_of(1 - xl, y)),
        "y+": (b, fiber_of(xl, y + 1)),
        "y-": (b, fiber_of(xl, y + 3)),
    }


def meet(to):
    barrier = pltpu.get_barrier_semaphore()
    for device in to.values():
        pl.semaphore_signal(barrier, inc=1, device_id=device, device_id_type=MESH)
    pl.semaphore_wait(barrier, len(to))


def pair_words(words, block, stops, sub, room):
    slots, lanes = words.shape
    f32, bf16 = jnp.float32, jnp.bfloat16
    lane = lax.broadcasted_iota(jnp.int32, words.shape, 1)
    src = words & (2**SOURCE_BITS - 1)
    live = (words & (LIVE << SOURCE_BITS)) != 0
    picks = [jnp.where(live & (src == q), 1.0, 0.0) for q in range(sub)]

    def earlier(n, axis):
        shape = (n, n)
        return jnp.where(
            lax.broadcasted_iota(jnp.int32, shape, 1 - axis) < lax.broadcasted_iota(jnp.int32, shape, axis), 1.0, 0.0
        ).astype(bf16)

    before = earlier(slots, 0)
    ranks = [jnp.dot(before, pick.astype(bf16), preferred_element_type=f32) for pick in picks]
    held = [(jnp.sum(pick, axis=0, keepdims=True).astype(jnp.int32) + 1 >> 1).astype(f32) for pick in picks]
    in_stop = functools.reduce(lambda a, b: a + b, held)
    start = jnp.dot(
        jnp.broadcast_to(in_stop, (8, lanes)).astype(bf16), earlier(lanes, 1), preferred_element_type=f32
    )[:1]
    at = jnp.full(words.shape, -1.0, f32)
    for q in range(sub):
        at = jnp.where(picks[q] > 0.0, 2.0 * start + ranks[q], at)
        start = start + held[q]
    origin = block - lane
    origin = jnp.where(origin < 0, origin + stops, origin)
    code = (words >> SOURCE_BITS) | ((origin * sub + src) << G_AT)
    code = jnp.where(live, code, 0)

    def turned(values):
        tall = jnp.concatenate([values, jnp.zeros((lanes - slots, lanes), f32)], axis=0)
        return tall.T

    bytes_of = [turned(((code >> shift) & 255).astype(f32)) for shift in (0, 8, 16)]
    row = lax.broadcasted_iota(jnp.int32, (8, lanes), 0)
    spots = lax.broadcasted_iota(jnp.int32, (slots, room), 1).astype(f32)
    placed = jnp.zeros((8, room), f32)
    for stop in range(stops):
        parts = jnp.zeros((8, lanes), f32)
        for k in range(3):
            parts = jnp.where(row == k, jnp.broadcast_to(bytes_of[k][stop : stop + 1], (8, lanes)), parts)
        hit = jnp.where(jnp.broadcast_to(at[:, stop : stop + 1], spots.shape) == spots, 1.0, 0.0)
        placed = placed + jnp.dot(
            parts[:, :slots].astype(bf16), hit.astype(bf16), preferred_element_type=f32
        )
    placed = placed.astype(jnp.int32)
    listed = placed[0:1] | (placed[1:2] << 8) | (placed[2:3] << 16)
    total = jnp.sum(jnp.where(lane[:1] < stops, in_stop, 0.0), axis=1, keepdims=True).astype(jnp.int32)
    return jnp.where(lax.broadcasted_iota(jnp.int32, (1, room), 1) == room - 1, total, listed)


def gather_kernel(e_ref, slot_ref, neg_ref, d_ref, g_ref, gt_ref, list_ref, words, send, recv, local):
    rows = e_ref.shape[0]
    part = rows // PARTS
    z, xh, c, xl, y = place()
    to = peers()
    copies = {}

    def push(name, src, dst, peer):
        k = len(copies)
        copies[name] = pltpu.make_async_remote_copy(
            src_ref=src,
            dst_ref=dst,
            send_sem=send.at[k],
            recv_sem=recv.at[k],
            device_id=to[peer],
            device_id_type=MESH,
        )
        copies[name].start()

    def got(name, h):
        copies[name, h].wait_recv()

    def e_at(h):
        return e_ref.at[pl.ds(h * part, part)]

    def g_at(zz, xx, h):
        return g_ref.at[pl.ds(blk_of(zz, xx, c) * rows + h * part, part)]

    def d_at(xx, yy, h):
        return d_ref.at[pl.ds(fiber_of(xx, yy) * rows + h * part, part)]

    def pass_g(name, zz, xx, h, peer):
        push((name, h), g_at(zz, xx, h), g_at(zz, xx, h), peer)

    def pass_d(name, xx, yy, h, peer):
        push((name, h), d_at(xx, yy, h), d_at(xx, yy, h), peer)

    def turn(block, from_ref=None):
        def one(i, carry):
            at = pl.ds(pl.multiple_of((0 if from_ref is not None else block * rows) + i * T, T), T)
            gt_ref[block * (rows // T) + i] = (g_ref if from_ref is None else from_ref)[at, :].T
            return carry

        lax.fori_loop(0, rows // T, one, 0)

    shared = []

    def share(zz, xx, src=None):
        whole = g_ref.at[pl.ds(blk_of(zz, xx, c) * rows, rows)]
        push(("sib", len(copies)), whole if src is None else src, whole, "sib")
        shared.append((copies["sib", len(copies) - 1], blk_of(zz, xx, 1 - c)))
        turn(blk_of(zz, xx, c), src)

    keep_d = pltpu.make_async_copy(e_ref, d_ref.at[pl.ds(fiber_of(xl, y) * rows, rows)], local.at[0])
    keep_g = pltpu.make_async_copy(e_ref, g_ref.at[pl.ds(blk_of(z, xh, c) * rows, rows)], local.at[1])
    keep_d.start()
    keep_g.start()
    meet(to)
    for h in range(PARTS):
        push(("xh", h), e_at(h), g_at(z, xh, h), "xh")
        push(("xl", h), e_at(h), d_at(xl, y, h), "xl")
        push(("z+", h), e_at(h), g_at(z, xh, h), "z+")
        push(("y+", h), e_at(h), d_at(xl, y, h), "y+")
        push(("z-", h), e_at(h), g_at(z, xh, h), "z-")
        push(("y-", h), e_at(h), d_at(xl, y, h), "y-")

    share(z, xh, e_ref)
    stops, cap = slot_ref.shape[2:]
    neg = neg_ref.shape[2]
    words[...] = jnp.zeros_like(words)
    words[0:stops, 0:cap] = slot_ref[0, 0]
    by_slot = words[...].T
    words[...] = jnp.zeros_like(words)
    words[0:cap, :] = by_slot[0:cap]
    words[cap : cap + neg, 0:stops] = neg_ref[0, 0]
    list_ref[...] = pair_words(
        words[0 : cap + neg + 4, :], lax.axis_index("blk"), stops, gt_ref.shape[0] // stops, list_ref.shape[1]
    )

    def second_hop(h):
        got("xl-", h)
        pass_d("xl--", 1 - xl, y + 1, h, "y-")
        got("xh-", h)
        pass_g("xh--", z + 1, 1 - xh, h, "z-")

    for h in range(PARTS):
        got("z+", h)
        pass_g("z++", z + 3, xh, h, "z+")
        got("y+", h)
        pass_d("y++", xl, y + 3, h, "y+")
        got("xl", h)
        pass_d("xl-", 1 - xl, y, h, "y-")
        pass_d("xl+", 1 - xl, y, h, "y+")
        got("xh", h)
        pass_g("xh-", z, 1 - xh, h, "z-")
        pass_g("xh+", z, 1 - xh, h, "z+")
        if h:
            second_hop(h - 1)
    share(z + 3, xh)
    share(z, 1 - xh)
    second_hop(PARTS - 1)
    share(z + 1, 1 - xh)
    for name, zz, xx in (("z-", z + 1, xh), ("z++", z + 2, xh), ("xh+", z + 3, 1 - xh), ("xh--", z + 2, 1 - xh)):
        for h in range(PARTS):
            got(name, h)
        share(zz, xx)
    for h in range(PARTS):
        for name in ("y-", "xl+", "y++", "xl--"):
            got(name, h)
    for copy, block in shared:
        copy.wait_recv()
        turn(block)
    for copy in copies.values():
        copy.wait_send()
    keep_d.wait()
    keep_g.wait()


def gather(e, slots, negatives):
    rows, width = e.shape
    copies = 14 * PARTS + 8
    stops, cap = slots.shape[2:]
    total = ZS * XS * 2 * rows
    room = stops * (cap + negatives.shape[2] + total // T // stops) + 2 * UNROLL + 1
    room += (-room) % T
    vmem, anywhere = pl.BlockSpec(memory_space=pltpu.VMEM), pl.BlockSpec(memory_space=pl.ANY)
    return pl.pallas_call(
        gather_kernel,
        out_shape=(
            jax.ShapeDtypeStruct((XS * YS * rows, width), e.dtype),
            jax.ShapeDtypeStruct((total, width), e.dtype),
            jax.ShapeDtypeStruct((total // T, width, T), e.dtype),
            jax.ShapeDtypeStruct((1, room), jnp.int32),
        ),
        in_specs=[vmem, vmem, vmem],
        out_specs=(anywhere, vmem, vmem, vmem),
        scratch_shapes=[
            pltpu.VMEM((T, T), jnp.int32),
            pltpu.SemaphoreType.DMA((copies,)),
            pltpu.SemaphoreType.DMA((copies,)),
            pltpu.SemaphoreType.DMA((2,)),
        ],
        compiler_params=pltpu.CompilerParams(
            collective_id=0, has_side_effects=True, vmem_limit_bytes=GATHER_VMEM << 20
        ),
    )(e, slots, negatives)


def pair_kernel(list_ref, bank_ref, d_ref, g_ref, gt_ref, dp_ref, sp_ref):
    def clear(i, carry):
        dp_ref[i] = jnp.zeros(dp_ref.shape[1:], dp_ref.dtype)
        for k in range(sp_ref.shape[0] // dp_ref.shape[0]):
            sp_ref[i * (sp_ref.shape[0] // dp_ref.shape[0]) + k] = jnp.zeros(sp_ref.shape[1:], sp_ref.dtype)
        return carry

    lax.fori_loop(0, dp_ref.shape[0], clear, 0)
    pairs = list_ref[0, list_ref.shape[1] - 1]
    one_bit = jnp.left_shift(1, lax.broadcasted_iota(jnp.int32, (32, T), 0))

    def mask_less_half(index, keep):
        words = bank_ref[index] & keep
        return jnp.concatenate(
            [
                jnp.where((jnp.broadcast_to(words[k : k + 1, :], (32, T)) & one_bit) != 0, 0.5, -0.5)
                for k in range(words.shape[0])
            ],
            axis=0,
        )

    def first(i):
        codes = [list_ref[0, 2 * i], list_ref[0, 2 * i + 1]]
        g = codes[0] >> G_AT
        p = [code & (2**DEST_BITS - 1) for code in codes]
        ids = [(code >> DEST_BITS) & (2**BANK_BITS - 1) for code in codes]
        keep = [((code >> (DEST_BITS + BANK_BITS + 1)) & 1) - 1 for code in codes]
        live = [((code >> (DEST_BITS + BANK_BITS)) & 1).astype(jnp.float32) for code in codes]
        zq = g_ref[pl.ds(pl.multiple_of(g * T, T), T), :]
        zp = jnp.concatenate([d_ref[pl.ds(pl.multiple_of(k * T, T), T), :] for k in p], axis=0)
        s = lax.dot_general(zq, zp, (((1,), (1,)), ((), ())), preferred_element_type=jnp.float32)
        half = 0.5 * jnp.tanh(0.5 * s)
        r = jnp.concatenate(
            [live[u] * (mask_less_half(ids[u], keep[u]) - half[:, u * T : (u + 1) * T]) for u in range(2)], axis=1
        ).astype(jnp.bfloat16)
        return g, p, zp, r

    def second(g, p, zp, r):
        to_source = jnp.dot(r, zp, preferred_element_type=jnp.float32)
        to_dest = jnp.dot(gt_ref[g], r, preferred_element_type=jnp.float32)
        sp_ref[g] += to_source
        dp_ref[p[0]] += to_dest[:, :T]
        dp_ref[p[1]] += to_dest[:, T:]

    def body(step, carry):
        for held in [first(step * UNROLL + u) for u in range(UNROLL)]:
            second(*held)
        return carry

    lax.fori_loop(0, (pairs + UNROLL - 1) // UNROLL, body, 0)


def pair_sums(words, bank, d, g, gt):
    width = d.shape[1]
    smem = pl.BlockSpec(memory_space=pltpu.SMEM)
    vmem = pl.BlockSpec(memory_space=pltpu.VMEM)
    return pl.pallas_call(
        pair_kernel,
        out_shape=(
            jax.ShapeDtypeStruct((d.shape[0] // T, width, T), jnp.float32),
            jax.ShapeDtypeStruct((g.shape[0] // T, T, width), jnp.float32),
        ),
        in_specs=[smem] + [vmem] * 4,
        out_specs=(vmem, vmem),
        compiler_params=pltpu.CompilerParams(vmem_limit_bytes=PAIR_VMEM << 20),
    )(words, bank, d, g, gt)


LEVELS = 32760.0
HEAD = 16


def power_of(bound):
    return jnp.ceil(jnp.log2(jnp.maximum(bound, 1e-37)))


def reduce_kernel(scale, dp_ref, sp_ref, out_ref, core, s_send, s_recv, d_send, d_recv, send, recv):
    sub = core.shape[1]
    z, xh, c, xl, y = place()
    to = peers()
    copies = {}

    def push(name, src, dst, peer):
        k = len(copies)
        copies[name] = pltpu.make_async_remote_copy(
            src_ref=src,
            dst_ref=dst,
            send_sem=send.at[k],
            recv_sem=recv.at[k],
            device_id=to[peer],
            device_id_type=MESH,
        )
        copies[name].start()

    order = [(2, 0), (2, 1), (1, 1), (3, 0), (1, 0), (3, 1), (0, 0), (0, 1)]

    def s_at(n, core_at):
        dz, xx = order[n]
        return sp_ref.at[pl.ds(blk_of(z + dz, xx, core_at) * sub, sub)]

    def d_at(dy, xx):
        return dp_ref.at[pl.ds(fiber_of(xx, y + dy) * sub, sub)]

    def largest(ref):
        def one(i, most):
            return jnp.maximum(most, jnp.max(jnp.abs(ref[i]), axis=0, keepdims=True))

        return lax.fori_loop(0, sub, one, jnp.zeros((1, ref.shape[2]), jnp.float32))

    def sum_cores(n):
        copies[f"c{n}"].wait_recv()
        mine, total = s_at(n, c), core.at[n]

        def one(i, most):
            value = total[i] + mine[i]
            total[i] = value
            return jnp.maximum(most, jnp.max(jnp.abs(value), axis=0, keepdims=True))

        return lax.fori_loop(0, sub, one, jnp.zeros((1, core.shape[3]), jnp.float32))

    def span(h, height):
        return pl.ds(0, HEAD + height) if h == 0 else pl.ds(HEAD + h * height, height)

    def send_tile(name, h, value, power, out_buf, in_buf, peer):
        height = value.shape[0]
        q = jnp.round(value * (jnp.exp2(-power) * LEVELS))
        out_buf[pl.ds(HEAD + h * height, height), :] = q.astype(jnp.int32).astype(jnp.int16)
        if h == 0:
            out_buf[pl.ds(0, HEAD), :] = (
                jnp.broadcast_to(power, (HEAD, power.shape[1])).astype(jnp.int32).astype(jnp.int16)
            )
        push(f"{name}{h}", out_buf.at[span(h, height)], in_buf.at[span(h, height)], peer)

    def bound_in(buf):
        return jnp.exp2(buf[pl.ds(0, HEAD), :].astype(jnp.float32)[:1])

    def tile_in(buf, h, bound):
        height = (buf.shape[0] - HEAD) // sub
        return buf[pl.ds(HEAD + h * height, height), :].astype(jnp.float32) * (bound * (1.0 / LEVELS))

    def got(*names):
        for name in names:
            copies[name].wait_recv()

    def y_send(k, h, value, power):
        send_tile(f"y{k}_", h, value, power, d_send.at[k], d_recv.at[k], "y+" if k % 2 == 0 else "y-")

    def z_send(k, h, value, power):
        send_tile(f"z{k}_", h, value, power, s_send.at[k], s_recv.at[k], "z+" if k % 2 == 0 else "z-")

    meet(to)
    for n in range(8):
        push(f"c{n}", s_at(n, 1 - c), core.at[n], "sib")
    for k in (0, 1):
        part = d_at(*order[k])
        power = power_of(largest(part))
        for h in range(sub):
            y_send(k, h, part[h], power)
    for k in (0, 1):
        power = power_of(sum_cores(k))
        for h in range(sub):
            z_send(k, h, core[k, h], power)
    most_d = [largest(d_at(*order[k])) for k in (4, 5, 2, 3)]
    most_s = [sum_cores(k) for k in (4, 5, 2, 3)]
    own_d, own_s = [power_of(most) for most in most_d[2:]], [power_of(most) for most in most_s[2:]]
    on_d, on_s, from_d, from_s = [], [], [], []
    for h in range(sub):
        for k in (0, 1):
            got(f"y{k}_{h}")
            if h == 0:
                from_d.append(bound_in(d_recv.at[k]))
                on_d.append(power_of(most_d[k] + from_d[k]))
            y_send(4 + k, h, d_at(*order[4 + k])[h] + tile_in(d_recv.at[k], h, from_d[k]), on_d[k])
            y_send(2 + k, h, d_at(*order[2 + k])[h], own_d[k])
            got(f"z{k}_{h}")
            if h == 0:
                from_s.append(bound_in(s_recv.at[k]))
                on_s.append(power_of(most_s[k] + from_s[k]))
            z_send(4 + k, h, core[4 + k, h] + tile_in(s_recv.at[k], h, from_s[k]), on_s[k])
            z_send(2 + k, h, core[2 + k, h], own_s[k])
    most_6, most_7 = sum_cores(6), sum_cores(7)
    away_d, away_s = d_at(0, 1 - xl), core.at[7 - xh]
    most_away_d = largest(away_d)
    most_away_s = jnp.where(xh == 0, most_7, most_6)
    for h in range(sub):
        got(f"y2_{h}", f"y3_{h}", f"y4_{h}", f"y5_{h}")
        if h == 0:
            near_d, far_d = bound_in(d_recv.at[2 + xl]), bound_in(d_recv.at[5 - xl])
            power_d = power_of(most_away_d + near_d + far_d)
        value = away_d[h] + tile_in(d_recv.at[2 + xl], h, near_d) + tile_in(d_recv.at[5 - xl], h, far_d)
        send_tile("xl", h, value, power_d, d_send.at[6], d_recv.at[6], "xl")
        got(f"z2_{h}", f"z3_{h}", f"z4_{h}", f"z5_{h}")
        if h == 0:
            near_s, far_s = bound_in(s_recv.at[2 + xh]), bound_in(s_recv.at[5 - xh])
            power_s = power_of(most_away_s + near_s + far_s)
        value = away_s[h] + tile_in(s_recv.at[2 + xh], h, near_s) + tile_in(s_recv.at[5 - xh], h, far_s)
        send_tile("xh", h, value, power_s, s_send.at[6], s_recv.at[6], "xh")
    home_d, home_s = d_at(0, xl), core.at[6 + xh]
    bufs_d = [d_recv.at[3 - xl], d_recv.at[4 + xl], d_recv.at[6]]
    bufs_s = [s_recv.at[3 - xh], s_recv.at[4 + xh], s_recv.at[6]]
    for h in range(sub):
        rows = pl.ds(h * T, T)
        got(f"xl{h}")
        by_dest = home_d[h]
        for buf in bufs_d:
            by_dest = by_dest + tile_in(buf, h, bound_in(buf))
        got(f"xh{h}")
        by_source = home_s[h]
        for buf in bufs_s:
            by_source = by_source + tile_in(buf, h, bound_in(buf))
        out_ref[rows, :] = (by_source + by_dest.T) * scale
    for copy in copies.values():
        copy.wait_send()


def reduce_sums(dp, sp, rows, scale):
    width = sp.shape[2]
    sub = rows // T
    copies = 8 + 14 * sub
    return pl.pallas_call(
        functools.partial(reduce_kernel, scale),
        out_shape=jax.ShapeDtypeStruct((rows, width), jnp.float32),
        in_specs=[pl.BlockSpec(memory_space=pltpu.VMEM)] * 2,
        out_specs=pl.BlockSpec(memory_space=pltpu.VMEM),
        scratch_shapes=[
            pltpu.VMEM((8, sub, T, width), jnp.float32),
            pltpu.VMEM((7, HEAD + sub * T, width), jnp.int16),
            pltpu.VMEM((7, HEAD + sub * T, width), jnp.int16),
            pltpu.VMEM((7, HEAD + sub * width, T), jnp.int16),
            pltpu.VMEM((7, HEAD + sub * width, T), jnp.int16),
            pltpu.SemaphoreType.DMA((copies,)),
            pltpu.SemaphoreType.DMA((copies,)),
        ],
        compiler_params=pltpu.CompilerParams(
            collective_id=1, has_side_effects=True, vmem_limit_bytes=REDUCE_VMEM << 20
        ),
    )(dp, sp)


def on_device(
    embedding, tile_dest, tile_source, tile_count, pattern_id, pattern_bank, negative_dest, negative_source
):
    rows = embedding.shape[0]
    live = jnp.arange(tile_dest.shape[3], dtype=jnp.int32) < tile_count[..., None]
    slots = ((pattern_id << DEST_BITS | tile_dest | jnp.where(live, LIVE, 0)) << SOURCE_BITS) | tile_source
    negatives = ((negative_dest | LIVE | NEGATIVE) << SOURCE_BITS) | negative_source
    d, g, gt, words = gather(embedding, slots, negatives.swapaxes(2, 3))
    dp, sp = pair_sums(words, pattern_bank, d, g, gt)
    scale = 1.0 / math.sqrt(T * tile_dest.shape[2])
    return reduce_sums(dp, sp, rows, scale)


def solution(mesh):
    in_specs = (
        P(("blk", "fiber"), None),
        P("blk", "fiber", None, None),
        P("blk", "fiber", None, None),
        P("blk", "fiber", None),
        P("blk", "fiber", None, None),
        P(),
        P("blk", "fiber", None, None),
        P("blk", "fiber", None, None),
    )
    out_specs = P(("blk", "fiber"), None)
    return jax.shard_map(
        on_device, mesh=mesh, in_specs=in_specs, out_specs=out_specs, check_vma=False
    )
```

```python
import functools
import math

import jax
import jax.numpy as jnp
from jax import lax
from jax.experimental import pallas as pl
from jax.experimental.pallas import tpu as pltpu
from jax.sharding import PartitionSpec as P

ZS, XS, YS = 4, 2, 4
T = 128
MESH = pl.DeviceIdType.MESH
UNROLL = 8
PARTS = 4
GATHER_VMEM, PAIR_VMEM, REDUCE_VMEM = 14, 28, 36
SOURCE_BITS, DEST_BITS, BANK_BITS = 3, 6, 7
LIVE = 1 << (DEST_BITS + BANK_BITS)
NEGATIVE = LIVE << 1
G_AT = DEST_BITS + BANK_BITS + 2


def place():
    b, f = lax.axis_index("blk"), lax.axis_index("fiber")
    return b // 4, (b // 2) % 2, b % 2, f // YS, f % YS


def blk_of(z, xh, c):
    return ((z % ZS) * XS + xh) * 2 + c


def fiber_of(xl, y):
    return xl * YS + y % YS


def peers():
    z, xh, c, xl, y = place()
    b, f = blk_of(z, xh, c), fiber_of(xl, y)
    return {
        "sib": (blk_of(z, xh, 1 - c), f),
        "xh": (blk_of(z, 1 - xh, c), f),
        "z+": (blk_of(z + 1, xh, c), f),
        "z-": (blk_of(z + 3, xh, c), f),
        "xl": (b, fiber_of(1 - xl, y)),
        "y+": (b, fiber_of(xl, y + 1)),
        "y-": (b, fiber_of(xl, y + 3)),
    }


def meet(to):
    barrier = pltpu.get_barrier_semaphore()
    for device in to.values():
        pl.semaphore_signal(barrier, inc=1, device_id=device, device_id_type=MESH)
    pl.semaphore_wait(barrier, len(to))


def pair_words(words, block, stops, sub, room):
    slots, lanes = words.shape
    f32, bf16 = jnp.float32, jnp.bfloat16
    lane = lax.broadcasted_iota(jnp.int32, words.shape, 1)
    src = words & (2**SOURCE_BITS - 1)
    live = (words & (LIVE << SOURCE_BITS)) != 0
    picks = [jnp.where(live & (src == q), 1.0, 0.0) for q in range(sub)]

    def earlier(n, axis):
        shape = (n, n)
        return jnp.where(
            lax.broadcasted_iota(jnp.int32, shape, 1 - axis) < lax.broadcasted_iota(jnp.int32, shape, axis), 1.0, 0.0
        ).astype(bf16)

    before = earlier(slots, 0)
    ranks = [jnp.dot(before, pick.astype(bf16), preferred_element_type=f32) for pick in picks]
    held = [(jnp.sum(pick, axis=0, keepdims=True).astype(jnp.int32) + 1 >> 1).astype(f32) for pick in picks]
    in_stop = functools.reduce(lambda a, b: a + b, held)
    start = jnp.dot(
        jnp.broadcast_to(in_stop, (8, lanes)).astype(bf16), earlier(lanes, 1), preferred_element_type=f32
    )[:1]
    at = jnp.full(words.shape, -1.0, f32)
    for q in range(sub):
        at = jnp.where(picks[q] > 0.0, 2.0 * start + ranks[q], at)
        start = start + held[q]
    origin = block - lane
    origin = jnp.where(origin < 0, origin + stops, origin)
    code = (words >> SOURCE_BITS) | ((origin * sub + src) << G_AT)
    code = jnp.where(live, code, 0)

    def turned(values):
        tall = jnp.concatenate([values, jnp.zeros((lanes - slots, lanes), f32)], axis=0)
        return tall.T

    bytes_of = [turned(((code >> shift) & 255).astype(f32)) for shift in (0, 8, 16)]
    row = lax.broadcasted_iota(jnp.int32, (8, lanes), 0)
    spots = lax.broadcasted_iota(jnp.int32, (slots, room), 1).astype(f32)
    placed = jnp.zeros((8, room), f32)
    for stop in range(stops):
        parts = jnp.zeros((8, lanes), f32)
        for k in range(3):
            parts = jnp.where(row == k, jnp.broadcast_to(bytes_of[k][stop : stop + 1], (8, lanes)), parts)
        hit = jnp.where(jnp.broadcast_to(at[:, stop : stop + 1], spots.shape) == spots, 1.0, 0.0)
        placed = placed + jnp.dot(
            parts[:, :slots].astype(bf16), hit.astype(bf16), preferred_element_type=f32
        )
    placed = placed.astype(jnp.int32)
    listed = placed[0:1] | (placed[1:2] << 8) | (placed[2:3] << 16)
    total = jnp.sum(jnp.where(lane[:1] < stops, in_stop, 0.0), axis=1, keepdims=True).astype(jnp.int32)
    return jnp.where(lax.broadcasted_iota(jnp.int32, (1, room), 1) == room - 1, total, listed)


def gather_kernel(stops, e_ref, slot_ref, d_ref, g_ref, gt_ref, list_ref, words, send, recv, local):
    rows = e_ref.shape[0]
    part = rows // PARTS
    z, xh, c, xl, y = place()
    to = peers()
    copies = {}

    def push(name, src, dst, peer):
        k = len(copies)
        copies[name] = pltpu.make_async_remote_copy(
            src_ref=src,
            dst_ref=dst,
            send_sem=send.at[k],
            recv_sem=recv.at[k],
            device_id=to[peer],
            device_id_type=MESH,
        )
        copies[name].start()

    def got(name, h):
        copies[name, h].wait_recv()

    def e_at(h):
        return e_ref.at[pl.ds(h * part, part)]

    def g_at(zz, xx, h):
        return g_ref.at[pl.ds(blk_of(zz, xx, c) * rows + h * part, part)]

    def d_at(xx, yy, h):
        return d_ref.at[pl.ds(fiber_of(xx, yy) * rows + h * part, part)]

    def pass_g(name, zz, xx, h, peer):
        push((name, h), g_at(zz, xx, h), g_at(zz, xx, h), peer)

    def pass_d(name, xx, yy, h, peer):
        push((name, h), d_at(xx, yy, h), d_at(xx, yy, h), peer)

    def turn(block, from_ref=None):
        def one(i, carry):
            at = pl.ds(pl.multiple_of((0 if from_ref is not None else block * rows) + i * T, T), T)
            gt_ref[block * (rows // T) + i] = (g_ref if from_ref is None else from_ref)[at, :].T
            return carry

        lax.fori_loop(0, rows // T, one, 0)

    shared = []

    def absorb():
        copy, block = shared.pop(0)
        copy.wait_recv()
        turn(block)


    def share(zz, xx, src=None):
        whole = g_ref.at[pl.ds(blk_of(zz, xx, c) * rows, rows)]
        push(("sib", len(copies)), whole if src is None else src, whole, "sib")
        shared.append((copies["sib", len(copies) - 1], blk_of(zz, xx, 1 - c)))
        turn(blk_of(zz, xx, c), src)

    keep_d = pltpu.make_async_copy(e_ref, d_ref.at[pl.ds(fiber_of(xl, y) * rows, rows)], local.at[0])
    keep_g = pltpu.make_async_copy(e_ref, g_ref.at[pl.ds(blk_of(z, xh, c) * rows, rows)], local.at[1])
    keep_d.start()
    keep_g.start()
    meet(to)
    for h in range(PARTS):
        push(("xh", h), e_at(h), g_at(z, xh, h), "xh")
        push(("xl", h), e_at(h), d_at(xl, y, h), "xl")
        push(("z+", h), e_at(h), g_at(z, xh, h), "z+")
        push(("y+", h), e_at(h), d_at(xl, y, h), "y+")
        push(("z-", h), e_at(h), g_at(z, xh, h), "z-")
        push(("y-", h), e_at(h), d_at(xl, y, h), "y-")

    share(z, xh, e_ref)
    cap = slot_ref.shape[3]
    neg = slot_ref.shape[2] - stops
    words[...] = jnp.zeros_like(words)
    words[0:stops, 0:cap] = slot_ref[0, 0, 0:stops]
    by_slot = words[...].T
    words[...] = jnp.zeros_like(words)
    words[0:cap, :] = by_slot[0:cap]
    words[cap : cap + neg, 0:stops] = slot_ref[0, 0, stops : stops + neg, 0:stops]
    list_ref[...] = pair_words(
        words[0 : cap + neg + 4, :], lax.axis_index("blk"), stops, gt_ref.shape[0] // stops, list_ref.shape[1]
    )

    def second_hop(h):
        got("xl-", h)
        pass_d("xl--", 1 - xl, y + 1, h, "y-")
        got("xh-", h)
        pass_g("xh--", z + 1, 1 - xh, h, "z-")

    for h in range(PARTS):
        got("z+", h)
        pass_g("z++", z + 3, xh, h, "z+")
        got("y+", h)
        pass_d("y++", xl, y + 3, h, "y+")
        got("xl", h)
        pass_d("xl-", 1 - xl, y, h, "y-")
        pass_d("xl+", 1 - xl, y, h, "y+")
        got("xh", h)
        pass_g("xh-", z, 1 - xh, h, "z-")
        pass_g("xh+", z, 1 - xh, h, "z+")
        if h:
            second_hop(h - 1)
    share(z + 3, xh)
    share(z, 1 - xh)
    second_hop(PARTS - 1)
    share(z + 1, 1 - xh)
    absorb()
    for name, zz, xx in (("z-", z + 1, xh), ("z++", z + 2, xh), ("xh+", z + 3, 1 - xh), ("xh--", z + 2, 1 - xh)):
        for h in range(PARTS):
            got(name, h)
        share(zz, xx)
        absorb()
    for h in range(PARTS):
        for name in ("y-", "xl+", "y++", "xl--"):
            got(name, h)
    while shared:
        absorb()
    for copy in copies.values():
        copy.wait_send()
    keep_d.wait()
    keep_g.wait()


def gather(e, slots, stops):
    rows, width = e.shape
    copies = 14 * PARTS + 8
    cap, neg = slots.shape[3], slots.shape[2] - stops
    total = ZS * XS * 2 * rows
    room = stops * (cap + neg + total // T // stops) + 4 * UNROLL + 1
    room += (-room) % T
    vmem, anywhere = pl.BlockSpec(memory_space=pltpu.VMEM), pl.BlockSpec(memory_space=pl.ANY)
    return pl.pallas_call(
        functools.partial(gather_kernel, stops),
        out_shape=(
            jax.ShapeDtypeStruct((XS * YS * rows, width), e.dtype),
            jax.ShapeDtypeStruct((total, width), e.dtype),
            jax.ShapeDtypeStruct((total // T, width, T), e.dtype),
            jax.ShapeDtypeStruct((1, room), jnp.int32),
        ),
        in_specs=[vmem, vmem],
        out_specs=(anywhere, vmem, vmem, vmem),
        scratch_shapes=[
            pltpu.VMEM((T, T), jnp.int32),
            pltpu.SemaphoreType.DMA((copies,)),
            pltpu.SemaphoreType.DMA((copies,)),
            pltpu.SemaphoreType.DMA((2,)),
        ],
        compiler_params=pltpu.CompilerParams(
            collective_id=0, has_side_effects=True, vmem_limit_bytes=GATHER_VMEM << 20
        ),
    )(e, slots)


def pair_kernel(list_ref, bank_ref, d_ref, g_ref, gt_ref, dp_ref, sp_ref, coded):
    def clear(i, carry):
        dp_ref[i] = jnp.zeros(dp_ref.shape[1:], dp_ref.dtype)
        for k in range(sp_ref.shape[0] // dp_ref.shape[0]):
            sp_ref[i * (sp_ref.shape[0] // dp_ref.shape[0]) + k] = jnp.zeros(sp_ref.shape[1:], sp_ref.dtype)
        return carry

    lax.fori_loop(0, dp_ref.shape[0], clear, 0)
    pairs = list_ref[0, list_ref.shape[1] - 1]
    one_bit = jnp.left_shift(1, lax.broadcasted_iota(jnp.int32, (32, T), 0))

    def mask_less_half(index, keep):
        words = bank_ref[index] & keep
        return jnp.concatenate(
            [
                jnp.where((jnp.broadcast_to(words[k : k + 1, :], (32, T)) & one_bit) != 0, 0.5, -0.5)
                for k in range(words.shape[0])
            ],
            axis=0,
        )

    def tiles(i):
        codes = [list_ref[0, 2 * i], list_ref[0, 2 * i + 1]]
        p = [code & (2**DEST_BITS - 1) for code in codes]
        zp = jnp.concatenate([d_ref[pl.ds(pl.multiple_of(k * T, T), T), :] for k in p], axis=0)
        return codes[0] >> G_AT, p, zp

    def first(i):
        codes = [list_ref[0, 2 * i], list_ref[0, 2 * i + 1]]
        g, _, zp = tiles(i)
        ids = [(code >> DEST_BITS) & (2**BANK_BITS - 1) for code in codes]
        keep = [((code >> (DEST_BITS + BANK_BITS + 1)) & 1) - 1 for code in codes]
        live = [((code >> (DEST_BITS + BANK_BITS)) & 1).astype(jnp.float32) for code in codes]
        zq = g_ref[pl.ds(pl.multiple_of(g * T, T), T), :]
        s = lax.dot_general(zq, zp, (((1,), (1,)), ((), ())), preferred_element_type=jnp.float32)
        half = 0.5 * jnp.tanh(0.5 * s)
        r = jnp.concatenate(
            [live[u] * (mask_less_half(ids[u], keep[u]) - half[:, u * T : (u + 1) * T]) for u in range(2)], axis=1
        ).astype(jnp.bfloat16)
        return r

    def second(i, r):
        g, p, zp = tiles(i)
        to_source = jnp.dot(r, zp, preferred_element_type=jnp.float32)
        to_dest = jnp.dot(gt_ref[g], r, preferred_element_type=jnp.float32)
        sp_ref[g] += to_source
        dp_ref[p[0]] += to_dest[:, :T]
        dp_ref[p[1]] += to_dest[:, T:]

    for u in range(UNROLL):
        coded[0, u] = first(u)

    def body(step, carry):
        now = lax.rem(step, 2)
        later = []
        for u in range(UNROLL):
            later.append(first((step + 1) * UNROLL + u))
            second(step * UNROLL + u, coded[now, u])
        for u in range(UNROLL):
            coded[1 - now, u] = later[u]
        return carry

    lax.fori_loop(0, (pairs + UNROLL - 1) // UNROLL, body, 0)


def pair_sums(words, bank, d, g, gt):
    width = d.shape[1]
    smem = pl.BlockSpec(memory_space=pltpu.SMEM)
    vmem = pl.BlockSpec(memory_space=pltpu.VMEM)
    return pl.pallas_call(
        pair_kernel,
        out_shape=(
            jax.ShapeDtypeStruct((d.shape[0] // T, width, T), jnp.float32),
            jax.ShapeDtypeStruct((g.shape[0] // T, T, width), jnp.float32),
        ),
        in_specs=[smem] + [vmem] * 4,
        out_specs=(vmem, vmem),
        scratch_shapes=[pltpu.VMEM((2, UNROLL, T, 2 * T), d.dtype)],
        compiler_params=pltpu.CompilerParams(vmem_limit_bytes=PAIR_VMEM << 20),
    )(words, bank, d, g, gt)


LEVELS = 32760.0
HEAD = 16


def power_of(bound):
    return jnp.ceil(jnp.log2(jnp.maximum(bound, 1e-37)))


def reduce_kernel(scale, dp_ref, sp_ref, out_ref, core, s_send, s_recv, d_send, d_recv, send, recv):
    sub = core.shape[1]
    z, xh, c, xl, y = place()
    to = peers()
    copies = {}

    def push(name, src, dst, peer):
        k = len(copies)
        copies[name] = pltpu.make_async_remote_copy(
            src_ref=src,
            dst_ref=dst,
            send_sem=send.at[k],
            recv_sem=recv.at[k],
            device_id=to[peer],
            device_id_type=MESH,
        )
        copies[name].start()

    order = [(2, 0), (2, 1), (1, 1), (3, 0), (1, 0), (3, 1), (0, 0), (0, 1)]

    def s_at(n, core_at):
        dz, xx = order[n]
        return sp_ref.at[pl.ds(blk_of(z + dz, xx, core_at) * sub, sub)]

    def d_at(dy, xx):
        return dp_ref.at[pl.ds(fiber_of(xx, y + dy) * sub, sub)]

    def largest(ref):
        def one(i, most):
            return jnp.maximum(most, jnp.max(jnp.abs(ref[i]), axis=0, keepdims=True))

        return lax.fori_loop(0, sub, one, jnp.zeros((1, ref.shape[2]), jnp.float32))

    def sum_cores(n):
        copies[f"c{n}"].wait_recv()
        mine, total = s_at(n, c), core.at[n]

        def one(i, most):
            value = total[i] + mine[i]
            total[i] = value
            return jnp.maximum(most, jnp.max(jnp.abs(value), axis=0, keepdims=True))

        return lax.fori_loop(0, sub, one, jnp.zeros((1, core.shape[3]), jnp.float32))

    def span(h, height):
        return pl.ds(0, HEAD + height) if h == 0 else pl.ds(HEAD + h * height, height)

    def send_tile(name, h, value, power, out_buf, in_buf, peer):
        height = value.shape[0]
        q = jnp.round(value * (jnp.exp2(-power) * LEVELS))
        out_buf[pl.ds(HEAD + h * height, height), :] = q.astype(jnp.int32).astype(jnp.int16)
        if h == 0:
            out_buf[pl.ds(0, HEAD), :] = (
                jnp.broadcast_to(power, (HEAD, power.shape[1])).astype(jnp.int32).astype(jnp.int16)
            )
        push(f"{name}{h}", out_buf.at[span(h, height)], in_buf.at[span(h, height)], peer)

    def bound_in(buf):
        return jnp.exp2(buf[pl.ds(0, HEAD), :].astype(jnp.float32)[:1])

    def tile_in(buf, h, bound):
        height = (buf.shape[0] - HEAD) // sub
        return buf[pl.ds(HEAD + h * height, height), :].astype(jnp.float32) * (bound * (1.0 / LEVELS))

    def got(*names):
        for name in names:
            copies[name].wait_recv()

    def y_send(k, h, value, power):
        send_tile(f"y{k}_", h, value, power, d_send.at[k], d_recv.at[k], "y+" if k % 2 == 0 else "y-")

    def z_send(k, h, value, power):
        send_tile(f"z{k}_", h, value, power, s_send.at[k], s_recv.at[k], "z+" if k % 2 == 0 else "z-")

    meet(to)
    for n in range(8):
        push(f"c{n}", s_at(n, 1 - c), core.at[n], "sib")
    for k in (0, 1):
        part = d_at(*order[k])
        power = power_of(largest(part))
        for h in range(sub):
            y_send(k, h, part[h], power)
    for k in (0, 1):
        power = power_of(sum_cores(k))
        for h in range(sub):
            z_send(k, h, core[k, h], power)
    most_d = [largest(d_at(*order[k])) for k in (4, 5, 2, 3)]
    most_s = [sum_cores(k) for k in (4, 5, 2, 3)]
    own_d, own_s = [power_of(most) for most in most_d[2:]], [power_of(most) for most in most_s[2:]]
    on_d, on_s, from_d, from_s = [], [], [], []
    for h in range(sub):
        for k in (0, 1):
            got(f"y{k}_{h}")
            if h == 0:
                from_d.append(bound_in(d_recv.at[k]))
                on_d.append(power_of(most_d[k] + from_d[k]))
            y_send(4 + k, h, d_at(*order[4 + k])[h] + tile_in(d_recv.at[k], h, from_d[k]), on_d[k])
            y_send(2 + k, h, d_at(*order[2 + k])[h], own_d[k])
            got(f"z{k}_{h}")
            if h == 0:
                from_s.append(bound_in(s_recv.at[k]))
                on_s.append(power_of(most_s[k] + from_s[k]))
            z_send(4 + k, h, core[4 + k, h] + tile_in(s_recv.at[k], h, from_s[k]), on_s[k])
            z_send(2 + k, h, core[2 + k, h], own_s[k])
    most_6, most_7 = sum_cores(6), sum_cores(7)
    away_d, away_s = d_at(0, 1 - xl), core.at[7 - xh]
    most_away_d = largest(away_d)
    most_away_s = jnp.where(xh == 0, most_7, most_6)
    for h in range(sub):
        got(f"y2_{h}", f"y3_{h}", f"y4_{h}", f"y5_{h}")
        if h == 0:
            near_d, far_d = bound_in(d_recv.at[2 + xl]), bound_in(d_recv.at[5 - xl])
            power_d = power_of(most_away_d + near_d + far_d)
        value = away_d[h] + tile_in(d_recv.at[2 + xl], h, near_d) + tile_in(d_recv.at[5 - xl], h, far_d)
        send_tile("xl", h, value, power_d, d_send.at[6], d_recv.at[6], "xl")
        got(f"z2_{h}", f"z3_{h}", f"z4_{h}", f"z5_{h}")
        if h == 0:
            near_s, far_s = bound_in(s_recv.at[2 + xh]), bound_in(s_recv.at[5 - xh])
            power_s = power_of(most_away_s + near_s + far_s)
        value = away_s[h] + tile_in(s_recv.at[2 + xh], h, near_s) + tile_in(s_recv.at[5 - xh], h, far_s)
        send_tile("xh", h, value, power_s, s_send.at[6], s_recv.at[6], "xh")
    home_d, home_s = d_at(0, xl), core.at[6 + xh]
    bufs_d = [d_recv.at[3 - xl], d_recv.at[4 + xl], d_recv.at[6]]
    bufs_s = [s_recv.at[3 - xh], s_recv.at[4 + xh], s_recv.at[6]]
    for h in range(sub):
        rows = pl.ds(h * T, T)
        got(f"xl{h}")
        by_dest = home_d[h]
        for buf in bufs_d:
            by_dest = by_dest + tile_in(buf, h, bound_in(buf))
        got(f"xh{h}")
        by_source = home_s[h]
        for buf in bufs_s:
            by_source = by_source + tile_in(buf, h, bound_in(buf))
        out_ref[rows, :] = (by_source + by_dest.T) * scale
    for copy in copies.values():
        copy.wait_send()


def reduce_sums(dp, sp, rows, scale):
    width = sp.shape[2]
    sub = rows // T
    copies = 8 + 14 * sub
    return pl.pallas_call(
        functools.partial(reduce_kernel, scale),
        out_shape=jax.ShapeDtypeStruct((rows, width), jnp.float32),
        in_specs=[pl.BlockSpec(memory_space=pltpu.VMEM)] * 2,
        out_specs=pl.BlockSpec(memory_space=pltpu.VMEM),
        scratch_shapes=[
            pltpu.VMEM((8, sub, T, width), jnp.float32),
            pltpu.VMEM((7, HEAD + sub * T, width), jnp.int16),
            pltpu.VMEM((7, HEAD + sub * T, width), jnp.int16),
            pltpu.VMEM((7, HEAD + sub * width, T), jnp.int16),
            pltpu.VMEM((7, HEAD + sub * width, T), jnp.int16),
            pltpu.SemaphoreType.DMA((copies,)),
            pltpu.SemaphoreType.DMA((copies,)),
        ],
        compiler_params=pltpu.CompilerParams(
            collective_id=1, has_side_effects=True, vmem_limit_bytes=REDUCE_VMEM << 20
        ),
    )(dp, sp)


def on_device(
    embedding, tile_dest, tile_source, tile_count, pattern_id, pattern_bank, negative_dest, negative_source
):
    rows = embedding.shape[0]
    live = jnp.arange(tile_dest.shape[3], dtype=jnp.int32) < tile_count[..., None]
    slots = ((pattern_id << DEST_BITS | tile_dest | jnp.where(live, LIVE, 0)) << SOURCE_BITS) | tile_source
    negatives = ((negative_dest | LIVE | NEGATIVE) << SOURCE_BITS) | negative_source
    negatives = negatives.swapaxes(2, 3)
    wide = jnp.pad(negatives, ((0, 0), (0, 0), (0, 0), (0, slots.shape[3] - negatives.shape[3])))
    d, g, gt, words = gather(embedding, jnp.concatenate([slots, wide], axis=2), tile_dest.shape[2])
    dp, sp = pair_sums(words, pattern_bank, d, g, gt)
    scale = 1.0 / math.sqrt(T * tile_dest.shape[2])
    return reduce_sums(dp, sp, rows, scale)


def solution(mesh):
    in_specs = (
        P(("blk", "fiber"), None),
        P("blk", "fiber", None, None),
        P("blk", "fiber", None, None),
        P("blk", "fiber", None),
        P("blk", "fiber", None, None),
        P(),
        P("blk", "fiber", None, None),
        P("blk", "fiber", None, None),
    )
    out_specs = P(("blk", "fiber"), None)
    return jax.shard_map(
        on_device, mesh=mesh, in_specs=in_specs, out_specs=out_specs, check_vma=False
    )
```

```python
import functools
import math

import jax
import jax.numpy as jnp
from jax import lax
from jax.experimental import pallas as pl
from jax.experimental.pallas import tpu as pltpu
from jax.sharding import PartitionSpec as P

ZS, XS, YS = 4, 2, 4
T = 128
MESH = pl.DeviceIdType.MESH
UNROLL = 8
PARTS = 4
GATHER_VMEM, PAIR_VMEM, REDUCE_VMEM = 14, 28, 36
SOURCE_BITS, DEST_BITS, BANK_BITS = 3, 6, 7
LIVE = 1 << (DEST_BITS + BANK_BITS)
NEGATIVE = LIVE << 1
G_AT = DEST_BITS + BANK_BITS + 2


def place():
    b, f = lax.axis_index("blk"), lax.axis_index("fiber")
    return b // 4, (b // 2) % 2, b % 2, f // YS, f % YS


def blk_of(z, xh, c):
    return ((z % ZS) * XS + xh) * 2 + c


def fiber_of(xl, y):
    return xl * YS + y % YS


def peers():
    z, xh, c, xl, y = place()
    b, f = blk_of(z, xh, c), fiber_of(xl, y)
    return {
        "sib": (blk_of(z, xh, 1 - c), f),
        "xh": (blk_of(z, 1 - xh, c), f),
        "z+": (blk_of(z + 1, xh, c), f),
        "z-": (blk_of(z + 3, xh, c), f),
        "xl": (b, fiber_of(1 - xl, y)),
        "y+": (b, fiber_of(xl, y + 1)),
        "y-": (b, fiber_of(xl, y + 3)),
    }


def meet(to):
    barrier = pltpu.get_barrier_semaphore()
    for device in to.values():
        pl.semaphore_signal(barrier, inc=1, device_id=device, device_id_type=MESH)
    pl.semaphore_wait(barrier, len(to))


def pair_words(words, block, stops, sub, room):
    slots, lanes = words.shape
    f32, bf16 = jnp.float32, jnp.bfloat16
    lane = lax.broadcasted_iota(jnp.int32, words.shape, 1)
    src = words & (2**SOURCE_BITS - 1)
    live = (words & (LIVE << SOURCE_BITS)) != 0
    picks = [jnp.where(live & (src == q), 1.0, 0.0) for q in range(sub)]

    def earlier(n, axis):
        shape = (n, n)
        return jnp.where(
            lax.broadcasted_iota(jnp.int32, shape, 1 - axis) < lax.broadcasted_iota(jnp.int32, shape, axis), 1.0, 0.0
        ).astype(bf16)

    before = earlier(slots, 0)
    ranks = [jnp.dot(before, pick.astype(bf16), preferred_element_type=f32) for pick in picks]
    held = [(jnp.sum(pick, axis=0, keepdims=True).astype(jnp.int32) + 1 >> 1).astype(f32) for pick in picks]
    in_stop = functools.reduce(lambda a, b: a + b, held)
    start = jnp.dot(
        jnp.broadcast_to(in_stop, (8, lanes)).astype(bf16), earlier(lanes, 1), preferred_element_type=f32
    )[:1]
    at = jnp.full(words.shape, -1.0, f32)
    for q in range(sub):
        at = jnp.where(picks[q] > 0.0, 2.0 * start + ranks[q], at)
        start = start + held[q]
    origin = block - lane
    origin = jnp.where(origin < 0, origin + stops, origin)
    code = (words >> SOURCE_BITS) | ((origin * sub + src) << G_AT)
    code = jnp.where(live, code, 0)

    def turned(values):
        tall = jnp.concatenate([values, jnp.zeros((lanes - slots, lanes), f32)], axis=0)
        return tall.T

    bytes_of = [turned(((code >> shift) & 255).astype(f32)) for shift in (0, 8, 16)]
    row = lax.broadcasted_iota(jnp.int32, (8, lanes), 0)
    spots = lax.broadcasted_iota(jnp.int32, (slots, room), 1).astype(f32)
    placed = jnp.zeros((8, room), f32)
    for stop in range(stops):
        parts = jnp.zeros((8, lanes), f32)
        for k in range(3):
            parts = jnp.where(row == k, jnp.broadcast_to(bytes_of[k][stop : stop + 1], (8, lanes)), parts)
        hit = jnp.where(jnp.broadcast_to(at[:, stop : stop + 1], spots.shape) == spots, 1.0, 0.0)
        placed = placed + jnp.dot(
            parts[:, :slots].astype(bf16), hit.astype(bf16), preferred_element_type=f32
        )
    placed = placed.astype(jnp.int32)
    listed = placed[0:1] | (placed[1:2] << 8) | (placed[2:3] << 16)
    total = jnp.sum(jnp.where(lane[:1] < stops, in_stop, 0.0), axis=1, keepdims=True).astype(jnp.int32)
    return jnp.where(lax.broadcasted_iota(jnp.int32, (1, room), 1) == room - 1, total, listed)


def gather_kernel(stops, e_ref, slot_ref, d_ref, g_ref, gt_ref, list_ref, words, send, recv, local):
    rows = e_ref.shape[0]
    part = rows // PARTS
    z, xh, c, xl, y = place()
    to = peers()
    copies = {}

    def push(name, src, dst, peer):
        k = len(copies)
        copies[name] = pltpu.make_async_remote_copy(
            src_ref=src,
            dst_ref=dst,
            send_sem=send.at[k],
            recv_sem=recv.at[k],
            device_id=to[peer],
            device_id_type=MESH,
        )
        copies[name].start()

    def got(name, h):
        copies[name, h].wait_recv()

    def e_at(h):
        return e_ref.at[pl.ds(h * part, part)]

    def g_at(zz, xx, h):
        return g_ref.at[pl.ds(blk_of(zz, xx, c) * rows + h * part, part)]

    def d_at(xx, yy, h):
        return d_ref.at[pl.ds(fiber_of(xx, yy) * rows + h * part, part)]

    def pass_g(name, zz, xx, h, peer):
        push((name, h), g_at(zz, xx, h), g_at(zz, xx, h), peer)

    def pass_d(name, xx, yy, h, peer):
        push((name, h), d_at(xx, yy, h), d_at(xx, yy, h), peer)

    def turn(block, from_ref=None):
        def one(i, carry):
            at = pl.ds(pl.multiple_of((0 if from_ref is not None else block * rows) + i * T, T), T)
            gt_ref[block * (rows // T) + i] = (g_ref if from_ref is None else from_ref)[at, :].T
            return carry

        lax.fori_loop(0, rows // T, one, 0)

    shared = []

    def absorb():
        copy, block = shared.pop(0)
        copy.wait_recv()
        turn(block)


    def share(zz, xx, src=None):
        whole = g_ref.at[pl.ds(blk_of(zz, xx, c) * rows, rows)]
        push(("sib", len(copies)), whole if src is None else src, whole, "sib")
        shared.append((copies["sib", len(copies) - 1], blk_of(zz, xx, 1 - c)))
        turn(blk_of(zz, xx, c), src)

    keep_d = pltpu.make_async_copy(e_ref, d_ref.at[pl.ds(fiber_of(xl, y) * rows, rows)], local.at[0])
    keep_g = pltpu.make_async_copy(e_ref, g_ref.at[pl.ds(blk_of(z, xh, c) * rows, rows)], local.at[1])
    keep_d.start()
    keep_g.start()
    meet(to)
    for h in range(PARTS):
        push(("xh", h), e_at(h), g_at(z, xh, h), "xh")
        push(("xl", h), e_at(h), d_at(xl, y, h), "xl")
        push(("z+", h), e_at(h), g_at(z, xh, h), "z+")
        push(("y+", h), e_at(h), d_at(xl, y, h), "y+")
        push(("z-", h), e_at(h), g_at(z, xh, h), "z-")
        push(("y-", h), e_at(h), d_at(xl, y, h), "y-")

    share(z, xh, e_ref)
    cap = slot_ref.shape[3]
    neg = slot_ref.shape[2] - stops
    words[...] = jnp.zeros_like(words)
    words[0:stops, 0:cap] = slot_ref[0, 0, 0:stops]
    by_slot = words[...].T
    words[...] = jnp.zeros_like(words)
    words[0:cap, :] = by_slot[0:cap]
    words[cap : cap + neg, 0:stops] = slot_ref[0, 0, stops : stops + neg, 0:stops]
    list_ref[...] = pair_words(
        words[0 : cap + neg + 4, :], lax.axis_index("blk"), stops, gt_ref.shape[0] // stops, list_ref.shape[1]
    )

    def second_hop(h):
        got("xl-", h)
        pass_d("xl--", 1 - xl, y + 1, h, "y-")
        got("xh-", h)
        pass_g("xh--", z + 1, 1 - xh, h, "z-")

    for h in range(PARTS):
        got("z+", h)
        pass_g("z++", z + 3, xh, h, "z+")
        got("y+", h)
        pass_d("y++", xl, y + 3, h, "y+")
        got("xl", h)
        pass_d("xl-", 1 - xl, y, h, "y-")
        pass_d("xl+", 1 - xl, y, h, "y+")
        got("xh", h)
        pass_g("xh-", z, 1 - xh, h, "z-")
        pass_g("xh+", z, 1 - xh, h, "z+")
        if h:
            second_hop(h - 1)
    share(z + 3, xh)
    share(z, 1 - xh)
    second_hop(PARTS - 1)
    share(z + 1, 1 - xh)
    absorb()
    for name, zz, xx in (("z-", z + 1, xh), ("z++", z + 2, xh), ("xh+", z + 3, 1 - xh), ("xh--", z + 2, 1 - xh)):
        for h in range(PARTS):
            got(name, h)
        share(zz, xx)
        absorb()
    for h in range(PARTS):
        for name in ("y-", "xl+", "y++", "xl--"):
            got(name, h)
    while shared:
        absorb()
    for copy in copies.values():
        copy.wait_send()
    keep_d.wait()
    keep_g.wait()


def gather(e, slots, stops):
    rows, width = e.shape
    copies = 14 * PARTS + 8
    cap, neg = slots.shape[3], slots.shape[2] - stops
    total = ZS * XS * 2 * rows
    room = stops * (cap + neg + total // T // stops) + 4 * UNROLL + 1
    room += (-room) % T
    vmem, anywhere = pl.BlockSpec(memory_space=pltpu.VMEM), pl.BlockSpec(memory_space=pl.ANY)
    return pl.pallas_call(
        functools.partial(gather_kernel, stops),
        out_shape=(
            jax.ShapeDtypeStruct((XS * YS * rows, width), e.dtype),
            jax.ShapeDtypeStruct((total, width), e.dtype),
            jax.ShapeDtypeStruct((total // T, width, T), e.dtype),
            jax.ShapeDtypeStruct((1, room), jnp.int32),
        ),
        in_specs=[vmem, vmem],
        out_specs=(anywhere, vmem, vmem, vmem),
        scratch_shapes=[
            pltpu.VMEM((T, T), jnp.int32),
            pltpu.SemaphoreType.DMA((copies,)),
            pltpu.SemaphoreType.DMA((copies,)),
            pltpu.SemaphoreType.DMA((2,)),
        ],
        compiler_params=pltpu.CompilerParams(
            collective_id=0, has_side_effects=True, vmem_limit_bytes=GATHER_VMEM << 20
        ),
    )(e, slots)


def pair_kernel(list_ref, bank_ref, d_ref, g_ref, gt_ref, dp_ref, sp_ref, coded):
    def clear(i, carry):
        dp_ref[i] = jnp.zeros(dp_ref.shape[1:], dp_ref.dtype)
        for k in range(sp_ref.shape[0] // dp_ref.shape[0]):
            sp_ref[i * (sp_ref.shape[0] // dp_ref.shape[0]) + k] = jnp.zeros(sp_ref.shape[1:], sp_ref.dtype)
        return carry

    lax.fori_loop(0, dp_ref.shape[0], clear, 0)
    pairs = list_ref[0, list_ref.shape[1] - 1]
    one_bit = jnp.left_shift(1, lax.broadcasted_iota(jnp.int32, (32, T), 0))

    def mask_less_half(index, keep):
        words = bank_ref[index] & keep
        return jnp.concatenate(
            [
                jnp.where((jnp.broadcast_to(words[k : k + 1, :], (32, T)) & one_bit) != 0, 0.5, -0.5)
                for k in range(words.shape[0])
            ],
            axis=0,
        )

    def tiles(i):
        codes = [list_ref[0, 2 * i], list_ref[0, 2 * i + 1]]
        p = [code & (2**DEST_BITS - 1) for code in codes]
        zp = jnp.concatenate([d_ref[pl.ds(pl.multiple_of(k * T, T), T), :] for k in p], axis=0)
        return codes[0] >> G_AT, p, zp

    def first(i):
        codes = [list_ref[0, 2 * i], list_ref[0, 2 * i + 1]]
        g, _, zp = tiles(i)
        ids = [(code >> DEST_BITS) & (2**BANK_BITS - 1) for code in codes]
        keep = [((code >> (DEST_BITS + BANK_BITS + 1)) & 1) - 1 for code in codes]
        live = [((code >> (DEST_BITS + BANK_BITS)) & 1).astype(jnp.float32) for code in codes]
        zq = g_ref[pl.ds(pl.multiple_of(g * T, T), T), :]
        s = lax.dot_general(zq, zp, (((1,), (1,)), ((), ())), preferred_element_type=jnp.float32)
        half = 0.5 * jnp.tanh(0.5 * s)
        r = jnp.concatenate(
            [live[u] * (mask_less_half(ids[u], keep[u]) - half[:, u * T : (u + 1) * T]) for u in range(2)], axis=1
        ).astype(jnp.bfloat16)
        return r

    def second(i, r):
        g, p, zp = tiles(i)
        to_source = jnp.dot(r, zp, preferred_element_type=jnp.float32)
        to_dest = jnp.dot(gt_ref[g], r, preferred_element_type=jnp.float32)
        sp_ref[g] += to_source
        dp_ref[p[0]] += to_dest[:, :T]
        dp_ref[p[1]] += to_dest[:, T:]

    for u in range(UNROLL):
        coded[0, u] = first(u)

    def body(step, carry):
        now = lax.rem(step, 2)
        later = []
        for u in range(UNROLL):
            later.append(first((step + 1) * UNROLL + u))
            second(step * UNROLL + u, coded[now, u])
        for u in range(UNROLL):
            coded[1 - now, u] = later[u]
        return carry

    lax.fori_loop(0, (pairs + UNROLL - 1) // UNROLL, body, 0)


def pair_sums(words, bank, d, g, gt):
    width = d.shape[1]
    smem = pl.BlockSpec(memory_space=pltpu.SMEM)
    vmem = pl.BlockSpec(memory_space=pltpu.VMEM)
    return pl.pallas_call(
        pair_kernel,
        out_shape=(
            jax.ShapeDtypeStruct((d.shape[0] // T, width, T), jnp.float32),
            jax.ShapeDtypeStruct((g.shape[0] // T, T, width), jnp.float32),
        ),
        in_specs=[smem] + [vmem] * 4,
        out_specs=(vmem, vmem),
        scratch_shapes=[pltpu.VMEM((2, UNROLL, T, 2 * T), d.dtype)],
        compiler_params=pltpu.CompilerParams(vmem_limit_bytes=PAIR_VMEM << 20),
    )(words, bank, d, g, gt)


LEVELS = 32760.0
HEAD = 16


def power_of(bound):
    return jnp.ceil(jnp.log2(jnp.maximum(bound, 1e-37)))


def reduce_kernel(scale, dp_ref, sp_ref, out_ref, core, s_send, s_recv, d_send, d_recv, send, recv):
    sub = core.shape[1]
    z, xh, c, xl, y = place()
    to = peers()
    copies = {}

    def push(name, src, dst, peer):
        k = len(copies)
        copies[name] = pltpu.make_async_remote_copy(
            src_ref=src,
            dst_ref=dst,
            send_sem=send.at[k],
            recv_sem=recv.at[k],
            device_id=to[peer],
            device_id_type=MESH,
        )
        copies[name].start()

    order = [(2, 0), (2, 1), (1, 1), (3, 0), (1, 0), (3, 1), (0, 0), (0, 1)]

    def s_at(n, core_at):
        dz, xx = order[n]
        return sp_ref.at[pl.ds(blk_of(z + dz, xx, core_at) * sub, sub)]

    def d_at(dy, xx):
        return dp_ref.at[pl.ds(fiber_of(xx, y + dy) * sub, sub)]

    def largest(ref):
        def one(i, most):
            return jnp.maximum(most, jnp.max(jnp.abs(ref[i]), axis=0, keepdims=True))

        return lax.fori_loop(0, sub, one, jnp.zeros((1, ref.shape[2]), jnp.float32))

    def sum_cores(n):
        copies[f"c{n}"].wait_recv()
        mine, total = s_at(n, c), core.at[n]

        def one(i, most):
            value = total[i] + mine[i]
            total[i] = value
            return jnp.maximum(most, jnp.max(jnp.abs(value), axis=0, keepdims=True))

        return lax.fori_loop(0, sub, one, jnp.zeros((1, core.shape[3]), jnp.float32))

    def span(h, height):
        return pl.ds(0, HEAD + height) if h == 0 else pl.ds(HEAD + h * height, height)

    def send_tile(name, h, value, power, out_buf, in_buf, peer):
        height = value.shape[0]
        q = jnp.round((value * jnp.exp2(-power)) * LEVELS)
        out_buf[pl.ds(HEAD + h * height, height), :] = q.astype(jnp.int32).astype(jnp.int16)
        if h == 0:
            out_buf[pl.ds(0, HEAD), :] = (
                jnp.broadcast_to(power, (HEAD, power.shape[1])).astype(jnp.int32).astype(jnp.int16)
            )
        push(f"{name}{h}", out_buf.at[span(h, height)], in_buf.at[span(h, height)], peer)

    def bound_in(buf):
        return jnp.exp2(buf[pl.ds(0, HEAD), :].astype(jnp.float32)[:1])

    def tile_in(buf, h, bound):
        height = (buf.shape[0] - HEAD) // sub
        return buf[pl.ds(HEAD + h * height, height), :].astype(jnp.float32) * (1.0 / LEVELS) * bound

    def got(*names):
        for name in names:
            copies[name].wait_recv()

    def y_send(k, h, value, power):
        send_tile(f"y{k}_", h, value, power, d_send.at[k], d_recv.at[k], "y+" if k % 2 == 0 else "y-")

    def z_send(k, h, value, power):
        send_tile(f"z{k}_", h, value, power, s_send.at[k], s_recv.at[k], "z+" if k % 2 == 0 else "z-")

    meet(to)
    for n in range(8):
        push(f"c{n}", s_at(n, 1 - c), core.at[n], "sib")
    for k in (0, 1):
        part = d_at(*order[k])
        power = power_of(largest(part))
        for h in range(sub):
            y_send(k, h, part[h], power)
    for k in (0, 1):
        power = power_of(sum_cores(k))
        for h in range(sub):
            z_send(k, h, core[k, h], power)
    most_d = [largest(d_at(*order[k])) for k in (4, 5, 2, 3)]
    most_s = [sum_cores(k) for k in (4, 5, 2, 3)]
    own_d, own_s = [power_of(most) for most in most_d[2:]], [power_of(most) for most in most_s[2:]]
    on_d, on_s, from_d, from_s = [], [], [], []
    for h in range(sub):
        for k in (0, 1):
            got(f"y{k}_{h}")
            if h == 0:
                from_d.append(bound_in(d_recv.at[k]))
                on_d.append(power_of(most_d[k] + from_d[k]))
            y_send(4 + k, h, d_at(*order[4 + k])[h] + tile_in(d_recv.at[k], h, from_d[k]), on_d[k])
            y_send(2 + k, h, d_at(*order[2 + k])[h], own_d[k])
            got(f"z{k}_{h}")
            if h == 0:
                from_s.append(bound_in(s_recv.at[k]))
                on_s.append(power_of(most_s[k] + from_s[k]))
            z_send(4 + k, h, core[4 + k, h] + tile_in(s_recv.at[k], h, from_s[k]), on_s[k])
            z_send(2 + k, h, core[2 + k, h], own_s[k])
    most_6, most_7 = sum_cores(6), sum_cores(7)
    away_d, away_s = d_at(0, 1 - xl), core.at[7 - xh]
    most_away_d = largest(away_d)
    most_away_s = jnp.where(xh == 0, most_7, most_6)
    for h in range(sub):
        got(f"y2_{h}", f"y3_{h}", f"y4_{h}", f"y5_{h}")
        if h == 0:
            near_d, far_d = bound_in(d_recv.at[2 + xl]), bound_in(d_recv.at[5 - xl])
            power_d = power_of(most_away_d + near_d + far_d)
        value = away_d[h] + tile_in(d_recv.at[2 + xl], h, near_d) + tile_in(d_recv.at[5 - xl], h, far_d)
        send_tile("xl", h, value, power_d, d_send.at[6], d_recv.at[6], "xl")
        got(f"z2_{h}", f"z3_{h}", f"z4_{h}", f"z5_{h}")
        if h == 0:
            near_s, far_s = bound_in(s_recv.at[2 + xh]), bound_in(s_recv.at[5 - xh])
            power_s = power_of(most_away_s + near_s + far_s)
        value = away_s[h] + tile_in(s_recv.at[2 + xh], h, near_s) + tile_in(s_recv.at[5 - xh], h, far_s)
        send_tile("xh", h, value, power_s, s_send.at[6], s_recv.at[6], "xh")
    home_d, home_s = d_at(0, xl), core.at[6 + xh]
    bufs_d = [d_recv.at[3 - xl], d_recv.at[4 + xl], d_recv.at[6]]
    bufs_s = [s_recv.at[3 - xh], s_recv.at[4 + xh], s_recv.at[6]]
    for h in range(sub):
        rows = pl.ds(h * T, T)
        got(f"xl{h}")
        by_dest = home_d[h]
        for buf in bufs_d:
            by_dest = by_dest + tile_in(buf, h, bound_in(buf))
        got(f"xh{h}")
        by_source = home_s[h]
        for buf in bufs_s:
            by_source = by_source + tile_in(buf, h, bound_in(buf))
        out_ref[rows, :] = (by_source + by_dest.T) * scale
    for copy in copies.values():
        copy.wait_send()


def reduce_sums(dp, sp, rows, scale):
    width = sp.shape[2]
    sub = rows // T
    copies = 8 + 14 * sub
    return pl.pallas_call(
        functools.partial(reduce_kernel, scale),
        out_shape=jax.ShapeDtypeStruct((rows, width), jnp.float32),
        in_specs=[pl.BlockSpec(memory_space=pltpu.VMEM)] * 2,
        out_specs=pl.BlockSpec(memory_space=pltpu.VMEM),
        scratch_shapes=[
            pltpu.VMEM((8, sub, T, width), jnp.float32),
            pltpu.VMEM((7, HEAD + sub * T, width), jnp.int16),
            pltpu.VMEM((7, HEAD + sub * T, width), jnp.int16),
            pltpu.VMEM((7, HEAD + sub * width, T), jnp.int16),
            pltpu.VMEM((7, HEAD + sub * width, T), jnp.int16),
            pltpu.SemaphoreType.DMA((copies,)),
            pltpu.SemaphoreType.DMA((copies,)),
        ],
        compiler_params=pltpu.CompilerParams(
            collective_id=1, has_side_effects=True, vmem_limit_bytes=REDUCE_VMEM << 20
        ),
    )(dp, sp)


def on_device(
    embedding, tile_dest, tile_source, tile_count, pattern_id, pattern_bank, negative_dest, negative_source
):
    rows = embedding.shape[0]
    live = jnp.arange(tile_dest.shape[3], dtype=jnp.int32) < tile_count[..., None]
    slots = ((pattern_id << DEST_BITS | tile_dest | jnp.where(live, LIVE, 0)) << SOURCE_BITS) | tile_source
    negatives = ((negative_dest | LIVE | NEGATIVE) << SOURCE_BITS) | negative_source
    negatives = negatives.swapaxes(2, 3)
    wide = jnp.pad(negatives, ((0, 0), (0, 0), (0, 0), (0, slots.shape[3] - negatives.shape[3])))
    d, g, gt, words = gather(embedding, jnp.concatenate([slots, wide], axis=2), tile_dest.shape[2])
    dp, sp = pair_sums(words, pattern_bank, d, g, gt)
    scale = 1.0 / math.sqrt(T * tile_dest.shape[2])
    return reduce_sums(dp, sp, rows, scale)


def solution(mesh):
    in_specs = (
        P(("blk", "fiber"), None),
        P("blk", "fiber", None, None),
        P("blk", "fiber", None, None),
        P("blk", "fiber", None),
        P("blk", "fiber", None, None),
        P(),
        P("blk", "fiber", None, None),
        P("blk", "fiber", None, None),
    )
    out_specs = P(("blk", "fiber"), None)
    return jax.shard_map(
        on_device, mesh=mesh, in_specs=in_specs, out_specs=out_specs, check_vma=False
    )
```

```python
import functools
import math

import jax
import jax.numpy as jnp
from jax import lax
from jax.experimental import pallas as pl
from jax.experimental.pallas import tpu as pltpu
from jax.sharding import PartitionSpec as P

ZS, XS, YS = 4, 2, 4
T = 128
MESH = pl.DeviceIdType.MESH
UNROLL = 8
PARTS = 4
GATHER_VMEM, PAIR_VMEM, REDUCE_VMEM = 14, 28, 36
SOURCE_BITS, DEST_BITS, BANK_BITS = 3, 6, 7
LIVE = 1 << (DEST_BITS + BANK_BITS)
NEGATIVE = LIVE << 1
G_AT = DEST_BITS + BANK_BITS + 2


def place():
    b, f = lax.axis_index("blk"), lax.axis_index("fiber")
    return b // 4, (b // 2) % 2, b % 2, f // YS, f % YS


def blk_of(z, xh, c):
    return ((z % ZS) * XS + xh) * 2 + c


def fiber_of(xl, y):
    return xl * YS + y % YS


def peers():
    z, xh, c, xl, y = place()
    b, f = blk_of(z, xh, c), fiber_of(xl, y)
    return {
        "sib": (blk_of(z, xh, 1 - c), f),
        "xh": (blk_of(z, 1 - xh, c), f),
        "z+": (blk_of(z + 1, xh, c), f),
        "z-": (blk_of(z + 3, xh, c), f),
        "xl": (b, fiber_of(1 - xl, y)),
        "y+": (b, fiber_of(xl, y + 1)),
        "y-": (b, fiber_of(xl, y + 3)),
    }


def meet(to):
    barrier = pltpu.get_barrier_semaphore()
    for device in to.values():
        pl.semaphore_signal(barrier, inc=1, device_id=device, device_id_type=MESH)
    pl.semaphore_wait(barrier, len(to))


def pair_words(words, block, stops, sub, room):
    slots, lanes = words.shape
    f32, bf16 = jnp.float32, jnp.bfloat16
    lane = lax.broadcasted_iota(jnp.int32, words.shape, 1)
    src = words & (2**SOURCE_BITS - 1)
    live = (words & (LIVE << SOURCE_BITS)) != 0
    picks = [jnp.where(live & (src == q), 1.0, 0.0) for q in range(sub)]

    def earlier(n, axis):
        shape = (n, n)
        return jnp.where(
            lax.broadcasted_iota(jnp.int32, shape, 1 - axis) < lax.broadcasted_iota(jnp.int32, shape, axis), 1.0, 0.0
        ).astype(bf16)

    before = earlier(slots, 0)
    ranks = [jnp.dot(before, pick.astype(bf16), preferred_element_type=f32) for pick in picks]
    held = [(jnp.sum(pick, axis=0, keepdims=True).astype(jnp.int32) + 1 >> 1).astype(f32) for pick in picks]
    in_stop = functools.reduce(lambda a, b: a + b, held)
    start = jnp.dot(
        jnp.broadcast_to(in_stop, (8, lanes)).astype(bf16), earlier(lanes, 1), preferred_element_type=f32
    )[:1]
    at = jnp.full(words.shape, -1.0, f32)
    for q in range(sub):
        at = jnp.where(picks[q] > 0.0, 2.0 * start + ranks[q], at)
        start = start + held[q]
    origin = block - lane
    origin = jnp.where(origin < 0, origin + stops, origin)
    code = (words >> SOURCE_BITS) | ((origin * sub + src) << G_AT)
    code = jnp.where(live, code, 0)

    def turned(values):
        tall = jnp.concatenate([values, jnp.zeros((lanes - slots, lanes), f32)], axis=0)
        return tall.T

    bytes_of = [turned(((code >> shift) & 255).astype(f32)) for shift in (0, 8, 16)]
    row = lax.broadcasted_iota(jnp.int32, (8, lanes), 0)
    spots = lax.broadcasted_iota(jnp.int32, (slots, room), 1).astype(f32)
    placed = jnp.zeros((8, room), f32)
    for stop in range(stops):
        parts = jnp.zeros((8, lanes), f32)
        for k in range(3):
            parts = jnp.where(row == k, jnp.broadcast_to(bytes_of[k][stop : stop + 1], (8, lanes)), parts)
        hit = jnp.where(jnp.broadcast_to(at[:, stop : stop + 1], spots.shape) == spots, 1.0, 0.0)
        placed = placed + jnp.dot(
            parts[:, :slots].astype(bf16), hit.astype(bf16), preferred_element_type=f32
        )
    placed = placed.astype(jnp.int32)
    listed = placed[0:1] | (placed[1:2] << 8) | (placed[2:3] << 16)
    total = jnp.sum(jnp.where(lane[:1] < stops, in_stop, 0.0), axis=1, keepdims=True).astype(jnp.int32)
    return jnp.where(lax.broadcasted_iota(jnp.int32, (1, room), 1) == room - 1, total, listed)


def gather_kernel(stops, e_ref, slot_ref, d_ref, g_ref, gt_ref, list_ref, words, send, recv, local):
    rows = e_ref.shape[0]
    part = rows // PARTS
    z, xh, c, xl, y = place()
    to = peers()
    copies = {}

    def push(name, src, dst, peer):
        k = len(copies)
        copies[name] = pltpu.make_async_remote_copy(
            src_ref=src,
            dst_ref=dst,
            send_sem=send.at[k],
            recv_sem=recv.at[k],
            device_id=to[peer],
            device_id_type=MESH,
        )
        copies[name].start()

    def got(name, h):
        copies[name, h].wait_recv()

    def e_at(h):
        return e_ref.at[pl.ds(h * part, part)]

    def g_at(zz, xx, h):
        return g_ref.at[pl.ds(blk_of(zz, xx, c) * rows + h * part, part)]

    def d_at(xx, yy, h):
        return d_ref.at[pl.ds(fiber_of(xx, yy) * rows + h * part, part)]

    def pass_g(name, zz, xx, h, peer):
        push((name, h), g_at(zz, xx, h), g_at(zz, xx, h), peer)

    def pass_d(name, xx, yy, h, peer):
        push((name, h), d_at(xx, yy, h), d_at(xx, yy, h), peer)

    def turn(block, from_ref=None):
        def one(i, carry):
            at = pl.ds(pl.multiple_of((0 if from_ref is not None else block * rows) + i * T, T), T)
            gt_ref[block * (rows // T) + i] = (g_ref if from_ref is None else from_ref)[at, :].T
            return carry

        lax.fori_loop(0, rows // T, one, 0)

    shared = []

    def absorb():
        copy, block = shared.pop(0)
        copy.wait_recv()
        turn(block)


    def share(zz, xx, src=None):
        whole = g_ref.at[pl.ds(blk_of(zz, xx, c) * rows, rows)]
        push(("sib", len(copies)), whole if src is None else src, whole, "sib")
        shared.append((copies["sib", len(copies) - 1], blk_of(zz, xx, 1 - c)))
        turn(blk_of(zz, xx, c), src)

    keep_d = pltpu.make_async_copy(e_ref, d_ref.at[pl.ds(fiber_of(xl, y) * rows, rows)], local.at[0])
    keep_g = pltpu.make_async_copy(e_ref, g_ref.at[pl.ds(blk_of(z, xh, c) * rows, rows)], local.at[1])
    keep_d.start()
    keep_g.start()
    meet(to)
    for h in range(PARTS):
        push(("xh", h), e_at(h), g_at(z, xh, h), "xh")
        push(("xl", h), e_at(h), d_at(xl, y, h), "xl")
        push(("z+", h), e_at(h), g_at(z, xh, h), "z+")
        push(("y+", h), e_at(h), d_at(xl, y, h), "y+")
        push(("z-", h), e_at(h), g_at(z, xh, h), "z-")
        push(("y-", h), e_at(h), d_at(xl, y, h), "y-")

    share(z, xh, e_ref)
    cap = slot_ref.shape[3]
    neg = slot_ref.shape[2] - stops
    words[...] = jnp.zeros_like(words)
    words[0:stops, 0:cap] = slot_ref[0, 0, 0:stops]
    by_slot = words[...].T
    words[...] = jnp.zeros_like(words)
    words[0:cap, :] = by_slot[0:cap]
    words[cap : cap + neg, 0:stops] = slot_ref[0, 0, stops : stops + neg, 0:stops]
    list_ref[...] = pair_words(
        words[0 : cap + neg + 4, :], lax.axis_index("blk"), stops, gt_ref.shape[0] // stops, list_ref.shape[1]
    )

    def second_hop(h):
        got("xl-", h)
        pass_d("xl--", 1 - xl, y + 1, h, "y-")
        got("xh-", h)
        pass_g("xh--", z + 1, 1 - xh, h, "z-")

    for h in range(PARTS):
        got("z+", h)
        pass_g("z++", z + 3, xh, h, "z+")
        got("y+", h)
        pass_d("y++", xl, y + 3, h, "y+")
        got("xl", h)
        pass_d("xl-", 1 - xl, y, h, "y-")
        pass_d("xl+", 1 - xl, y, h, "y+")
        got("xh", h)
        pass_g("xh-", z, 1 - xh, h, "z-")
        pass_g("xh+", z, 1 - xh, h, "z+")
        if h:
            second_hop(h - 1)
    share(z + 3, xh)
    share(z, 1 - xh)
    second_hop(PARTS - 1)
    share(z + 1, 1 - xh)
    absorb()
    for name, zz, xx in (("z-", z + 1, xh), ("z++", z + 2, xh), ("xh+", z + 3, 1 - xh), ("xh--", z + 2, 1 - xh)):
        for h in range(PARTS):
            got(name, h)
        share(zz, xx)
        absorb()
    for h in range(PARTS):
        for name in ("y-", "xl+", "y++", "xl--"):
            got(name, h)
    while shared:
        absorb()
    for copy in copies.values():
        copy.wait_send()
    keep_d.wait()
    keep_g.wait()


def gather(e, slots, stops):
    rows, width = e.shape
    copies = 14 * PARTS + 8
    cap, neg = slots.shape[3], slots.shape[2] - stops
    total = ZS * XS * 2 * rows
    room = stops * (cap + neg + total // T // stops) + 4 * UNROLL + 1
    room += (-room) % T
    vmem, anywhere = pl.BlockSpec(memory_space=pltpu.VMEM), pl.BlockSpec(memory_space=pl.ANY)
    return pl.pallas_call(
        functools.partial(gather_kernel, stops),
        out_shape=(
            jax.ShapeDtypeStruct((XS * YS * rows, width), e.dtype),
            jax.ShapeDtypeStruct((total, width), e.dtype),
            jax.ShapeDtypeStruct((total // T, width, T), e.dtype),
            jax.ShapeDtypeStruct((1, room), jnp.int32),
        ),
        in_specs=[vmem, vmem],
        out_specs=(anywhere, vmem, vmem, vmem),
        scratch_shapes=[
            pltpu.VMEM((T, T), jnp.int32),
            pltpu.SemaphoreType.DMA((copies,)),
            pltpu.SemaphoreType.DMA((copies,)),
            pltpu.SemaphoreType.DMA((2,)),
        ],
        compiler_params=pltpu.CompilerParams(
            collective_id=0, has_side_effects=True, vmem_limit_bytes=GATHER_VMEM << 20
        ),
    )(e, slots)


def pair_kernel(list_ref, bank_ref, d_ref, g_ref, gt_ref, dp_ref, sp_ref, coded):
    pairs = list_ref[0, list_ref.shape[1] - 1]
    one_bit = jnp.left_shift(1, lax.broadcasted_iota(jnp.int32, (32, T), 0))

    def mask_less_half(index, keep):
        words = bank_ref[index] & keep
        return jnp.concatenate(
            [
                jnp.where((jnp.broadcast_to(words[k : k + 1, :], (32, T)) & one_bit) != 0, 0.5, -0.5)
                for k in range(words.shape[0])
            ],
            axis=0,
        )

    def tiles(i):
        codes = [list_ref[0, 2 * i], list_ref[0, 2 * i + 1]]
        p = [code & (2**DEST_BITS - 1) for code in codes]
        zp = jnp.concatenate([d_ref[pl.ds(pl.multiple_of(k * T, T), T), :] for k in p], axis=0)
        return codes[0] >> G_AT, p, zp

    def first(i):
        codes = [list_ref[0, 2 * i], list_ref[0, 2 * i + 1]]
        g, _, zp = tiles(i)
        ids = [(code >> DEST_BITS) & (2**BANK_BITS - 1) for code in codes]
        keep = [((code >> (DEST_BITS + BANK_BITS + 1)) & 1) - 1 for code in codes]
        live = [((code >> (DEST_BITS + BANK_BITS)) & 1).astype(jnp.float32) for code in codes]
        zq = g_ref[pl.ds(pl.multiple_of(g * T, T), T), :]
        s = lax.dot_general(zq, zp, (((1,), (1,)), ((), ())), preferred_element_type=jnp.float32)
        half = 0.5 * jnp.tanh(0.5 * s)
        r = jnp.concatenate(
            [live[u] * (mask_less_half(ids[u], keep[u]) - half[:, u * T : (u + 1) * T]) for u in range(2)], axis=1
        ).astype(jnp.bfloat16)
        return r

    def second(i, r):
        g, p, zp = tiles(i)
        to_source = jnp.dot(r, zp, preferred_element_type=jnp.float32)
        to_dest = jnp.dot(gt_ref[g], r, preferred_element_type=jnp.float32)
        sp_ref[g] += to_source
        dp_ref[p[0]] += to_dest[:, :T]
        dp_ref[p[1]] += to_dest[:, T:]

    def begin(u, carry):
        coded[0, u] = first(u)
        for ref in (dp_ref, sp_ref):
            share = ref.shape[0] // UNROLL
            for k in range(share):
                ref[u * share + k] = jnp.zeros(ref.shape[1:], ref.dtype)
        return carry

    assert dp_ref.shape[0] % UNROLL == 0 and sp_ref.shape[0] % UNROLL == 0
    lax.fori_loop(0, UNROLL, begin, 0)

    def body(step, carry):
        now = lax.rem(step, 2)
        later = []
        for u in range(UNROLL):
            later.append(first((step + 1) * UNROLL + u))
            second(step * UNROLL + u, coded[now, u])
        for u in range(UNROLL):
            coded[1 - now, u] = later[u]
        return carry

    lax.fori_loop(0, (pairs + UNROLL - 1) // UNROLL, body, 0)


def pair_sums(words, bank, d, g, gt):
    width = d.shape[1]
    smem = pl.BlockSpec(memory_space=pltpu.SMEM)
    vmem = pl.BlockSpec(memory_space=pltpu.VMEM)
    return pl.pallas_call(
        pair_kernel,
        out_shape=(
            jax.ShapeDtypeStruct((d.shape[0] // T, width, T), jnp.float32),
            jax.ShapeDtypeStruct((g.shape[0] // T, T, width), jnp.float32),
        ),
        in_specs=[smem] + [vmem] * 4,
        out_specs=(vmem, vmem),
        scratch_shapes=[pltpu.VMEM((2, UNROLL, T, 2 * T), d.dtype)],
        compiler_params=pltpu.CompilerParams(vmem_limit_bytes=PAIR_VMEM << 20),
    )(words, bank, d, g, gt)


LEVELS = 32760.0
HEAD = 16


def power_of(bound):
    return jnp.ceil(jnp.log2(jnp.maximum(bound, 1e-37)))


def reduce_kernel(scale, dp_ref, sp_ref, out_ref, core, s_send, s_recv, d_send, d_recv, send, recv):
    sub = core.shape[1]
    z, xh, c, xl, y = place()
    to = peers()
    copies = {}

    def push(name, src, dst, peer):
        k = len(copies)
        copies[name] = pltpu.make_async_remote_copy(
            src_ref=src,
            dst_ref=dst,
            send_sem=send.at[k],
            recv_sem=recv.at[k],
            device_id=to[peer],
            device_id_type=MESH,
        )
        copies[name].start()

    order = [(2, 0), (2, 1), (1, 1), (3, 0), (1, 0), (3, 1), (0, 0), (0, 1)]

    def s_at(n, core_at):
        dz, xx = order[n]
        return sp_ref.at[pl.ds(blk_of(z + dz, xx, core_at) * sub, sub)]

    def d_at(dy, xx):
        return dp_ref.at[pl.ds(fiber_of(xx, y + dy) * sub, sub)]

    def largest(ref):
        def one(i, most):
            return jnp.maximum(most, jnp.max(jnp.abs(ref[i]), axis=0, keepdims=True))

        return lax.fori_loop(0, sub, one, jnp.zeros((1, ref.shape[2]), jnp.float32))

    def sum_cores(n):
        copies[f"c{n}"].wait_recv()
        mine, total = s_at(n, c), core.at[n]

        def one(i, most):
            value = total[i] + mine[i]
            total[i] = value
            return jnp.maximum(most, jnp.max(jnp.abs(value), axis=0, keepdims=True))

        return lax.fori_loop(0, sub, one, jnp.zeros((1, core.shape[3]), jnp.float32))

    def span(h, height):
        return pl.ds(0, HEAD + height) if h == 0 else pl.ds(HEAD + h * height, height)

    def send_tile(name, h, value, power, out_buf, in_buf, peer):
        height = value.shape[0]
        q = jnp.round((value * jnp.exp2(-power)) * LEVELS)
        out_buf[pl.ds(HEAD + h * height, height), :] = q.astype(jnp.int32).astype(jnp.int16)
        if h == 0:
            out_buf[pl.ds(0, HEAD), :] = (
                jnp.broadcast_to(power, (HEAD, power.shape[1])).astype(jnp.int32).astype(jnp.int16)
            )
        push(f"{name}{h}", out_buf.at[span(h, height)], in_buf.at[span(h, height)], peer)

    def bound_in(buf):
        return jnp.exp2(buf[pl.ds(0, HEAD), :].astype(jnp.float32)[:1])

    def tile_in(buf, h, bound):
        height = (buf.shape[0] - HEAD) // sub
        return buf[pl.ds(HEAD + h * height, height), :].astype(jnp.float32) * (1.0 / LEVELS) * bound

    def got(*names):
        for name in names:
            copies[name].wait_recv()

    def y_send(k, h, value, power):
        send_tile(f"y{k}_", h, value, power, d_send.at[k], d_recv.at[k], "y+" if k % 2 == 0 else "y-")

    def z_send(k, h, value, power):
        send_tile(f"z{k}_", h, value, power, s_send.at[k], s_recv.at[k], "z+" if k % 2 == 0 else "z-")

    meet(to)
    for n in range(8):
        push(f"c{n}", s_at(n, 1 - c), core.at[n], "sib")
    for k in (0, 1):
        part = d_at(*order[k])
        power = power_of(largest(part))
        for h in range(sub):
            y_send(k, h, part[h], power)
    for k in (0, 1):
        power = power_of(sum_cores(k))
        for h in range(sub):
            z_send(k, h, core[k, h], power)
    most_d = [largest(d_at(*order[k])) for k in (4, 5, 2, 3)]
    most_s = [sum_cores(k) for k in (4, 5, 2, 3)]
    own_d, own_s = [power_of(most) for most in most_d[2:]], [power_of(most) for most in most_s[2:]]
    on_d, on_s, from_d, from_s = [], [], [], []
    for h in range(sub):
        for k in (0, 1):
            got(f"y{k}_{h}")
            if h == 0:
                from_d.append(bound_in(d_recv.at[k]))
                on_d.append(power_of(most_d[k] + from_d[k]))
            y_send(4 + k, h, d_at(*order[4 + k])[h] + tile_in(d_recv.at[k], h, from_d[k]), on_d[k])
            y_send(2 + k, h, d_at(*order[2 + k])[h], own_d[k])
            got(f"z{k}_{h}")
            if h == 0:
                from_s.append(bound_in(s_recv.at[k]))
                on_s.append(power_of(most_s[k] + from_s[k]))
            z_send(4 + k, h, core[4 + k, h] + tile_in(s_recv.at[k], h, from_s[k]), on_s[k])
            z_send(2 + k, h, core[2 + k, h], own_s[k])
    most_6, most_7 = sum_cores(6), sum_cores(7)
    away_d, away_s = d_at(0, 1 - xl), core.at[7 - xh]
    most_away_d = largest(away_d)
    most_away_s = jnp.where(xh == 0, most_7, most_6)
    for h in range(sub):
        got(f"y2_{h}", f"y3_{h}", f"y4_{h}", f"y5_{h}")
        if h == 0:
            near_d, far_d = bound_in(d_recv.at[2 + xl]), bound_in(d_recv.at[5 - xl])
            power_d = power_of(most_away_d + near_d + far_d)
        value = away_d[h] + tile_in(d_recv.at[2 + xl], h, near_d) + tile_in(d_recv.at[5 - xl], h, far_d)
        send_tile("xl", h, value, power_d, d_send.at[6], d_recv.at[6], "xl")
        got(f"z2_{h}", f"z3_{h}", f"z4_{h}", f"z5_{h}")
        if h == 0:
            near_s, far_s = bound_in(s_recv.at[2 + xh]), bound_in(s_recv.at[5 - xh])
            power_s = power_of(most_away_s + near_s + far_s)
        value = away_s[h] + tile_in(s_recv.at[2 + xh], h, near_s) + tile_in(s_recv.at[5 - xh], h, far_s)
        send_tile("xh", h, value, power_s, s_send.at[6], s_recv.at[6], "xh")
    home_d, home_s = d_at(0, xl), core.at[6 + xh]
    bufs_d = [d_recv.at[3 - xl], d_recv.at[4 + xl], d_recv.at[6]]
    bufs_s = [s_recv.at[3 - xh], s_recv.at[4 + xh], s_recv.at[6]]
    for h in range(sub):
        rows = pl.ds(h * T, T)
        got(f"xl{h}")
        by_dest = home_d[h]
        for buf in bufs_d:
            by_dest = by_dest + tile_in(buf, h, bound_in(buf))
        got(f"xh{h}")
        by_source = home_s[h]
        for buf in bufs_s:
            by_source = by_source + tile_in(buf, h, bound_in(buf))
        out_ref[rows, :] = (by_source + by_dest.T) * scale
    for copy in copies.values():
        copy.wait_send()


def reduce_sums(dp, sp, rows, scale):
    width = sp.shape[2]
    sub = rows // T
    copies = 8 + 14 * sub
    return pl.pallas_call(
        functools.partial(reduce_kernel, scale),
        out_shape=jax.ShapeDtypeStruct((rows, width), jnp.float32),
        in_specs=[pl.BlockSpec(memory_space=pltpu.VMEM)] * 2,
        out_specs=pl.BlockSpec(memory_space=pltpu.VMEM),
        scratch_shapes=[
            pltpu.VMEM((8, sub, T, width), jnp.float32),
            pltpu.VMEM((7, HEAD + sub * T, width), jnp.int16),
            pltpu.VMEM((7, HEAD + sub * T, width), jnp.int16),
            pltpu.VMEM((7, HEAD + sub * width, T), jnp.int16),
            pltpu.VMEM((7, HEAD + sub * width, T), jnp.int16),
            pltpu.SemaphoreType.DMA((copies,)),
            pltpu.SemaphoreType.DMA((copies,)),
        ],
        compiler_params=pltpu.CompilerParams(
            collective_id=1, has_side_effects=True, vmem_limit_bytes=REDUCE_VMEM << 20
        ),
    )(dp, sp)


def on_device(
    embedding, tile_dest, tile_source, tile_count, pattern_id, pattern_bank, negative_dest, negative_source
):
    rows = embedding.shape[0]
    live = jnp.arange(tile_dest.shape[3], dtype=jnp.int32) < tile_count[..., None]
    slots = ((pattern_id << DEST_BITS | tile_dest | jnp.where(live, LIVE, 0)) << SOURCE_BITS) | tile_source
    negatives = ((negative_dest | LIVE | NEGATIVE) << SOURCE_BITS) | negative_source
    negatives = negatives.swapaxes(2, 3)
    wide = jnp.pad(negatives, ((0, 0), (0, 0), (0, 0), (0, slots.shape[3] - negatives.shape[3])))
    d, g, gt, words = gather(embedding, jnp.concatenate([slots, wide], axis=2), tile_dest.shape[2])
    dp, sp = pair_sums(words, pattern_bank, d, g, gt)
    scale = 1.0 / math.sqrt(T * tile_dest.shape[2])
    return reduce_sums(dp, sp, rows, scale)


def solution(mesh):
    in_specs = (
        P(("blk", "fiber"), None),
        P("blk", "fiber", None, None),
        P("blk", "fiber", None, None),
        P("blk", "fiber", None),
        P("blk", "fiber", None, None),
        P(),
        P("blk", "fiber", None, None),
        P("blk", "fiber", None, None),
    )
    out_specs = P(("blk", "fiber"), None)
    return jax.shard_map(
        on_device, mesh=mesh, in_specs=in_specs, out_specs=out_specs, check_vma=False
    )
```

```python
import functools
import math

import jax
import jax.numpy as jnp
from jax import lax
from jax.experimental import pallas as pl
from jax.experimental.pallas import tpu as pltpu
from jax.sharding import PartitionSpec as P

ZS, XS, YS = 4, 2, 4
T = 128
MESH = pl.DeviceIdType.MESH
UNROLL = 8
PARTS = 4
GATHER_VMEM, PAIR_VMEM, REDUCE_VMEM = 14, 28, 36
SOURCE_BITS, DEST_BITS, BANK_BITS = 3, 6, 7
LIVE = 1 << (DEST_BITS + BANK_BITS)
NEGATIVE = LIVE << 1
G_AT = DEST_BITS + BANK_BITS + 2


def place():
    b, f = lax.axis_index("blk"), lax.axis_index("fiber")
    return b // 4, (b // 2) % 2, b % 2, f // YS, f % YS


def blk_of(z, xh, c):
    return ((z % ZS) * XS + xh) * 2 + c


def fiber_of(xl, y):
    return xl * YS + y % YS


def peers():
    z, xh, c, xl, y = place()
    b, f = blk_of(z, xh, c), fiber_of(xl, y)
    return {
        "sib": (blk_of(z, xh, 1 - c), f),
        "xh": (blk_of(z, 1 - xh, c), f),
        "z+": (blk_of(z + 1, xh, c), f),
        "z-": (blk_of(z + 3, xh, c), f),
        "xl": (b, fiber_of(1 - xl, y)),
        "y+": (b, fiber_of(xl, y + 1)),
        "y-": (b, fiber_of(xl, y + 3)),
    }


def meet(to):
    barrier = pltpu.get_barrier_semaphore()
    for device in to.values():
        pl.semaphore_signal(barrier, inc=1, device_id=device, device_id_type=MESH)
    pl.semaphore_wait(barrier, len(to))


def pair_words(words, block, stops, sub, room):
    slots, lanes = words.shape
    f32, bf16 = jnp.float32, jnp.bfloat16
    lane = lax.broadcasted_iota(jnp.int32, words.shape, 1)
    src = words & (2**SOURCE_BITS - 1)
    live = (words & (LIVE << SOURCE_BITS)) != 0
    picks = [jnp.where(live & (src == q), 1.0, 0.0) for q in range(sub)]

    def earlier(n, axis):
        shape = (n, n)
        return jnp.where(
            lax.broadcasted_iota(jnp.int32, shape, 1 - axis) < lax.broadcasted_iota(jnp.int32, shape, axis), 1.0, 0.0
        ).astype(bf16)

    before = earlier(slots, 0)
    ranks = [jnp.dot(before, pick.astype(bf16), preferred_element_type=f32) for pick in picks]
    held = [(jnp.sum(pick, axis=0, keepdims=True).astype(jnp.int32) + 1 >> 1).astype(f32) for pick in picks]
    in_stop = functools.reduce(lambda a, b: a + b, held)
    start = jnp.dot(
        jnp.broadcast_to(in_stop, (8, lanes)).astype(bf16), earlier(lanes, 1), preferred_element_type=f32
    )[:1]
    at = jnp.full(words.shape, -1.0, f32)
    for q in range(sub):
        at = jnp.where(picks[q] > 0.0, 2.0 * start + ranks[q], at)
        start = start + held[q]
    origin = block - lane
    origin = jnp.where(origin < 0, origin + stops, origin)
    code = (words >> SOURCE_BITS) | ((origin * sub + src) << G_AT)
    code = jnp.where(live, code, 0)

    def turned(values):
        tall = jnp.concatenate([values, jnp.zeros((lanes - slots, lanes), f32)], axis=0)
        return tall.T

    bytes_of = [turned(((code >> shift) & 255).astype(f32)) for shift in (0, 8, 16)]
    row = lax.broadcasted_iota(jnp.int32, (8, lanes), 0)
    spots = lax.broadcasted_iota(jnp.int32, (slots, room), 1).astype(f32)
    placed = jnp.zeros((8, room), f32)
    for stop in range(stops):
        parts = jnp.zeros((8, lanes), f32)
        for k in range(3):
            parts = jnp.where(row == k, jnp.broadcast_to(bytes_of[k][stop : stop + 1], (8, lanes)), parts)
        hit = jnp.where(jnp.broadcast_to(at[:, stop : stop + 1], spots.shape) == spots, 1.0, 0.0)
        placed = placed + jnp.dot(
            parts[:, :slots].astype(bf16), hit.astype(bf16), preferred_element_type=f32
        )
    placed = placed.astype(jnp.int32)
    listed = placed[0:1] | (placed[1:2] << 8) | (placed[2:3] << 16)
    total = jnp.sum(jnp.where(lane[:1] < stops, in_stop, 0.0), axis=1, keepdims=True).astype(jnp.int32)
    return jnp.where(lax.broadcasted_iota(jnp.int32, (1, room), 1) == room - 1, total, listed)


def gather_kernel(stops, e_ref, slot_ref, d_ref, g_ref, gt_ref, list_ref, words, send, recv, local):
    rows = e_ref.shape[0]
    part = rows // PARTS
    z, xh, c, xl, y = place()
    to = peers()
    copies = {}

    def push(name, src, dst, peer):
        k = len(copies)
        copies[name] = pltpu.make_async_remote_copy(
            src_ref=src,
            dst_ref=dst,
            send_sem=send.at[k],
            recv_sem=recv.at[k],
            device_id=to[peer],
            device_id_type=MESH,
        )
        copies[name].start()

    def got(name, h):
        copies[name, h].wait_recv()

    def e_at(h):
        return e_ref.at[pl.ds(h * part, part)]

    def g_at(zz, xx, h):
        return g_ref.at[pl.ds(blk_of(zz, xx, c) * rows + h * part, part)]

    def d_at(xx, yy, h):
        return d_ref.at[pl.ds(fiber_of(xx, yy) * rows + h * part, part)]

    def pass_g(name, zz, xx, h, peer):
        push((name, h), g_at(zz, xx, h), g_at(zz, xx, h), peer)

    def pass_d(name, xx, yy, h, peer):
        push((name, h), d_at(xx, yy, h), d_at(xx, yy, h), peer)

    def turn(block, from_ref=None):
        def one(i, carry):
            at = pl.ds(pl.multiple_of((0 if from_ref is not None else block * rows) + i * T, T), T)
            gt_ref[block * (rows // T) + i] = (g_ref if from_ref is None else from_ref)[at, :].T
            return carry

        lax.fori_loop(0, rows // T, one, 0)

    shared = []

    def absorb():
        copy, block = shared.pop(0)
        copy.wait_recv()
        turn(block)


    def share(zz, xx, src=None):
        whole = g_ref.at[pl.ds(blk_of(zz, xx, c) * rows, rows)]
        push(("sib", len(copies)), whole if src is None else src, whole, "sib")
        shared.append((copies["sib", len(copies) - 1], blk_of(zz, xx, 1 - c)))
        turn(blk_of(zz, xx, c), src)

    keep_d = pltpu.make_async_copy(e_ref, d_ref.at[pl.ds(fiber_of(xl, y) * rows, rows)], local.at[0])
    keep_g = pltpu.make_async_copy(e_ref, g_ref.at[pl.ds(blk_of(z, xh, c) * rows, rows)], local.at[1])
    keep_d.start()
    keep_g.start()
    meet(to)
    for h in range(PARTS):
        push(("xh", h), e_at(h), g_at(z, xh, h), "xh")
        push(("xl", h), e_at(h), d_at(xl, y, h), "xl")
        push(("z+", h), e_at(h), g_at(z, xh, h), "z+")
        push(("y+", h), e_at(h), d_at(xl, y, h), "y+")
        push(("z-", h), e_at(h), g_at(z, xh, h), "z-")
        push(("y-", h), e_at(h), d_at(xl, y, h), "y-")

    share(z, xh, e_ref)
    cap = slot_ref.shape[3]
    neg = slot_ref.shape[2] - stops
    words[...] = jnp.zeros_like(words)
    words[0:stops, 0:cap] = slot_ref[0, 0, 0:stops]
    by_slot = words[...].T
    words[...] = jnp.zeros_like(words)
    words[0:cap, :] = by_slot[0:cap]
    words[cap : cap + neg, 0:stops] = slot_ref[0, 0, stops : stops + neg, 0:stops]
    list_ref[...] = pair_words(
        words[0 : cap + neg + 4, :], lax.axis_index("blk"), stops, gt_ref.shape[0] // stops, list_ref.shape[1]
    )

    def second_hop(h):
        got("xl-", h)
        pass_d("xl--", 1 - xl, y + 1, h, "y-")
        got("xh-", h)
        pass_g("xh--", z + 1, 1 - xh, h, "z-")

    for h in range(PARTS):
        got("z+", h)
        pass_g("z++", z + 3, xh, h, "z+")
        got("y+", h)
        pass_d("y++", xl, y + 3, h, "y+")
        got("xl", h)
        pass_d("xl-", 1 - xl, y, h, "y-")
        pass_d("xl+", 1 - xl, y, h, "y+")
        got("xh", h)
        pass_g("xh-", z, 1 - xh, h, "z-")
        pass_g("xh+", z, 1 - xh, h, "z+")
        if h:
            second_hop(h - 1)
    share(z + 3, xh)
    share(z, 1 - xh)
    second_hop(PARTS - 1)
    share(z + 1, 1 - xh)
    absorb()
    for name, zz, xx in (("z-", z + 1, xh), ("z++", z + 2, xh), ("xh+", z + 3, 1 - xh), ("xh--", z + 2, 1 - xh)):
        for h in range(PARTS):
            got(name, h)
        share(zz, xx)
        absorb()
    for h in range(PARTS):
        for name in ("y-", "xl+", "y++", "xl--"):
            got(name, h)
    while shared:
        absorb()
    for copy in copies.values():
        copy.wait_send()
    keep_d.wait()
    keep_g.wait()


def gather(e, slots, stops):
    rows, width = e.shape
    copies = 14 * PARTS + 8
    cap, neg = slots.shape[3], slots.shape[2] - stops
    total = ZS * XS * 2 * rows
    room = stops * (cap + neg + total // T // stops) + 4 * UNROLL + 1
    room += (-room) % T
    vmem, anywhere = pl.BlockSpec(memory_space=pltpu.VMEM), pl.BlockSpec(memory_space=pl.ANY)
    return pl.pallas_call(
        functools.partial(gather_kernel, stops),
        out_shape=(
            jax.ShapeDtypeStruct((XS * YS * rows, width), e.dtype),
            jax.ShapeDtypeStruct((total, width), e.dtype),
            jax.ShapeDtypeStruct((total // T, width, T), e.dtype),
            jax.ShapeDtypeStruct((1, room), jnp.int32),
        ),
        in_specs=[vmem, vmem],
        out_specs=(anywhere, vmem, vmem, vmem),
        scratch_shapes=[
            pltpu.VMEM((T, T), jnp.int32),
            pltpu.SemaphoreType.DMA((copies,)),
            pltpu.SemaphoreType.DMA((copies,)),
            pltpu.SemaphoreType.DMA((2,)),
        ],
        compiler_params=pltpu.CompilerParams(
            collective_id=0, has_side_effects=True, vmem_limit_bytes=GATHER_VMEM << 20
        ),
    )(e, slots)


def pair_kernel(list_ref, bank_ref, d_ref, g_ref, gt_ref, dp_ref, sp_ref, coded):
    pairs = list_ref[0, list_ref.shape[1] - 1]
    one_bit = jnp.left_shift(1, lax.broadcasted_iota(jnp.int32, (32, T), 0))

    def mask_less_half(index, keep):
        words = bank_ref[index] & keep
        return jnp.concatenate(
            [
                jnp.where((jnp.broadcast_to(words[k : k + 1, :], (32, T)) & one_bit) != 0, 0.5, -0.5)
                for k in range(words.shape[0])
            ],
            axis=0,
        )

    def tiles(i):
        codes = [list_ref[0, 2 * i], list_ref[0, 2 * i + 1]]
        p = [code & (2**DEST_BITS - 1) for code in codes]
        zp = jnp.concatenate([d_ref[pl.ds(pl.multiple_of(k * T, T), T), :] for k in p], axis=0)
        return codes[0] >> G_AT, p, zp

    def first(i):
        codes = [list_ref[0, 2 * i], list_ref[0, 2 * i + 1]]
        g, _, zp = tiles(i)
        ids = [(code >> DEST_BITS) & (2**BANK_BITS - 1) for code in codes]
        keep = [((code >> (DEST_BITS + BANK_BITS + 1)) & 1) - 1 for code in codes]
        live = [((code >> (DEST_BITS + BANK_BITS)) & 1).astype(jnp.float32) for code in codes]
        zq = g_ref[pl.ds(pl.multiple_of(g * T, T), T), :]
        s = lax.dot_general(zq, zp, (((1,), (1,)), ((), ())), preferred_element_type=jnp.float32)
        half = 0.5 * jnp.tanh(0.5 * s)
        r = jnp.concatenate(
            [live[u] * (mask_less_half(ids[u], keep[u]) - half[:, u * T : (u + 1) * T]) for u in range(2)], axis=1
        ).astype(jnp.bfloat16)
        return r

    def second(i, r):
        g, p, zp = tiles(i)
        to_source = jnp.dot(r, zp, preferred_element_type=jnp.float32)
        to_dest = jnp.dot(gt_ref[g], r, preferred_element_type=jnp.float32)
        sp_ref[g] += to_source
        dp_ref[p[0]] += to_dest[:, :T]
        dp_ref[p[1]] += to_dest[:, T:]

    for u in range(UNROLL):
        coded[0, u] = first(u)
        for ref in (dp_ref, sp_ref):
            for tile in range(u, ref.shape[0], UNROLL):
                ref[tile] = jnp.zeros(ref.shape[1:], ref.dtype)

    def body(step, carry):
        now = lax.rem(step, 2)
        later = []
        for u in range(UNROLL):
            later.append(first((step + 1) * UNROLL + u))
            second(step * UNROLL + u, coded[now, u])
        for u in range(UNROLL):
            coded[1 - now, u] = later[u]
        return carry

    lax.fori_loop(0, (pairs + UNROLL - 1) // UNROLL, body, 0)


def pair_sums(words, bank, d, g, gt):
    width = d.shape[1]
    smem = pl.BlockSpec(memory_space=pltpu.SMEM)
    vmem = pl.BlockSpec(memory_space=pltpu.VMEM)
    return pl.pallas_call(
        pair_kernel,
        out_shape=(
            jax.ShapeDtypeStruct((d.shape[0] // T, width, T), jnp.float32),
            jax.ShapeDtypeStruct((g.shape[0] // T, T, width), jnp.float32),
        ),
        in_specs=[smem] + [vmem] * 4,
        out_specs=(vmem, vmem),
        scratch_shapes=[pltpu.VMEM((2, UNROLL, T, 2 * T), d.dtype)],
        compiler_params=pltpu.CompilerParams(vmem_limit_bytes=PAIR_VMEM << 20),
    )(words, bank, d, g, gt)


LEVELS = 32760.0
HEAD = 16


def power_of(bound):
    return jnp.ceil(jnp.log2(jnp.maximum(bound, 1e-37)))


def reduce_kernel(scale, dp_ref, sp_ref, out_ref, core, s_send, s_recv, d_send, d_recv, send, recv):
    sub = core.shape[1]
    z, xh, c, xl, y = place()
    to = peers()
    copies = {}

    def push(name, src, dst, peer):
        k = len(copies)
        copies[name] = pltpu.make_async_remote_copy(
            src_ref=src,
            dst_ref=dst,
            send_sem=send.at[k],
            recv_sem=recv.at[k],
            device_id=to[peer],
            device_id_type=MESH,
        )
        copies[name].start()

    order = [(2, 0), (2, 1), (1, 1), (3, 0), (1, 0), (3, 1), (0, 0), (0, 1)]

    def s_at(n, core_at):
        dz, xx = order[n]
        return sp_ref.at[pl.ds(blk_of(z + dz, xx, core_at) * sub, sub)]

    def d_at(dy, xx):
        return dp_ref.at[pl.ds(fiber_of(xx, y + dy) * sub, sub)]

    def largest(ref):
        def one(i, most):
            return jnp.maximum(most, jnp.max(jnp.abs(ref[i]), axis=0, keepdims=True))

        return lax.fori_loop(0, sub, one, jnp.zeros((1, ref.shape[2]), jnp.float32))

    def sum_cores(n):
        copies[f"c{n}"].wait_recv()
        mine, total = s_at(n, c), core.at[n]

        def one(i, most):
            value = total[i] + mine[i]
            total[i] = value
            return jnp.maximum(most, jnp.max(jnp.abs(value), axis=0, keepdims=True))

        return lax.fori_loop(0, sub, one, jnp.zeros((1, core.shape[3]), jnp.float32))

    def span(h, height):
        return pl.ds(0, HEAD + height) if h == 0 else pl.ds(HEAD + h * height, height)

    def send_tile(name, h, value, power, out_buf, in_buf, peer):
        height = value.shape[0]
        q = jnp.round((value * jnp.exp2(-power)) * LEVELS)
        out_buf[pl.ds(HEAD + h * height, height), :] = q.astype(jnp.int32).astype(jnp.int16)
        if h == 0:
            out_buf[pl.ds(0, HEAD), :] = (
                jnp.broadcast_to(power, (HEAD, power.shape[1])).astype(jnp.int32).astype(jnp.int16)
            )
        push(f"{name}{h}", out_buf.at[span(h, height)], in_buf.at[span(h, height)], peer)

    def bound_in(buf):
        return jnp.exp2(buf[pl.ds(0, HEAD), :].astype(jnp.float32)[:1])

    def tile_in(buf, h, bound):
        height = (buf.shape[0] - HEAD) // sub
        return buf[pl.ds(HEAD + h * height, height), :].astype(jnp.float32) * (1.0 / LEVELS) * bound

    def got(*names):
        for name in names:
            copies[name].wait_recv()

    def y_send(k, h, value, power):
        send_tile(f"y{k}_", h, value, power, d_send.at[k], d_recv.at[k], "y+" if k % 2 == 0 else "y-")

    def z_send(k, h, value, power):
        send_tile(f"z{k}_", h, value, power, s_send.at[k], s_recv.at[k], "z+" if k % 2 == 0 else "z-")

    meet(to)
    for n in range(8):
        push(f"c{n}", s_at(n, 1 - c), core.at[n], "sib")
    for k in (0, 1):
        part = d_at(*order[k])
        power = power_of(largest(part))
        for h in range(sub):
            y_send(k, h, part[h], power)
    for k in (0, 1):
        power = power_of(sum_cores(k))
        for h in range(sub):
            z_send(k, h, core[k, h], power)
    most_d = [largest(d_at(*order[k])) for k in (4, 5, 2, 3)]
    most_s = [sum_cores(k) for k in (4, 5, 2, 3)]
    own_d, own_s = [power_of(most) for most in most_d[2:]], [power_of(most) for most in most_s[2:]]
    on_d, on_s, from_d, from_s = [], [], [], []
    for h in range(sub):
        for k in (0, 1):
            got(f"y{k}_{h}")
            if h == 0:
                from_d.append(bound_in(d_recv.at[k]))
                on_d.append(power_of(most_d[k] + from_d[k]))
            y_send(4 + k, h, d_at(*order[4 + k])[h] + tile_in(d_recv.at[k], h, from_d[k]), on_d[k])
            y_send(2 + k, h, d_at(*order[2 + k])[h], own_d[k])
            got(f"z{k}_{h}")
            if h == 0:
                from_s.append(bound_in(s_recv.at[k]))
                on_s.append(power_of(most_s[k] + from_s[k]))
            z_send(4 + k, h, core[4 + k, h] + tile_in(s_recv.at[k], h, from_s[k]), on_s[k])
            z_send(2 + k, h, core[2 + k, h], own_s[k])
    most_6, most_7 = sum_cores(6), sum_cores(7)
    away_d, away_s = d_at(0, 1 - xl), core.at[7 - xh]
    most_away_d = largest(away_d)
    most_away_s = jnp.where(xh == 0, most_7, most_6)
    for h in range(sub):
        got(f"y2_{h}", f"y3_{h}", f"y4_{h}", f"y5_{h}")
        if h == 0:
            near_d, far_d = bound_in(d_recv.at[2 + xl]), bound_in(d_recv.at[5 - xl])
            power_d = power_of(most_away_d + near_d + far_d)
        value = away_d[h] + tile_in(d_recv.at[2 + xl], h, near_d) + tile_in(d_recv.at[5 - xl], h, far_d)
        send_tile("xl", h, value, power_d, d_send.at[6], d_recv.at[6], "xl")
        got(f"z2_{h}", f"z3_{h}", f"z4_{h}", f"z5_{h}")
        if h == 0:
            near_s, far_s = bound_in(s_recv.at[2 + xh]), bound_in(s_recv.at[5 - xh])
            power_s = power_of(most_away_s + near_s + far_s)
        value = away_s[h] + tile_in(s_recv.at[2 + xh], h, near_s) + tile_in(s_recv.at[5 - xh], h, far_s)
        send_tile("xh", h, value, power_s, s_send.at[6], s_recv.at[6], "xh")
    home_d, home_s = d_at(0, xl), core.at[6 + xh]
    bufs_d = [d_recv.at[3 - xl], d_recv.at[4 + xl], d_recv.at[6]]
    bufs_s = [s_recv.at[3 - xh], s_recv.at[4 + xh], s_recv.at[6]]
    for h in range(sub):
        rows = pl.ds(h * T, T)
        got(f"xl{h}")
        by_dest = home_d[h]
        for buf in bufs_d:
            by_dest = by_dest + tile_in(buf, h, bound_in(buf))
        got(f"xh{h}")
        by_source = home_s[h]
        for buf in bufs_s:
            by_source = by_source + tile_in(buf, h, bound_in(buf))
        out_ref[rows, :] = (by_source + by_dest.T) * scale
    for copy in copies.values():
        copy.wait_send()


def reduce_sums(dp, sp, rows, scale):
    width = sp.shape[2]
    sub = rows // T
    copies = 8 + 14 * sub
    return pl.pallas_call(
        functools.partial(reduce_kernel, scale),
        out_shape=jax.ShapeDtypeStruct((rows, width), jnp.float32),
        in_specs=[pl.BlockSpec(memory_space=pltpu.VMEM)] * 2,
        out_specs=pl.BlockSpec(memory_space=pltpu.VMEM),
        scratch_shapes=[
            pltpu.VMEM((8, sub, T, width), jnp.float32),
            pltpu.VMEM((7, HEAD + sub * T, width), jnp.int16),
            pltpu.VMEM((7, HEAD + sub * T, width), jnp.int16),
            pltpu.VMEM((7, HEAD + sub * width, T), jnp.int16),
            pltpu.VMEM((7, HEAD + sub * width, T), jnp.int16),
            pltpu.SemaphoreType.DMA((copies,)),
            pltpu.SemaphoreType.DMA((copies,)),
        ],
        compiler_params=pltpu.CompilerParams(
            collective_id=1, has_side_effects=True, vmem_limit_bytes=REDUCE_VMEM << 20
        ),
    )(dp, sp)


def on_device(
    embedding, tile_dest, tile_source, tile_count, pattern_id, pattern_bank, negative_dest, negative_source
):
    rows = embedding.shape[0]
    live = jnp.arange(tile_dest.shape[3], dtype=jnp.int32) < tile_count[..., None]
    slots = ((pattern_id << DEST_BITS | tile_dest | jnp.where(live, LIVE, 0)) << SOURCE_BITS) | tile_source
    negatives = ((negative_dest | LIVE | NEGATIVE) << SOURCE_BITS) | negative_source
    negatives = negatives.swapaxes(2, 3)
    wide = jnp.pad(negatives, ((0, 0), (0, 0), (0, 0), (0, slots.shape[3] - negatives.shape[3])))
    d, g, gt, words = gather(embedding, jnp.concatenate([slots, wide], axis=2), tile_dest.shape[2])
    dp, sp = pair_sums(words, pattern_bank, d, g, gt)
    scale = 1.0 / math.sqrt(T * tile_dest.shape[2])
    return reduce_sums(dp, sp, rows, scale)


def solution(mesh):
    in_specs = (
        P(("blk", "fiber"), None),
        P("blk", "fiber", None, None),
        P("blk", "fiber", None, None),
        P("blk", "fiber", None),
        P("blk", "fiber", None, None),
        P(),
        P("blk", "fiber", None, None),
        P("blk", "fiber", None, None),
    )
    out_specs = P(("blk", "fiber"), None)
    return jax.shard_map(
        on_device, mesh=mesh, in_specs=in_specs, out_specs=out_specs, check_vma=False
    )
```
